32 devices in a mesh: grp: 2 (over x), seq: 4 (over y, core), sub: 4 (over z).
Axes of the slice: x: 2, y: 2, z: 4, core: 2. Of those that a mesh axis runs over, the one named last changes fastest.
Arguments:
- query_rows: bfloat16 [8, 512, 2048], P(('grp', 'sub'), 'seq'), parts along dimension 0, may hold values from -9 to 9
- key_rows: bfloat16 [8, 512, 256], P(('grp', 'sub'), 'seq'), parts along dimension 0, may hold values from -4 to 4
- value_rows: bfloat16 [8, 512, 256], P(('grp', 'sub'), 'seq'), parts along dimension 0, may hold values from -6 to 6
- residual_in: bfloat16 [8, 512, 2048], P(('grp', 'sub'), 'seq'), parts along dimension 0, may hold values from -6 to 6
- out_proj: bfloat16 [2048, 2048], P('seq'), may hold values from -0.5 to 0.5
- norm_gain: bfloat16 [2048], replicated, may hold values from 0.099609375 to 1.8984375
- expert_ids: int32 [8, 512, 8], P(('grp', 'sub'), 'seq'), parts along dimension 0, may hold values from 0 to 15, all different within a row; in each aligned block of 128 rows (0 to 127, 128 to 255, ..., all dimensions but the last counted through in order) at most 80 rows name the same one
- gate_weights: bfloat16 [8, 512, 8], P(('grp', 'sub'), 'seq'), parts along dimension 0, may hold values from 0.049804688 to 1
- expert_gate: bfloat16 [16, 2048, 768], P(('seq', 'sub')), may hold values from -0.125 to 0.125
- expert_up: bfloat16 [16, 2048, 768], P(('seq', 'sub')), may hold values from -0.125 to 0.125
- expert_down: bfloat16 [16, 768, 2048], P(('seq', 'sub')), may hold values from -0.21875 to 0.21875
Outputs:
- layer_out: bfloat16 [8, 512, 2048], P(('grp', 'sub'), 'seq'), parts along dimension 0
The draws below stay inside these ranges and needn't reach their ends.
There are 2 independent parts, one for each index of `grp`. The reference program is written for one: setup_inputs(seed, part) draws one part's arguments, and reference() takes and returns one part's arrays. A program takes and returns all parts, laid end to end along the dimension named above; an argument that names none is the same for every part. Nothing has to cross between parts.
Inputs may be any that keep to these rules, and one draw needn't show every extreme that they name: `expert_ids`: A row names 8 different experts. In each aligned block of 128 rows (the rows of one device) no expert is named by more than 80 rows, a bound that some block reaches.
All inputs are finite; a program needn't handle non-finite values.
Results may differ from the reference program's by a relative error of at most 0.013.
Values may be sent and summed in bfloat16 or wider, within the bound.
No kernel may reach another device: no remote copies, remote signals or barrier semaphores. Data moves between devices by JAX's collectives and lax.ppermute only.
A program may use at most 128 MiB of HBM per device.

```python
import math
import jax
import jax.numpy as jnp
import numpy as np
from jax import lax

D = 2048
HD = 128
QH = 16
KVH = 2
FF = 768
TOPK = 8
TOK_DEV = 128
SEQS = 4
SEQ_LEN = 512
EXPERTS = 16
CAP = 80


def draw_attention(key):
    query_key = jax.random.fold_in(key, 101)
    other_key = jax.random.fold_in(key, 202)
    query_shape = (SEQS, SEQ_LEN, QH * HD)
    key_shape = (SEQS, SEQ_LEN, KVH * HD)
    queries = 2.0 * jax.random.truncated_normal(query_key, -4.0, 4.0, query_shape, jnp.float32)
    keys = jax.random.truncated_normal(other_key, -4.0, 4.0, key_shape, jnp.float32)
    return (queries, keys)


def draw_query_rows(key, part):
    return draw_attention(key)[0].astype(jnp.bfloat16)


def draw_key_rows(key, part):
    return draw_attention(key)[1].astype(jnp.bfloat16)


def steps_of(rng, shape, split, least, largest):
    loudness, own = 1.0, jax.random.fold_in(rng, 6)
    for axis_at, parts in split:
        heights = jnp.exp(jax.random.uniform(jax.random.fold_in(own, axis_at), (parts,), jnp.float32, least / len(split), largest / len(split)))
        loudness = loudness * jnp.repeat(heights, shape[axis_at] // parts).reshape([-1 if axis == axis_at else 1 for axis in range(len(shape))])
    return loudness


def assign_block(key, own, number, rows, number_of, top, bound, skew):
    order = jax.random.permutation(key, number_of)
    crowded, common = load_shares(number_of, rows * top, bound, skew, True), load_shares(number_of, rows * top, bound, skew, False)
    places = jnp.arange(number_of)

    def named(tallies, turn):
        used = int((tallies > 0).sum())
        fixed = max(1, used // 4)
        moved = fixed + (places - fixed + turn * (used - fixed)) % max(1, number_of - fixed)
        return jnp.zeros((number_of,), jnp.int32).at[order[jnp.where(places < fixed, places, moved)]].set(jnp.asarray(tallies, jnp.int32))

    tallies = jnp.where(number % 4 == 0, named(crowded, number // 4), named(common, number - number // 4 - 1))
    mixed = jax.random.permutation(jax.random.fold_in(own, 3), number_of)
    giver, taker = mixed[0:number_of // 2 * 2:2], mixed[1:number_of // 2 * 2:2]
    slack = jnp.minimum(tallies[giver] - 1, bound - tallies[taker]) // 2
    slack = jnp.where((giver == order[0]) | (taker == order[0]) | (tallies[taker] == 0), 0, jnp.maximum(slack, 0))
    moved = jax.random.randint(jax.random.fold_in(own, 4), (number_of // 2,), 0, 1 << 20) % (slack + 1)
    tallies = tallies.at[giver].add(-moved).at[taker].add(moved)
    members = jnp.searchsorted(jnp.cumsum(tallies), jnp.arange(rows * top), side="right").astype(jnp.int32)
    listing = members.reshape(top, rows).T
    listing = listing[jax.random.permutation(jax.random.fold_in(own, 1), rows)]
    turn = jax.random.randint(jax.random.fold_in(own, 2), (rows, 1), 0, top)
    return jnp.take_along_axis(listing, (jnp.arange(top)[None, :] + turn) % top, axis=1)


def load_shares(count, total, bound, slope, full):
    weights = [(1 << 20) // math.isqrt(grade ** slope) + 1 for grade in range(1, count + 1)]
    largest = bound if full else min(bound, max(-(-total // count), total * weights[0] // sum(weights)))
    least = 1 if total - largest >= count - 1 else 0
    given, rest = [largest] + [least] * (count - 1), total - largest - least * (count - 1)
    while rest > 0:
        movable = [i for i in range(1, count) if given[i] < largest] or [i for i in range(1, count) if given[i] < bound]
        whole, left = sum([weights[i] for i in movable]), rest
        for i in movable:
            addition = min(bound - given[i], max(1, left * weights[i] // whole), rest)
            given[i] = given[i] + addition
            rest = rest - addition
    return np.array(given)


def centred(stream_key, shape, deviation, limit, cuts=(), held_as=jnp.bfloat16):
    values = deviation * jax.random.normal(stream_key, shape, jnp.float32)
    if cuts:
        values = values * steps_of(stream_key, shape, cuts, -0.22, 0.18)
    return jnp.clip(values, -limit, limit).astype(held_as)


def setup_inputs(seed: int = 0, part: int = 0) -> dict:
    seeds = jax.random.split(jax.random.key(seed), 12)
    part_keys = jax.random.split(jax.random.fold_in(seeds[11], part), 12)
    query_rows = draw_query_rows(jax.random.fold_in(jax.random.fold_in(seeds[11], part), 71), part)
    key_rows = draw_key_rows(jax.random.fold_in(jax.random.fold_in(seeds[11], part), 71), part)
    value_rows = centred(part_keys[2], (SEQS, SEQ_LEN, KVH * HD), 1.0, 6.0, ((0, 4), (1, 4)))
    residual_in = centred(part_keys[3], (SEQS, SEQ_LEN, D), 1.0, 6.0, ((0, 4), (1, 4)))
    out_proj = centred(seeds[4], (QH * HD, D), HD ** -0.5, 0.5, ((0, 4),))
    norm_gain = jnp.clip(1.0 + 0.18 * jax.random.normal(seeds[5], (D,), jnp.float32), 0.099609375, 1.8984375).astype(jnp.bfloat16)
    expert_ids_keys = jax.random.split(jax.random.fold_in(part_keys[6], 1), SEQS * SEQ_LEN // TOK_DEV)
    expert_ids_turns = jax.random.permutation(jax.random.fold_in(part_keys[6], 3), SEQS * SEQ_LEN // TOK_DEV)
    expert_ids = jax.vmap(lambda own, number: assign_block(jax.random.fold_in(part_keys[6], 2), own, number, TOK_DEV, EXPERTS, TOPK, CAP, 2))(expert_ids_keys, expert_ids_turns).reshape((SEQS, SEQ_LEN, TOPK))
    gate_weights = jnp.clip(jnp.exp(math.log(1.0) - 2.9996462 * jax.random.uniform(part_keys[7], (SEQS, SEQ_LEN, TOPK), jnp.float32) ** steps_of(part_keys[7], (SEQS, SEQ_LEN, TOPK), ((0, 4), (1, 4)), -0.2, 0.2)), 0.049804688, 1.0).astype(jnp.bfloat16)
    expert_gate = centred(seeds[8], (EXPERTS, D, FF), D ** -0.5, 0.125, ((0, 16),))
    expert_up = centred(seeds[9], (EXPERTS, D, FF), D ** -0.5, 0.125, ((0, 16),))
    expert_down = centred(seeds[10], (EXPERTS, FF, D), FF ** -0.5, 0.21875, ((0, 16),))
    return {"query_rows": query_rows, "key_rows": key_rows, "value_rows": value_rows, "residual_in": residual_in, "out_proj": out_proj, "norm_gain": norm_gain, "expert_ids": expert_ids, "gate_weights": gate_weights, "expert_gate": expert_gate, "expert_up": expert_up, "expert_down": expert_down}


def reference(query_rows, key_rows, value_rows, residual_in, out_proj, norm_gain, expert_ids, gate_weights, expert_gate, expert_up, expert_down):
    group = QH // KVH
    scale = 1.0 / HD ** 0.5
    length = SEQ_LEN
    query_heads = query_rows.reshape(SEQS, length, QH, HD).transpose(0, 2, 1, 3).reshape(SEQS * QH, length, HD)
    key_heads = key_rows.reshape(SEQS, length, KVH, HD).transpose(0, 2, 1, 3)
    value_heads = value_rows.reshape(SEQS, length, KVH, HD).transpose(0, 2, 1, 3)
    positions = jnp.arange(length, dtype=jnp.int32)
    causal = positions[:, None] >= positions[None, :]

    def one_head(index):
        seq_index = index // QH
        kv_index = index % QH // group
        scores = jnp.dot(query_heads[index].astype(jnp.float32), key_heads[seq_index, kv_index].astype(jnp.float32).T, precision=lax.Precision.HIGHEST) * scale
        scores = jnp.where(causal, scores, -1e+30)
        peak = lax.optimization_barrier(jnp.max(scores, axis=1, keepdims=True))
        weights = jnp.exp(scores - peak)
        probs = (weights / lax.optimization_barrier(jnp.sum(weights, axis=1, keepdims=True))).astype(jnp.bfloat16)
        probs = lax.optimization_barrier(probs)
        return jnp.dot(probs.astype(jnp.float32), value_heads[seq_index, kv_index].astype(jnp.float32), precision=lax.Precision.HIGHEST).astype(jnp.bfloat16)
    head_out = lax.map(one_head, jnp.arange(SEQS * QH, dtype=jnp.int32))
    attended = head_out.reshape(SEQS, QH, length, HD).transpose(0, 2, 1, 3).reshape(SEQS * length, QH * HD)
    projected = jnp.dot(attended, out_proj, preferred_element_type=jnp.float32)
    hidden = (residual_in.reshape(SEQS * length, D).astype(jnp.float32) + projected).astype(jnp.bfloat16)
    wide = hidden.astype(jnp.float32)
    normed = (wide * lax.rsqrt(lax.optimization_barrier(jnp.mean(wide * wide, axis=1, keepdims=True)) + 1e-06) * norm_gain.astype(jnp.float32)).astype(jnp.bfloat16)
    rows = SEQS * length
    flat_ids = expert_ids.reshape(-1).astype(jnp.int32)
    assigned = flat_ids.shape[0]
    flat_gates = gate_weights.reshape(-1)
    order = jnp.argsort(flat_ids, stable=True).astype(jnp.int32)
    sorted_ids = flat_ids[order]
    counts = jnp.zeros((EXPERTS,), jnp.int32).at[flat_ids].add(1)
    tiles = (counts + 127) // 128
    tile_end = jnp.cumsum(tiles).astype(jnp.int32)
    tile_first = tile_end - tiles
    row_first = (jnp.cumsum(counts) - counts).astype(jnp.int32)
    position = tile_first[sorted_ids] * 128 + jnp.arange(assigned, dtype=jnp.int32) - row_first[sorted_ids]
    n_tiles = assigned // 128 + EXPERTS
    slot_item = jnp.full((n_tiles * 128,), assigned, jnp.int32).at[position].set(order)
    tile_index = jnp.arange(n_tiles, dtype=jnp.int32)
    tile_owner = jnp.minimum(lax.optimization_barrier(jnp.sum((tile_end[None, :] <= tile_index[:, None]).astype(jnp.int32), axis=1)), EXPERTS - 1)
    padded_rows = jnp.concatenate([normed, jnp.zeros((1, D), jnp.bfloat16)], axis=0)
    padded_gates = jnp.concatenate([flat_gates, jnp.zeros((1,), jnp.bfloat16)], axis=0)
    slot_token = jnp.where(slot_item < assigned, slot_item // TOPK, rows).astype(jnp.int32)

    def tile_step(total, tile):
        owner = tile_owner[tile]
        tokens_here = lax.dynamic_slice_in_dim(slot_token, tile * 128, 128)
        items = lax.dynamic_slice_in_dim(slot_item, tile * 128, 128)
        inputs = padded_rows[tokens_here].astype(jnp.float32)
        gate_proj = jnp.dot(inputs, expert_gate[owner].astype(jnp.float32), precision=lax.Precision.HIGHEST)
        up_proj = jnp.dot(inputs, expert_up[owner].astype(jnp.float32), precision=lax.Precision.HIGHEST)
        inner = lax.optimization_barrier((jax.nn.silu(gate_proj) * up_proj).astype(jnp.bfloat16))
        result = jnp.dot(inner.astype(jnp.float32), expert_down[owner].astype(jnp.float32), precision=lax.Precision.HIGHEST)
        result = result * padded_gates[items].astype(jnp.float32)[:, None]
        rounded = lax.optimization_barrier(result.astype(jnp.bfloat16))
        return (total.at[tokens_here].add(rounded.astype(jnp.float32)), None)
    total, _ = lax.scan(tile_step, jnp.zeros((rows + 1, D), jnp.float32), tile_index)
    layer_out = (wide + total[:rows]).astype(jnp.bfloat16)
    return layer_out.reshape(SEQS, length, D)
```

```python
import jax
import jax.numpy as jnp
from jax import lax
from jax.experimental import pallas as pl
from jax.experimental.pallas import tpu as pltpu
from jax.sharding import PartitionSpec as P

D = 2048
HD = 128
QH = 16
KVH = 2


def attend_head(queries, keys_one, values_one, block):
    length = queries.shape[0]
    scale = 1.0 / queries.shape[1] ** 0.5
    pieces = []
    for part_index in range(length // block):
        stop = (part_index + 1) * block
        rows_here = queries[part_index * block : stop]
        scores = (
            jnp.einsum("qd,kd->qk", rows_here, keys_one[:stop], preferred_element_type=jnp.float32)
            * scale
        )
        row_pos = part_index * block + jnp.arange(block, dtype=jnp.int32)
        col_pos = jnp.arange(stop, dtype=jnp.int32)
        scores = jnp.where(row_pos[:, None] >= col_pos[None, :], scores, -1e30)
        peak = jnp.max(scores, axis=1, keepdims=True)
        weights = jnp.exp(scores - peak)
        probs = (weights / jnp.sum(weights, axis=1, keepdims=True)).astype(jnp.bfloat16)
        pieces.append(
            jnp.dot(probs, values_one[:stop], preferred_element_type=jnp.float32).astype(
                jnp.bfloat16
            )
        )
    return jnp.concatenate(pieces, axis=0)


def rank_in_expert(flat_ids, experts):
    items = flat_ids.shape[0]
    width = 128
    n_parts = items // width
    onehot = (
        (flat_ids[:, None] == jnp.arange(experts, dtype=jnp.int32)[None, :])
        .astype(jnp.bfloat16)
        .reshape(n_parts, width, experts)
    )
    lower = (
        jnp.arange(width, dtype=jnp.int32)[:, None] > jnp.arange(width, dtype=jnp.int32)[None, :]
    ).astype(jnp.bfloat16)
    within = jnp.einsum("ij,bje->bie", lower, onehot, preferred_element_type=jnp.float32)
    part_counts = jnp.sum(onehot.astype(jnp.float32), axis=1)
    earlier = jnp.cumsum(part_counts, axis=0) - part_counts
    ranks = jnp.sum((within + earlier[:, None, :]) * onehot.astype(jnp.float32), axis=2)
    return ranks.reshape(items).astype(jnp.int32)


def experts_kernel(gate_ref, row_ref, w_gate_ref, w_up_ref, w_down_ref, out_ref, packed, *, cap):
    gates = gate_ref[0]
    blocks, tokens = gates.shape
    named = gates > 0
    before = (
        lax.broadcasted_iota(jnp.int32, (tokens, tokens), 0)
        < lax.broadcasted_iota(jnp.int32, (tokens, tokens), 1)
    ).astype(jnp.bfloat16)
    rank = jnp.dot(named.astype(jnp.bfloat16), before, preferred_element_type=jnp.float32)
    slot = jnp.where(named, rank.astype(jnp.int32), -1)
    slots = lax.broadcasted_iota(jnp.int32, (cap, tokens), 0)
    picks = []
    weights = []
    for block in range(blocks):
        chosen = slots == slot[block : block + 1, :]
        pick = chosen.astype(jnp.bfloat16)
        picks.append(pick)
        weights.append(
            jnp.sum(jnp.where(chosen, gates[block : block + 1, :], 0.0), axis=1, keepdims=True)
        )
        packed[block * cap : (block + 1) * cap, :] = jnp.dot(
            pick,
            row_ref[block * tokens : (block + 1) * tokens, :],
            preferred_element_type=jnp.float32,
        ).astype(jnp.bfloat16)
    rows = packed[...]
    gate_proj = jnp.dot(rows, w_gate_ref[...], preferred_element_type=jnp.float32)
    up_proj = jnp.dot(rows, w_up_ref[...], preferred_element_type=jnp.float32)
    inner = (gate_proj / (1.0 + jnp.exp(-gate_proj)) * up_proj).astype(jnp.bfloat16)
    result = jnp.dot(inner, w_down_ref[...], preferred_element_type=jnp.float32)
    for block in range(blocks):
        part = (result[block * cap : (block + 1) * cap] * weights[block]).astype(jnp.bfloat16)
        out_ref[block * tokens : (block + 1) * tokens, :] = lax.dot_general(
            picks[block],
            part,
            (((0,), (0,)), ((), ())),
            preferred_element_type=jnp.float32,
        ).astype(jnp.bfloat16)


def experts_on_rows(gates, rows, w_gate, w_up, w_down, cap, blocks):
    parts, tokens = gates.shape
    width = rows.shape[1]
    hidden_units = w_gate.shape[1]
    steps = parts // blocks
    fixed = lambda step: (0, 0)
    return pl.pallas_call(
        lambda *refs: experts_kernel(*refs, cap=cap),
        grid=(steps,),
        in_specs=[
            pl.BlockSpec((1, blocks, tokens), lambda step: (step, 0, 0)),
            pl.BlockSpec((blocks * tokens, width), lambda step: (step, 0)),
            pl.BlockSpec((width, hidden_units), fixed),
            pl.BlockSpec((width, hidden_units), fixed),
            pl.BlockSpec((hidden_units, width), fixed),
        ],
        out_specs=pl.BlockSpec((blocks * tokens, width), lambda step: (step, 0)),
        out_shape=jax.ShapeDtypeStruct(rows.shape, jnp.bfloat16),
        scratch_shapes=[pltpu.VMEM((blocks * cap, width), jnp.bfloat16)],
        compiler_params=pltpu.CompilerParams(vmem_limit_bytes=56 * 1024 * 1024),
        cost_estimate=pl.CostEstimate(
            flops=6 * parts * cap * width * hidden_units,
            bytes_accessed=4 * rows.size + 6 * width * hidden_units,
            transcendentals=parts * cap * hidden_units,
        ),
    )(gates.reshape(steps, blocks, tokens), rows, w_gate, w_up, w_down)


def per_device(
    query_rows,
    key_rows,
    value_rows,
    residual_in,
    out_proj,
    norm_gain,
    expert_ids,
    gate_weights,
    expert_gate,
    expert_up,
    expert_down,
):
    tokens = query_rows.shape[1]
    n_seq = lax.axis_size("seq")
    n_sub = lax.axis_size("sub")
    heads_here = QH // n_seq
    group = QH // KVH
    query_local = lax.all_to_all(query_rows, "seq", split_axis=2, concat_axis=1, tiled=True)
    key_full, value_full = (
        lax.all_gather(key_rows, "seq", axis=1, tiled=True),
        lax.all_gather(value_rows, "seq", axis=1, tiled=True),
    )
    first_head = lax.axis_index("seq") * heads_here
    key_list = []
    value_list = []
    for head in range(heads_here):
        kv_start = (first_head + head) // group * HD
        key_list.append(lax.dynamic_slice_in_dim(key_full[0], kv_start, HD, 1))
        value_list.append(lax.dynamic_slice_in_dim(value_full[0], kv_start, HD, 1))
    length = query_local.shape[1]
    block = min(length, max(512, length // 8))
    outputs = [
        attend_head(
            query_local[0, :, head * HD : (head + 1) * HD], key_list[head], value_list[head], block
        )
        for head in range(heads_here)
    ]
    head_block = jnp.concatenate(outputs, axis=1)[None]
    attended = lax.all_to_all(head_block, "seq", split_axis=1, concat_axis=2, tiled=True)[0]
    projected = jnp.dot(
        attended,
        lax.all_gather(out_proj, "seq", axis=0, tiled=True),
        preferred_element_type=jnp.float32,
    )
    hidden = (residual_in[0].astype(jnp.float32) + projected).astype(jnp.bfloat16)
    wide = hidden.astype(jnp.float32)
    normed = (
        wide
        * lax.rsqrt(jnp.mean(wide * wide, axis=1, keepdims=True) + 1e-06)
        * norm_gain.astype(jnp.float32)
    ).astype(jnp.bfloat16)
    topk = expert_ids.shape[2]
    experts = n_seq * n_sub
    cap = max(2, (5 * tokens * topk + 4 * experts - 1) // (4 * experts))
    if experts <= 2 * topk:
        axes = ("seq", "sub")
        table = jnp.sum(
            jnp.where(
                expert_ids[0][None] == jnp.arange(experts, dtype=jnp.int32)[:, None, None],
                gate_weights[0].astype(jnp.float32)[None],
                0.0,
            ),
            axis=2,
        ).astype(jnp.bfloat16)
        tables = lax.all_gather(table, axes, axis=0, tiled=False)
        mine = lax.axis_index("seq") * n_sub + lax.axis_index("sub")
        gates = lax.dynamic_index_in_dim(tables, mine, 1, keepdims=False).astype(jnp.float32)
        rows = lax.all_gather(normed, axes, axis=0, tiled=True)
        parts = experts_on_rows(gates, rows, expert_gate[0], expert_up[0], expert_down[0], cap, 4)
        mixture = lax.psum_scatter(parts, axes, scatter_dimension=0, tiled=True)
        return (wide + mixture.astype(jnp.float32)).astype(jnp.bfloat16)[None]
    flat_ids = expert_ids[0].reshape(-1)
    items = flat_ids.shape[0]
    ranks = rank_in_expert(flat_ids, experts)
    slot_of = flat_ids * cap + ranks
    slots_out = experts * cap
    item_of_slot = (
        jnp.full((slots_out,), items, jnp.int32).at[slot_of].set(jnp.arange(items, dtype=jnp.int32))
    )
    padded_rows = jnp.concatenate([normed, jnp.zeros((1, D), jnp.bfloat16)], axis=0)
    padded_gates = jnp.concatenate(
        [gate_weights[0].reshape(-1), jnp.zeros((1,), jnp.bfloat16)], axis=0
    )
    token_of_slot = jnp.where(item_of_slot < items, item_of_slot // topk, tokens)
    send_rows = padded_rows[token_of_slot].reshape(experts, cap, D)
    send_gates = padded_gates[item_of_slot].reshape(experts, cap)
    recv_rows, recv_gates = (
        lax.all_to_all(send_rows, ("seq", "sub"), split_axis=0, concat_axis=0, tiled=True),
        lax.all_to_all(send_gates, ("seq", "sub"), split_axis=0, concat_axis=0, tiled=True),
    )
    slots_in = experts * cap
    valid = recv_gates > 0
    counts = jnp.sum(valid.astype(jnp.int32), axis=1)
    offsets = jnp.cumsum(counts) - counts
    dest = jnp.where(
        valid, offsets[:, None] + jnp.arange(cap, dtype=jnp.int32)[None, :], slots_in
    ).reshape(-1)
    source_of = (
        jnp.full((slots_in + 1,), slots_in, jnp.int32)
        .at[dest]
        .set(jnp.arange(slots_in, dtype=jnp.int32))[:slots_in]
    )
    compact_rows = jnp.concatenate(
        [recv_rows.reshape(slots_in, D), jnp.zeros((1, D), jnp.bfloat16)], axis=0
    )[source_of]
    compact_gates = jnp.concatenate(
        [recv_gates.reshape(-1), jnp.zeros((1,), jnp.bfloat16)], axis=0
    )[source_of].astype(jnp.float32)
    filled = jnp.sum(counts)
    n_blocks = (filled + slots_in - 1) // slots_in
    w_gate = expert_gate[0]
    w_up = expert_up[0]
    w_down = expert_down[0]

    def expert_block(index, results):
        gate_proj = jnp.dot(compact_rows, w_gate, preferred_element_type=jnp.float32)
        up_proj = jnp.dot(compact_rows, w_up, preferred_element_type=jnp.float32)
        inner = (jax.nn.silu(gate_proj) * up_proj).astype(jnp.bfloat16)
        weighted = (
            jnp.dot(inner, w_down, preferred_element_type=jnp.float32) * compact_gates[:, None]
        )
        return weighted.astype(jnp.bfloat16)

    results = lax.fori_loop(0, n_blocks, expert_block, jnp.zeros((slots_in, D), jnp.bfloat16))
    returned = jnp.concatenate([results, jnp.zeros((1, D), jnp.bfloat16)], axis=0)[dest].reshape(
        experts, cap, D
    )
    back = lax.all_to_all(
        returned, ("seq", "sub"), split_axis=0, concat_axis=0, tiled=True
    ).reshape(slots_out, D)
    gathered = back[slot_of].reshape(tokens, topk, D).astype(jnp.float32)
    mixture = jnp.sum(gathered, axis=1)
    return (wide + mixture).astype(jnp.bfloat16)[None]


def solution(mesh):
    placed = (
        P(("grp", "sub"), "seq", None),
        P(("grp", "sub"), "seq", None),
        P(("grp", "sub"), "seq", None),
        P(("grp", "sub"), "seq", None),
        P("seq", None),
        P(),
        P(("grp", "sub"), "seq", None),
        P(("grp", "sub"), "seq", None),
        P(("seq", "sub"), None, None),
        P(("seq", "sub"), None, None),
        P(("seq", "sub"), None, None),
    )
    return jax.shard_map(
        per_device,
        mesh=mesh,
        in_specs=placed,
        out_specs=P(("grp", "sub"), "seq", None),
        check_vma=False,
    )
```

```python
import functools

import jax
import jax.numpy as jnp
from jax import lax
from jax.experimental import pallas as pl
from jax.experimental.pallas import tpu as pltpu
from jax.sharding import PartitionSpec as P

D = 2048
HD = 128
QH = 16
KVH = 2


def attend_head(queries, keys_one, values_one, block):
    length = queries.shape[0]
    scale = 1.0 / queries.shape[1] ** 0.5
    pieces = []
    for part_index in range(length // block):
        stop = (part_index + 1) * block
        rows_here = queries[part_index * block : stop]
        scores = (
            jnp.einsum("qd,kd->qk", rows_here, keys_one[:stop], preferred_element_type=jnp.float32)
            * scale
        )
        row_pos = part_index * block + jnp.arange(block, dtype=jnp.int32)
        col_pos = jnp.arange(stop, dtype=jnp.int32)
        scores = jnp.where(row_pos[:, None] >= col_pos[None, :], scores, -1e30)
        peak = jnp.max(scores, axis=1, keepdims=True)
        weights = jnp.exp(scores - peak)
        probs = (weights / jnp.sum(weights, axis=1, keepdims=True)).astype(jnp.bfloat16)
        pieces.append(
            jnp.dot(probs, values_one[:stop], preferred_element_type=jnp.float32).astype(
                jnp.bfloat16
            )
        )
    return jnp.concatenate(pieces, axis=0)


def rank_in_expert(flat_ids, experts):
    items = flat_ids.shape[0]
    width = 128
    n_parts = items // width
    onehot = (
        (flat_ids[:, None] == jnp.arange(experts, dtype=jnp.int32)[None, :])
        .astype(jnp.bfloat16)
        .reshape(n_parts, width, experts)
    )
    lower = (
        jnp.arange(width, dtype=jnp.int32)[:, None] > jnp.arange(width, dtype=jnp.int32)[None, :]
    ).astype(jnp.bfloat16)
    within = jnp.einsum("ij,bje->bie", lower, onehot, preferred_element_type=jnp.float32)
    part_counts = jnp.sum(onehot.astype(jnp.float32), axis=1)
    earlier = jnp.cumsum(part_counts, axis=0) - part_counts
    ranks = jnp.sum((within + earlier[:, None, :]) * onehot.astype(jnp.float32), axis=2)
    return ranks.reshape(items).astype(jnp.int32)


def attend_kernel(place_ref, query_ref, *refs, scale):
    kv_refs, (w_own_ref, w_other_ref, out_ref, keys, values, heads) = refs[:4], refs[4:]
    rows = keys.shape[0] // 4
    head_size = keys.shape[1]
    core = place_ref[0]
    query_start = pl.multiple_of(place_ref[1], head_size)
    row_pos = place_ref[2] * rows + lax.broadcasted_iota(jnp.int32, (rows, 1), 0)
    lane = lax.broadcasted_iota(jnp.int32, (1, rows), 1)
    col_pos = jnp.concatenate([place_ref[3 + part] * rows + lane for part in range(4)], axis=1)
    allowed = row_pos >= col_pos
    for part, kv_ref in enumerate(kv_refs):
        start = kv_ref.shape[1] - 2 * head_size
        keys[part * rows : (part + 1) * rows, :] = kv_ref[:, start : start + head_size]
        values[part * rows : (part + 1) * rows, :] = kv_ref[:, start + head_size :]
    key_block = keys[...]
    value_block = values[...]
    for head in range(heads.shape[1] // head_size):
        query = query_ref[:, pl.ds(query_start + head * head_size, head_size)]
        scores = (
            lax.dot_general(
                query, key_block, (((1,), (1,)), ((), ())), preferred_element_type=jnp.float32
            )
            * scale
        )
        scores = jnp.where(allowed, scores, -1e30)
        weights = jnp.exp(scores - jnp.max(scores, axis=1, keepdims=True))
        probs = (weights / jnp.sum(weights, axis=1, keepdims=True)).astype(jnp.bfloat16)
        heads[:, head * head_size : (head + 1) * head_size] = jnp.dot(
            probs, value_block, preferred_element_type=jnp.float32
        ).astype(jnp.bfloat16)
    half = heads.shape[1] // 2
    own = heads[:, pl.ds(pl.multiple_of(core * half, half), half)]
    other = heads[:, pl.ds(pl.multiple_of((1 - core) * half, half), half)]
    out_ref[...] = (
        jnp.dot(own, w_own_ref[...], preferred_element_type=jnp.float32)
        + jnp.dot(other, w_other_ref[...], preferred_element_type=jnp.float32)
    ).astype(out_ref.dtype)


def attend(place, queries, kv_parts, w_own, w_other, dtype):
    tokens = queries.shape[0]
    width = w_own.shape[1]
    chip_width = 2 * w_own.shape[0]
    return pl.pallas_call(
        functools.partial(attend_kernel, scale=1.0 / HD**0.5),
        in_specs=[pl.BlockSpec(memory_space=pltpu.SMEM)]
        + [pl.BlockSpec(memory_space=pltpu.VMEM)] * 7,
        out_specs=pl.BlockSpec(memory_space=pltpu.VMEM),
        out_shape=jax.ShapeDtypeStruct((tokens, width), dtype),
        scratch_shapes=[
            pltpu.VMEM((4 * tokens, HD), jnp.bfloat16),
            pltpu.VMEM((4 * tokens, HD), jnp.bfloat16),
            pltpu.VMEM((tokens, chip_width), jnp.bfloat16),
        ],
        compiler_params=pltpu.CompilerParams(vmem_limit_bytes=32 * 1024 * 1024),
        cost_estimate=pl.CostEstimate(
            flops=16 * tokens * tokens * chip_width + 2 * tokens * chip_width * width,
            bytes_accessed=4 * w_own.size + 4 * tokens * width,
            transcendentals=4 * tokens * tokens * chip_width // HD,
        ),
    )(place, queries, *kv_parts, w_own, w_other)


def norm_kernel(residual_ref, own_ref, other_ref, gain_ref, hidden_ref, normed_ref):
    hidden = (
        residual_ref[...].astype(jnp.float32) + own_ref[...] + other_ref[...].astype(jnp.float32)
    ).astype(jnp.bfloat16)
    hidden_ref[...] = hidden
    wide = hidden.astype(jnp.float32)
    normed_ref[...] = (
        wide
        * lax.rsqrt(jnp.mean(wide * wide, axis=1, keepdims=True) + 1e-06)
        * gain_ref[...].astype(jnp.float32)
    ).astype(jnp.bfloat16)


def add_and_norm(residual, own, other, gain):
    return pl.pallas_call(
        norm_kernel,
        in_specs=[pl.BlockSpec(memory_space=pltpu.VMEM)] * 4,
        out_specs=[pl.BlockSpec(memory_space=pltpu.VMEM)] * 2,
        out_shape=[jax.ShapeDtypeStruct(residual.shape, jnp.bfloat16)] * 2,
        compiler_params=pltpu.CompilerParams(vmem_limit_bytes=32 * 1024 * 1024),
    )(residual, own, other, gain)


def experts_kernel(gate_ref, *refs, cap):
    row_refs, refs = refs[:4], refs[4:]
    w_gate_ref, w_up_ref, w_down_ref, own_ref, across_ref, other_ref, packed, total = refs
    tokens = row_refs[0].shape[0]
    step = pl.program_id(0)
    gates = gate_ref[...]
    named = gates > 0
    before = (
        lax.broadcasted_iota(jnp.int32, (tokens, tokens), 0)
        < lax.broadcasted_iota(jnp.int32, (tokens, tokens), 1)
    ).astype(jnp.bfloat16)
    rank = jnp.dot(named.astype(jnp.bfloat16), before, preferred_element_type=jnp.float32)
    slot = jnp.where(named, rank.astype(jnp.int32), -1)
    slots = lax.broadcasted_iota(jnp.int32, (cap, tokens), 0)

    def chosen_of(block):
        return slots == slot[block : block + 1, :]

    @pl.when(step == 0)
    def _():
        for block in range(4):
            packed[block * cap : (block + 1) * cap, :] = jnp.dot(
                chosen_of(block).astype(jnp.bfloat16),
                row_refs[block][...],
                preferred_element_type=jnp.float32,
            ).astype(jnp.bfloat16)

    rows = packed[...]
    gate_proj = jnp.dot(rows, w_gate_ref[...], preferred_element_type=jnp.float32)
    up_proj = jnp.dot(rows, w_up_ref[...], preferred_element_type=jnp.float32)
    inner = (gate_proj / (1.0 + jnp.exp(-gate_proj)) * up_proj).astype(jnp.bfloat16)
    result = jnp.dot(inner, w_down_ref[...], preferred_element_type=jnp.float32)

    @pl.when(step == 0)
    def _():
        total[...] = result

    @pl.when(step > 0)
    def _():
        total[...] += result

    @pl.when(step == pl.num_programs(0) - 1)
    def _():
        targets = (
            own_ref.at[...],
            other_ref.at[0:tokens],
            across_ref.at[...],
            other_ref.at[tokens : 2 * tokens],
        )
        for block in range(4):
            chosen = chosen_of(block)
            weights = jnp.sum(
                jnp.where(chosen, gates[block : block + 1, :], 0.0), axis=1, keepdims=True
            )
            part = (total[block * cap : (block + 1) * cap, :] * weights).astype(jnp.bfloat16)
            targets[block][...] = lax.dot_general(
                chosen.astype(jnp.bfloat16),
                part,
                (((0,), (0,)), ((), ())),
                preferred_element_type=jnp.float32,
            ).astype(jnp.bfloat16)


def experts_on_rows(gates, row_blocks, w_gate, w_up, w_down, cap):
    tokens, width = row_blocks[0].shape
    hidden_units = w_gate.shape[1]
    chunk = hidden_units // 3 if hidden_units % 384 == 0 else hidden_units
    whole = pl.BlockSpec((tokens, width), lambda step: (0, 0))
    return pl.pallas_call(
        functools.partial(experts_kernel, cap=cap),
        grid=(hidden_units // chunk,),
        in_specs=[
            pl.BlockSpec((4, tokens), lambda step: (0, 0)),
            whole,
            whole,
            whole,
            whole,
            pl.BlockSpec((width, chunk), lambda step: (0, step)),
            pl.BlockSpec((width, chunk), lambda step: (0, step)),
            pl.BlockSpec((chunk, width), lambda step: (step, 0)),
        ],
        out_specs=[whole, whole, pl.BlockSpec((2 * tokens, width), lambda step: (0, 0))],
        out_shape=[
            jax.ShapeDtypeStruct((tokens, width), jnp.bfloat16),
            jax.ShapeDtypeStruct((tokens, width), jnp.bfloat16),
            jax.ShapeDtypeStruct((2 * tokens, width), jnp.bfloat16),
        ],
        scratch_shapes=[
            pltpu.VMEM((4 * cap, width), jnp.bfloat16),
            pltpu.VMEM((4 * cap, width), jnp.float32),
        ],
        compiler_params=pltpu.CompilerParams(vmem_limit_bytes=40 * 1024 * 1024),
        cost_estimate=pl.CostEstimate(
            flops=24 * cap * width * hidden_units,
            bytes_accessed=16 * tokens * width + 6 * width * hidden_units,
            transcendentals=4 * cap * hidden_units,
        ),
    )(gates, *row_blocks, w_gate, w_up, w_down)


def gathered_plan(
    query_rows,
    key_rows,
    value_rows,
    residual_in,
    out_proj,
    norm_gain,
    expert_ids,
    gate_weights,
    expert_gate,
    expert_up,
    expert_down,
    cap,
):
    n_seq = lax.axis_size("seq")
    n_sub = lax.axis_size("sub")
    experts = n_seq * n_sub
    place = lax.axis_index("seq")
    core = place % 2
    chip = place // 2
    twin = [(index, index ^ 1) for index in range(n_seq)]
    across = [(index, (index + 2) % n_seq) for index in range(n_seq)]
    diagonal = [(index, (index ^ 1) ^ 2) for index in range(n_seq)]
    order = [0] + list(range(1, n_sub, 2)) + list(reversed(range(2, n_sub, 2)))

    def ring(steps):
        return [(order[at], order[(at + steps) % n_sub]) for at in range(n_sub)]

    queries = query_rows[0]
    chip_width = queries.shape[1] // 2

    def kv_of(head):
        start = head * HD
        return jnp.concatenate(
            [
                lax.dynamic_slice_in_dim(key_rows[0], start, HD, 1),
                lax.dynamic_slice_in_dim(value_rows[0], start, HD, 1),
            ],
            axis=1,
        )

    kv_here = kv_of(chip)
    kv_away = kv_of(1 - chip)
    outgoing = jnp.concatenate(
        [lax.dynamic_slice_in_dim(queries, (1 - chip) * chip_width, chip_width, 1), kv_away], axis=1
    )
    incoming = lax.ppermute(outgoing, "seq", across)
    kv_twin = lax.ppermute(kv_here, "seq", twin)
    kv_diagonal = lax.ppermute(kv_away, "seq", diagonal)
    w_other = lax.ppermute(out_proj, "seq", twin)

    table = jnp.sum(
        jnp.where(
            expert_ids[0][None] == jnp.arange(experts, dtype=jnp.int32)[:, None, None],
            gate_weights[0].astype(jnp.float32)[None],
            0.0,
        ),
        axis=2,
    ).astype(jnp.bfloat16)
    quad = jnp.stack(
        [
            table,
            lax.ppermute(table, "seq", twin),
            lax.ppermute(table, "seq", across),
            lax.ppermute(table, "seq", diagonal),
        ]
    )
    quads = [quad] + [lax.ppermute(quad, "sub", ring(steps)) for steps in range(1, n_sub)]
    mine = place * n_sub + lax.axis_index("sub")
    gates = lax.dynamic_index_in_dim(jnp.stack(quads), mine, 2, keepdims=False).astype(jnp.float32)

    kv_parts = (kv_here, kv_twin, incoming, kv_diagonal)
    columns = [place, place ^ 1, place ^ 2, place ^ 3]

    def place_of(query_start, row_block):
        return jnp.stack([core, query_start, row_block] + columns).astype(jnp.int32)

    sent = attend(place_of(0 * place, place ^ 2), incoming, kv_parts, out_proj, w_other, jnp.bfloat16)
    projected_across = lax.ppermute(sent, "seq", across)
    projected = attend(
        place_of(chip * chip_width, place), queries, kv_parts, out_proj, w_other, jnp.float32
    )
    hidden, normed = add_and_norm(residual_in[0], projected, projected_across, norm_gain[None])

    rows = normed
    sums = []
    for step in range(n_sub):
        rows_twin = lax.ppermute(rows, "seq", twin)
        rows_across = lax.ppermute(rows, "seq", across)
        rows_diagonal = lax.ppermute(rows_across, "seq", twin)
        blocks = (rows, rows_twin, rows_across, rows_diagonal)
        if step < n_sub - 1:
            rows = lax.ppermute(rows, "sub", ring(1))
        sums.append(
            experts_on_rows(gates[step], blocks, expert_gate[0], expert_up[0], expert_down[0], cap)
        )
    tokens = queries.shape[0]
    carried = None
    for step in list(range(1, n_sub)) + [0]:
        own, away, other = sums[step]
        met = lax.ppermute(other, "seq", twin).astype(jnp.float32)
        away = (away.astype(jnp.float32) + met[tokens:]).astype(jnp.bfloat16)
        part = (
            own.astype(jnp.float32)
            + met[:tokens]
            + lax.ppermute(away, "seq", across).astype(jnp.float32)
        )
        if carried is not None:
            part = part + carried.astype(jnp.float32)
        if step:
            carried = lax.ppermute(part.astype(jnp.bfloat16), "sub", ring(1))
    return (hidden.astype(jnp.float32) + part).astype(jnp.bfloat16)[None]


def per_device(
    query_rows,
    key_rows,
    value_rows,
    residual_in,
    out_proj,
    norm_gain,
    expert_ids,
    gate_weights,
    expert_gate,
    expert_up,
    expert_down,
):
    tokens = query_rows.shape[1]
    n_seq = lax.axis_size("seq")
    n_sub = lax.axis_size("sub")
    experts = n_seq * n_sub
    topk = expert_ids.shape[2]
    cap = max(2, (5 * tokens * topk + 4 * experts - 1) // (4 * experts))
    if n_seq == 2 * KVH and KVH == 2 and experts <= 2 * topk and cap % 16 == 0:
        return gathered_plan(
            query_rows,
            key_rows,
            value_rows,
            residual_in,
            out_proj,
            norm_gain,
            expert_ids,
            gate_weights,
            expert_gate,
            expert_up,
            expert_down,
            cap,
        )
    heads_here = QH // n_seq
    group = QH // KVH
    query_local = lax.all_to_all(query_rows, "seq", split_axis=2, concat_axis=1, tiled=True)
    key_full, value_full = (
        lax.all_gather(key_rows, "seq", axis=1, tiled=True),
        lax.all_gather(value_rows, "seq", axis=1, tiled=True),
    )
    first_head = lax.axis_index("seq") * heads_here
    key_list = []
    value_list = []
    for head in range(heads_here):
        kv_start = (first_head + head) // group * HD
        key_list.append(lax.dynamic_slice_in_dim(key_full[0], kv_start, HD, 1))
        value_list.append(lax.dynamic_slice_in_dim(value_full[0], kv_start, HD, 1))
    length = query_local.shape[1]
    block = min(length, max(512, length // 8))
    outputs = [
        attend_head(
            query_local[0, :, head * HD : (head + 1) * HD], key_list[head], value_list[head], block
        )
        for head in range(heads_here)
    ]
    head_block = jnp.concatenate(outputs, axis=1)[None]
    attended = lax.all_to_all(head_block, "seq", split_axis=1, concat_axis=2, tiled=True)[0]
    projected = jnp.dot(
        attended,
        lax.all_gather(out_proj, "seq", axis=0, tiled=True),
        preferred_element_type=jnp.float32,
    )
    hidden = (residual_in[0].astype(jnp.float32) + projected).astype(jnp.bfloat16)
    wide = hidden.astype(jnp.float32)
    normed = (
        wide
        * lax.rsqrt(jnp.mean(wide * wide, axis=1, keepdims=True) + 1e-06)
        * norm_gain.astype(jnp.float32)
    ).astype(jnp.bfloat16)
    flat_ids = expert_ids[0].reshape(-1)
    items = flat_ids.shape[0]
    ranks = rank_in_expert(flat_ids, experts)
    slot_of = flat_ids * cap + ranks
    slots_out = experts * cap
    item_of_slot = (
        jnp.full((slots_out,), items, jnp.int32).at[slot_of].set(jnp.arange(items, dtype=jnp.int32))
    )
    padded_rows = jnp.concatenate([normed, jnp.zeros((1, D), jnp.bfloat16)], axis=0)
    padded_gates = jnp.concatenate(
        [gate_weights[0].reshape(-1), jnp.zeros((1,), jnp.bfloat16)], axis=0
    )
    token_of_slot = jnp.where(item_of_slot < items, item_of_slot // topk, tokens)
    send_rows = padded_rows[token_of_slot].reshape(experts, cap, D)
    send_gates = padded_gates[item_of_slot].reshape(experts, cap)
    recv_rows, recv_gates = (
        lax.all_to_all(send_rows, ("seq", "sub"), split_axis=0, concat_axis=0, tiled=True),
        lax.all_to_all(send_gates, ("seq", "sub"), split_axis=0, concat_axis=0, tiled=True),
    )
    slots_in = experts * cap
    valid = recv_gates > 0
    counts = jnp.sum(valid.astype(jnp.int32), axis=1)
    offsets = jnp.cumsum(counts) - counts
    dest = jnp.where(
        valid, offsets[:, None] + jnp.arange(cap, dtype=jnp.int32)[None, :], slots_in
    ).reshape(-1)
    source_of = (
        jnp.full((slots_in + 1,), slots_in, jnp.int32)
        .at[dest]
        .set(jnp.arange(slots_in, dtype=jnp.int32))[:slots_in]
    )
    compact_rows = jnp.concatenate(
        [recv_rows.reshape(slots_in, D), jnp.zeros((1, D), jnp.bfloat16)], axis=0
    )[source_of]
    compact_gates = jnp.concatenate(
        [recv_gates.reshape(-1), jnp.zeros((1,), jnp.bfloat16)], axis=0
    )[source_of].astype(jnp.float32)
    filled = jnp.sum(counts)
    n_blocks = (filled + slots_in - 1) // slots_in
    w_gate = expert_gate[0]
    w_up = expert_up[0]
    w_down = expert_down[0]

    def expert_block(index, results):
        gate_proj = jnp.dot(compact_rows, w_gate, preferred_element_type=jnp.float32)
        up_proj = jnp.dot(compact_rows, w_up, preferred_element_type=jnp.float32)
        inner = (jax.nn.silu(gate_proj) * up_proj).astype(jnp.bfloat16)
        weighted = (
            jnp.dot(inner, w_down, preferred_element_type=jnp.float32) * compact_gates[:, None]
        )
        return weighted.astype(jnp.bfloat16)

    results = lax.fori_loop(0, n_blocks, expert_block, jnp.zeros((slots_in, D), jnp.bfloat16))
    returned = jnp.concatenate([results, jnp.zeros((1, D), jnp.bfloat16)], axis=0)[dest].reshape(
        experts, cap, D
    )
    back = lax.all_to_all(
        returned, ("seq", "sub"), split_axis=0, concat_axis=0, tiled=True
    ).reshape(slots_out, D)
    gathered = back[slot_of].reshape(tokens, topk, D).astype(jnp.float32)
    mixture = jnp.sum(gathered, axis=1)
    return (wide + mixture).astype(jnp.bfloat16)[None]


def solution(mesh):
    placed = (
        P(("grp", "sub"), "seq", None),
        P(("grp", "sub"), "seq", None),
        P(("grp", "sub"), "seq", None),
        P(("grp", "sub"), "seq", None),
        P("seq", None),
        P(),
        P(("grp", "sub"), "seq", None),
        P(("grp", "sub"), "seq", None),
        P(("seq", "sub"), None, None),
        P(("seq", "sub"), None, None),
        P(("seq", "sub"), None, None),
    )
    return jax.shard_map(
        per_device,
        mesh=mesh,
        in_specs=placed,
        out_specs=P(("grp", "sub"), "seq", None),
        check_vma=False,
    )
```

```python
import functools

import jax
import jax.numpy as jnp
from jax import lax
from jax.experimental import pallas as pl
from jax.experimental.pallas import tpu as pltpu
from jax.sharding import PartitionSpec as P

D = 2048
HD = 128
QH = 16
KVH = 2


def attend_head(queries, keys_one, values_one, block):
    length = queries.shape[0]
    scale = 1.0 / queries.shape[1] ** 0.5
    pieces = []
    for part_index in range(length // block):
        stop = (part_index + 1) * block
        rows_here = queries[part_index * block : stop]
        scores = (
            jnp.einsum("qd,kd->qk", rows_here, keys_one[:stop], preferred_element_type=jnp.float32)
            * scale
        )
        row_pos = part_index * block + jnp.arange(block, dtype=jnp.int32)
        col_pos = jnp.arange(stop, dtype=jnp.int32)
        scores = jnp.where(row_pos[:, None] >= col_pos[None, :], scores, -1e30)
        peak = jnp.max(scores, axis=1, keepdims=True)
        weights = jnp.exp(scores - peak)
        probs = (weights / jnp.sum(weights, axis=1, keepdims=True)).astype(jnp.bfloat16)
        pieces.append(
            jnp.dot(probs, values_one[:stop], preferred_element_type=jnp.float32).astype(
                jnp.bfloat16
            )
        )
    return jnp.concatenate(pieces, axis=0)


def rank_in_expert(flat_ids, experts):
    items = flat_ids.shape[0]
    width = 128
    n_parts = items // width
    onehot = (
        (flat_ids[:, None] == jnp.arange(experts, dtype=jnp.int32)[None, :])
        .astype(jnp.bfloat16)
        .reshape(n_parts, width, experts)
    )
    lower = (
        jnp.arange(width, dtype=jnp.int32)[:, None] > jnp.arange(width, dtype=jnp.int32)[None, :]
    ).astype(jnp.bfloat16)
    within = jnp.einsum("ij,bje->bie", lower, onehot, preferred_element_type=jnp.float32)
    part_counts = jnp.sum(onehot.astype(jnp.float32), axis=1)
    earlier = jnp.cumsum(part_counts, axis=0) - part_counts
    ranks = jnp.sum((within + earlier[:, None, :]) * onehot.astype(jnp.float32), axis=2)
    return ranks.reshape(items).astype(jnp.int32)


def attend_kernel(place_ref, query_ref, *refs, scale):
    kv_refs, (w_own_ref, w_other_ref, out_ref, keys, values, heads, w_own, w_other, done) = (
        refs[:4],
        refs[4:],
    )
    fetches = [
        pltpu.make_async_copy(w_own_ref, w_own, done.at[0]),
        pltpu.make_async_copy(w_other_ref, w_other, done.at[1]),
    ]
    for fetch in fetches:
        fetch.start()
    rows = keys.shape[0] // 4
    head_size = keys.shape[1]
    core = place_ref[0]
    query_start = pl.multiple_of(place_ref[1], head_size)
    row_pos = place_ref[2] * rows + lax.broadcasted_iota(jnp.int32, (rows, 1), 0)
    lane = lax.broadcasted_iota(jnp.int32, (1, rows), 1)
    col_pos = jnp.concatenate([place_ref[3 + part] * rows + lane for part in range(4)], axis=1)
    allowed = row_pos >= col_pos
    for part, kv_ref in enumerate(kv_refs):
        start = kv_ref.shape[1] - 2 * head_size
        keys[part * rows : (part + 1) * rows, :] = kv_ref[:, start : start + head_size]
        values[part * rows : (part + 1) * rows, :] = kv_ref[:, start + head_size :]
    key_block = keys[...]
    value_block = values[...]
    for head in range(heads.shape[1] // head_size):
        query = query_ref[:, pl.ds(query_start + head * head_size, head_size)]
        scores = (
            lax.dot_general(
                query, key_block, (((1,), (1,)), ((), ())), preferred_element_type=jnp.float32
            )
            * scale
        )
        scores = jnp.where(allowed, scores, -1e30)
        weights = jnp.exp(scores - jnp.max(scores, axis=1, keepdims=True))
        probs = (weights / jnp.sum(weights, axis=1, keepdims=True)).astype(jnp.bfloat16)
        heads[:, head * head_size : (head + 1) * head_size] = jnp.dot(
            probs, value_block, preferred_element_type=jnp.float32
        ).astype(jnp.bfloat16)
    for fetch in fetches:
        fetch.wait()
    half = heads.shape[1] // 2
    own = heads[:, pl.ds(pl.multiple_of(core * half, half), half)]
    other = heads[:, pl.ds(pl.multiple_of((1 - core) * half, half), half)]
    out_ref[...] = (
        jnp.dot(own, w_own[...], preferred_element_type=jnp.float32)
        + jnp.dot(other, w_other[...], preferred_element_type=jnp.float32)
    ).astype(out_ref.dtype)


def attend(place, queries, kv_parts, w_own, w_other, dtype):
    tokens = queries.shape[0]
    width = w_own.shape[1]
    chip_width = 2 * w_own.shape[0]
    return pl.pallas_call(
        functools.partial(attend_kernel, scale=1.0 / HD**0.5),
        in_specs=[pl.BlockSpec(memory_space=pltpu.SMEM)]
        + [pl.BlockSpec(memory_space=pltpu.VMEM)] * 5
        + [pl.BlockSpec(memory_space=pl.ANY)] * 2,
        out_specs=pl.BlockSpec(memory_space=pltpu.VMEM),
        out_shape=jax.ShapeDtypeStruct((tokens, width), dtype),
        scratch_shapes=[
            pltpu.VMEM((4 * tokens, HD), jnp.bfloat16),
            pltpu.VMEM((4 * tokens, HD), jnp.bfloat16),
            pltpu.VMEM((tokens, chip_width), jnp.bfloat16),
            pltpu.VMEM(w_own.shape, jnp.bfloat16),
            pltpu.VMEM(w_other.shape, jnp.bfloat16),
            pltpu.SemaphoreType.DMA((2,)),
        ],
        compiler_params=pltpu.CompilerParams(vmem_limit_bytes=24 * 1024 * 1024),
        cost_estimate=pl.CostEstimate(
            flops=16 * tokens * tokens * chip_width + 2 * tokens * chip_width * width,
            bytes_accessed=4 * w_own.size + 4 * tokens * width,
            transcendentals=4 * tokens * tokens * chip_width // HD,
        ),
    )(place, queries, *kv_parts, w_own, w_other)


def norm_kernel(residual_ref, own_ref, other_ref, gain_ref, hidden_ref, normed_ref):
    hidden = (
        residual_ref[...].astype(jnp.float32) + own_ref[...] + other_ref[...].astype(jnp.float32)
    ).astype(jnp.bfloat16)
    hidden_ref[...] = hidden
    wide = hidden.astype(jnp.float32)
    normed_ref[...] = (
        wide
        * lax.rsqrt(jnp.mean(wide * wide, axis=1, keepdims=True) + 1e-06)
        * gain_ref[...].astype(jnp.float32)
    ).astype(jnp.bfloat16)


def add_and_norm(residual, own, other, gain):
    return pl.pallas_call(
        norm_kernel,
        in_specs=[pl.BlockSpec(memory_space=pltpu.VMEM)] * 4,
        out_specs=[pl.BlockSpec(memory_space=pltpu.VMEM)] * 2,
        out_shape=[jax.ShapeDtypeStruct(residual.shape, jnp.bfloat16)] * 2,
        compiler_params=pltpu.CompilerParams(vmem_limit_bytes=32 * 1024 * 1024),
    )(residual, own, other, gain)


def pass_kernel(*refs):
    del refs


def meet(*arrays):
    return pl.pallas_call(
        pass_kernel,
        in_specs=[pl.BlockSpec(memory_space=pl.ANY)] * len(arrays),
        out_specs=[pl.BlockSpec(memory_space=pl.ANY)] * len(arrays),
        out_shape=[jax.ShapeDtypeStruct(array.shape, array.dtype) for array in arrays],
        input_output_aliases={index: index for index in range(len(arrays))},
    )(*arrays)


def experts_kernel(gate_ref, *refs, cap, span):
    row_refs, refs = refs[:4], refs[4:]
    w_gate_ref, w_up_ref, w_down_ref, own_ref, across_ref, other_ref, packed, inner = refs
    tokens, width = row_refs[0].shape
    gates = gate_ref[...]
    named = gates > 0
    before = (
        lax.broadcasted_iota(jnp.int32, (tokens, tokens), 0)
        < lax.broadcasted_iota(jnp.int32, (tokens, tokens), 1)
    ).astype(jnp.bfloat16)
    rank = jnp.dot(named.astype(jnp.bfloat16), before, preferred_element_type=jnp.float32)
    slot = jnp.where(named, rank.astype(jnp.int32), -1)
    slots = lax.broadcasted_iota(jnp.int32, (cap, tokens), 0)
    picks, places, weights = [], [], []
    for block in range(4):
        chosen = slots == slot[block : block + 1, :]
        pick = jnp.where(chosen, 1.0, 0.0)
        picks.append(pick.astype(jnp.bfloat16))
        places.append(jnp.transpose(pick).astype(jnp.bfloat16))
        weights.append(
            jnp.sum(jnp.where(chosen, gates[block : block + 1, :], 0.0), axis=1, keepdims=True)
        )

    for block in range(4):
        packed[block * cap : (block + 1) * cap, :] = jnp.dot(
            picks[block], row_refs[block][...], preferred_element_type=jnp.float32
        ).astype(jnp.bfloat16)

    @pl.loop(0, inner.shape[1] // span)
    def _(index):
        columns = pl.ds(pl.multiple_of(index * span, span), span)
        gate_proj = jnp.dot(packed[...], w_gate_ref[:, columns], preferred_element_type=jnp.float32)
        up_proj = jnp.dot(packed[...], w_up_ref[:, columns], preferred_element_type=jnp.float32)
        inner[:, columns] = (gate_proj / (1.0 + jnp.exp(-gate_proj)) * up_proj).astype(jnp.bfloat16)

    @pl.loop(0, width // span)
    def _(index):
        columns = pl.ds(pl.multiple_of(index * span, span), span)
        result = jnp.dot(inner[...], w_down_ref[:, columns], preferred_element_type=jnp.float32)
        targets = (
            own_ref.at[:, columns],
            other_ref.at[0:tokens, columns],
            across_ref.at[:, columns],
            other_ref.at[tokens : 2 * tokens, columns],
        )
        for block in range(4):
            part = (result[block * cap : (block + 1) * cap] * weights[block]).astype(jnp.bfloat16)
            targets[block][...] = jnp.dot(
                places[block], part, preferred_element_type=jnp.float32
            ).astype(jnp.bfloat16)


def experts_on_rows(gates, row_blocks, w_gate, w_up, w_down, cap):
    tokens, width = row_blocks[0].shape
    hidden_units = w_gate.shape[1]
    return pl.pallas_call(
        functools.partial(experts_kernel, cap=cap, span=256),
        in_specs=[pl.BlockSpec(memory_space=pltpu.VMEM)] * 8,
        out_specs=[pl.BlockSpec(memory_space=pltpu.VMEM)] * 3,
        out_shape=[
            jax.ShapeDtypeStruct((tokens, width), jnp.bfloat16),
            jax.ShapeDtypeStruct((tokens, width), jnp.bfloat16),
            jax.ShapeDtypeStruct((2 * tokens, width), jnp.bfloat16),
        ],
        scratch_shapes=[
            pltpu.VMEM((4 * cap, width), jnp.bfloat16),
            pltpu.VMEM((4 * cap, hidden_units), jnp.bfloat16),
        ],
        compiler_params=pltpu.CompilerParams(vmem_limit_bytes=28 * 1024 * 1024),
        cost_estimate=pl.CostEstimate(
            flops=24 * cap * width * hidden_units,
            bytes_accessed=16 * tokens * width + 6 * width * hidden_units,
            transcendentals=4 * cap * hidden_units,
        ),
    )(gates, *row_blocks, w_gate, w_up, w_down)


def gathered_plan(
    query_rows,
    key_rows,
    value_rows,
    residual_in,
    out_proj,
    norm_gain,
    expert_ids,
    gate_weights,
    expert_gate,
    expert_up,
    expert_down,
    cap,
):
    n_seq = lax.axis_size("seq")
    n_sub = lax.axis_size("sub")
    experts = n_seq * n_sub
    place = lax.axis_index("seq")
    core = place % 2
    chip = place // 2
    twin = [(index, index ^ 1) for index in range(n_seq)]
    across = [(index, (index + 2) % n_seq) for index in range(n_seq)]
    diagonal = [(index, (index ^ 1) ^ 2) for index in range(n_seq)]
    order = [0] + list(range(1, n_sub, 2)) + list(reversed(range(2, n_sub, 2)))

    def ring(steps):
        return [(order[at], order[(at + steps) % n_sub]) for at in range(n_sub)]

    queries = query_rows[0]
    chip_width = queries.shape[1] // 2

    def kv_of(head):
        start = head * HD
        return jnp.concatenate(
            [
                lax.dynamic_slice_in_dim(key_rows[0], start, HD, 1),
                lax.dynamic_slice_in_dim(value_rows[0], start, HD, 1),
            ],
            axis=1,
        )

    kv_here = kv_of(chip)
    kv_away = kv_of(1 - chip)
    outgoing = jnp.concatenate(
        [lax.dynamic_slice_in_dim(queries, (1 - chip) * chip_width, chip_width, 1), kv_away], axis=1
    )
    incoming = lax.ppermute(outgoing, "seq", across)
    kv_twin = lax.ppermute(kv_here, "seq", twin)
    kv_diagonal = lax.ppermute(kv_away, "seq", diagonal)
    w_other = lax.ppermute(out_proj, "seq", twin)

    table = jnp.sum(
        jnp.where(
            expert_ids[0][None] == jnp.arange(experts, dtype=jnp.int32)[:, None, None],
            gate_weights[0].astype(jnp.float32)[None],
            0.0,
        ),
        axis=2,
    ).astype(jnp.bfloat16)
    incoming, table_twin, table_across, table_diagonal = meet(
        incoming,
        lax.ppermute(table, "seq", twin),
        lax.ppermute(table, "seq", across),
        lax.ppermute(table, "seq", diagonal),
    )
    quad = jnp.stack([table, table_twin, table_across, table_diagonal])
    quads = [lax.ppermute(quad, "sub", ring(steps)) for steps in range(1, n_sub)]

    kv_parts = (kv_here, kv_twin, incoming, kv_diagonal)
    columns = [place, place ^ 1, place ^ 2, place ^ 3]

    def place_of(query_start, row_block):
        return jnp.stack([core, query_start, row_block] + columns).astype(jnp.int32)

    sent = attend(place_of(0 * place, place ^ 2), incoming, kv_parts, out_proj, w_other, jnp.bfloat16)
    projected_across = lax.ppermute(sent, "seq", across)
    projected = attend(
        place_of(chip * chip_width, place), queries, kv_parts, out_proj, w_other, jnp.float32
    )
    projected_across, *quads = meet(projected_across, *quads)
    mine = place * n_sub + lax.axis_index("sub")
    gates = lax.dynamic_index_in_dim(
        jnp.stack([quad] + quads), mine, 2, keepdims=False
    ).astype(jnp.float32)
    hidden, normed = add_and_norm(residual_in[0], projected, projected_across, norm_gain[None])

    tokens = queries.shape[0]
    last = n_sub - 1
    lag = max(n_sub, 4)
    held = {("row", 0): normed}
    halves = {}

    def move_twin(array):
        return lax.ppermute(array, "seq", twin)

    def move_across(array):
        return lax.ppermute(array, "seq", across)

    def move_on(array):
        return lax.ppermute(array, "sub", ring(1))

    for turn in range(1, lag + n_sub + 1):
        now = {}
        if turn <= n_sub:
            step = turn - 1
            now["across", step] = move_across(held["row", step])
            if step < last:
                now["row", step + 1] = move_on(held["row", step])
            held["twin", step] = move_twin(held["row", step])
        if 2 <= turn <= n_sub + 1:
            step = turn - 2
            held["diagonal", step] = move_twin(held["across", step])
        back = turn - lag
        if 1 <= back <= n_sub:
            step = back % n_sub
            now["back", step] = move_across(held["away", step])
        if 2 <= back:
            step = back - 1
            part = halves[step] + held["back", step].astype(jnp.float32)
            if step > 1:
                part = part + held["sum", step - 1].astype(jnp.float32)
            now["sum", step] = move_on(part.astype(jnp.bfloat16))
        step = turn - 2 if turn < lag + n_sub - 2 else 0
        if turn == lag + n_sub - 2 or 1 <= step <= last:
            own, away, other = experts_on_rows(
                gates[step],
                [held[name, step] for name in ("row", "twin", "across", "diagonal")],
                expert_gate[0],
                expert_up[0],
                expert_down[0],
                cap,
            )
            now["other", step] = other
            held["own", step] = own
            held["part", step] = away
        step = turn - 3 if turn < lag + n_sub - 1 else 0
        if turn == lag + n_sub - 1 or 1 <= step <= last:
            met = move_twin(held["other", step]).astype(jnp.float32)
            halves[step] = held["own", step].astype(jnp.float32) + met[:tokens]
            now["away", step] = (held["part", step].astype(jnp.float32) + met[tokens:]).astype(
                jnp.bfloat16
            )
        if turn < lag + n_sub:
            met = meet(*now.values())
            now = dict(zip(now.keys(), met))
        held.update(now)
    total = hidden.astype(jnp.float32) + halves[0] + held["back", 0].astype(jnp.float32)
    if last:
        total = total + held["sum", last].astype(jnp.float32)
    return total.astype(jnp.bfloat16)[None]


def per_device(
    query_rows,
    key_rows,
    value_rows,
    residual_in,
    out_proj,
    norm_gain,
    expert_ids,
    gate_weights,
    expert_gate,
    expert_up,
    expert_down,
):
    tokens = query_rows.shape[1]
    n_seq = lax.axis_size("seq")
    n_sub = lax.axis_size("sub")
    experts = n_seq * n_sub
    topk = expert_ids.shape[2]
    cap = max(2, (5 * tokens * topk + 4 * experts - 1) // (4 * experts))
    if n_seq == 2 * KVH and KVH == 2 and experts <= 2 * topk and cap % 16 == 0:
        return gathered_plan(
            query_rows,
            key_rows,
            value_rows,
            residual_in,
            out_proj,
            norm_gain,
            expert_ids,
            gate_weights,
            expert_gate,
            expert_up,
            expert_down,
            cap,
        )
    heads_here = QH // n_seq
    group = QH // KVH
    query_local = lax.all_to_all(query_rows, "seq", split_axis=2, concat_axis=1, tiled=True)
    key_full, value_full = (
        lax.all_gather(key_rows, "seq", axis=1, tiled=True),
        lax.all_gather(value_rows, "seq", axis=1, tiled=True),
    )
    first_head = lax.axis_index("seq") * heads_here
    key_list = []
    value_list = []
    for head in range(heads_here):
        kv_start = (first_head + head) // group * HD
        key_list.append(lax.dynamic_slice_in_dim(key_full[0], kv_start, HD, 1))
        value_list.append(lax.dynamic_slice_in_dim(value_full[0], kv_start, HD, 1))
    length = query_local.shape[1]
    block = min(length, max(512, length // 8))
    outputs = [
        attend_head(
            query_local[0, :, head * HD : (head + 1) * HD], key_list[head], value_list[head], block
        )
        for head in range(heads_here)
    ]
    head_block = jnp.concatenate(outputs, axis=1)[None]
    attended = lax.all_to_all(head_block, "seq", split_axis=1, concat_axis=2, tiled=True)[0]
    projected = jnp.dot(
        attended,
        lax.all_gather(out_proj, "seq", axis=0, tiled=True),
        preferred_element_type=jnp.float32,
    )
    hidden = (residual_in[0].astype(jnp.float32) + projected).astype(jnp.bfloat16)
    wide = hidden.astype(jnp.float32)
    normed = (
        wide
        * lax.rsqrt(jnp.mean(wide * wide, axis=1, keepdims=True) + 1e-06)
        * norm_gain.astype(jnp.float32)
    ).astype(jnp.bfloat16)
    flat_ids = expert_ids[0].reshape(-1)
    items = flat_ids.shape[0]
    ranks = rank_in_expert(flat_ids, experts)
    slot_of = flat_ids * cap + ranks
    slots_out = experts * cap
    item_of_slot = (
        jnp.full((slots_out,), items, jnp.int32).at[slot_of].set(jnp.arange(items, dtype=jnp.int32))
    )
    padded_rows = jnp.concatenate([normed, jnp.zeros((1, D), jnp.bfloat16)], axis=0)
    padded_gates = jnp.concatenate(
        [gate_weights[0].reshape(-1), jnp.zeros((1,), jnp.bfloat16)], axis=0
    )
    token_of_slot = jnp.where(item_of_slot < items, item_of_slot // topk, tokens)
    send_rows = padded_rows[token_of_slot].reshape(experts, cap, D)
    send_gates = padded_gates[item_of_slot].reshape(experts, cap)
    recv_rows, recv_gates = (
        lax.all_to_all(send_rows, ("seq", "sub"), split_axis=0, concat_axis=0, tiled=True),
        lax.all_to_all(send_gates, ("seq", "sub"), split_axis=0, concat_axis=0, tiled=True),
    )
    slots_in = experts * cap
    valid = recv_gates > 0
    counts = jnp.sum(valid.astype(jnp.int32), axis=1)
    offsets = jnp.cumsum(counts) - counts
    dest = jnp.where(
        valid, offsets[:, None] + jnp.arange(cap, dtype=jnp.int32)[None, :], slots_in
    ).reshape(-1)
    source_of = (
        jnp.full((slots_in + 1,), slots_in, jnp.int32)
        .at[dest]
        .set(jnp.arange(slots_in, dtype=jnp.int32))[:slots_in]
    )
    compact_rows = jnp.concatenate(
        [recv_rows.reshape(slots_in, D), jnp.zeros((1, D), jnp.bfloat16)], axis=0
    )[source_of]
    compact_gates = jnp.concatenate(
        [recv_gates.reshape(-1), jnp.zeros((1,), jnp.bfloat16)], axis=0
    )[source_of].astype(jnp.float32)
    filled = jnp.sum(counts)
    n_blocks = (filled + slots_in - 1) // slots_in
    w_gate = expert_gate[0]
    w_up = expert_up[0]
    w_down = expert_down[0]

    def expert_block(index, results):
        gate_proj = jnp.dot(compact_rows, w_gate, preferred_element_type=jnp.float32)
        up_proj = jnp.dot(compact_rows, w_up, preferred_element_type=jnp.float32)
        inner = (jax.nn.silu(gate_proj) * up_proj).astype(jnp.bfloat16)
        weighted = (
            jnp.dot(inner, w_down, preferred_element_type=jnp.float32) * compact_gates[:, None]
        )
        return weighted.astype(jnp.bfloat16)

    results = lax.fori_loop(0, n_blocks, expert_block, jnp.zeros((slots_in, D), jnp.bfloat16))
    returned = jnp.concatenate([results, jnp.zeros((1, D), jnp.bfloat16)], axis=0)[dest].reshape(
        experts, cap, D
    )
    back = lax.all_to_all(
        returned, ("seq", "sub"), split_axis=0, concat_axis=0, tiled=True
    ).reshape(slots_out, D)
    gathered = back[slot_of].reshape(tokens, topk, D).astype(jnp.float32)
    mixture = jnp.sum(gathered, axis=1)
    return (wide + mixture).astype(jnp.bfloat16)[None]


def solution(mesh):
    placed = (
        P(("grp", "sub"), "seq", None),
        P(("grp", "sub"), "seq", None),
        P(("grp", "sub"), "seq", None),
        P(("grp", "sub"), "seq", None),
        P("seq", None),
        P(),
        P(("grp", "sub"), "seq", None),
        P(("grp", "sub"), "seq", None),
        P(("seq", "sub"), None, None),
        P(("seq", "sub"), None, None),
        P(("seq", "sub"), None, None),
    )
    return jax.shard_map(
        per_device,
        mesh=mesh,
        in_specs=placed,
        out_specs=P(("grp", "sub"), "seq", None),
        check_vma=False,
    )
```

```python
import functools

import jax
import jax.numpy as jnp
from jax import lax
from jax.experimental import pallas as pl
from jax.experimental.pallas import tpu as pltpu
from jax.sharding import PartitionSpec as P

D = 2048
HD = 128
QH = 16
KVH = 2
VMEM_GRANT = 60 * 1024 * 1024


def attend_head(queries, keys_one, values_one, block):
    length = queries.shape[0]
    scale = 1.0 / queries.shape[1] ** 0.5
    pieces = []
    for part_index in range(length // block):
        stop = (part_index + 1) * block
        rows_here = queries[part_index * block : stop]
        scores = (
            jnp.einsum("qd,kd->qk", rows_here, keys_one[:stop], preferred_element_type=jnp.float32)
            * scale
        )
        row_pos = part_index * block + jnp.arange(block, dtype=jnp.int32)
        col_pos = jnp.arange(stop, dtype=jnp.int32)
        scores = jnp.where(row_pos[:, None] >= col_pos[None, :], scores, -1e30)
        peak = jnp.max(scores, axis=1, keepdims=True)
        weights = jnp.exp(scores - peak)
        probs = (weights / jnp.sum(weights, axis=1, keepdims=True)).astype(jnp.bfloat16)
        pieces.append(
            jnp.dot(probs, values_one[:stop], preferred_element_type=jnp.float32).astype(
                jnp.bfloat16
            )
        )
    return jnp.concatenate(pieces, axis=0)


def rank_in_expert(flat_ids, experts):
    items = flat_ids.shape[0]
    width = 128
    n_parts = items // width
    onehot = (
        (flat_ids[:, None] == jnp.arange(experts, dtype=jnp.int32)[None, :])
        .astype(jnp.bfloat16)
        .reshape(n_parts, width, experts)
    )
    lower = (
        jnp.arange(width, dtype=jnp.int32)[:, None] > jnp.arange(width, dtype=jnp.int32)[None, :]
    ).astype(jnp.bfloat16)
    within = jnp.einsum("ij,bje->bie", lower, onehot, preferred_element_type=jnp.float32)
    part_counts = jnp.sum(onehot.astype(jnp.float32), axis=1)
    earlier = jnp.cumsum(part_counts, axis=0) - part_counts
    ranks = jnp.sum((within + earlier[:, None, :]) * onehot.astype(jnp.float32), axis=2)
    return ranks.reshape(items).astype(jnp.int32)


def pack_kernel(chip_ref, query_ref, key_ref, value_ref, id_ref, gate_ref, away_ref, here_kv_ref, away_kv_ref):
    tokens = query_ref.shape[0]
    head_size = key_ref.shape[1] // 2
    chip_width = away_ref.shape[1]
    chip = chip_ref[0]
    experts = here_kv_ref.shape[0] - tokens
    away_ref[...] = query_ref[:, pl.ds(pl.multiple_of((1 - chip) * chip_width, chip_width), chip_width)]
    number = lax.broadcasted_iota(jnp.int32, (experts, tokens), 0)
    table = jnp.zeros((experts, tokens), jnp.float32)
    for choice in range(id_ref.shape[0]):
        table += jnp.where(
            number == id_ref[choice : choice + 1, :],
            gate_ref[choice : choice + 1, :].astype(jnp.float32),
            0.0,
        )
    for out_ref, head in ((here_kv_ref, chip), (away_kv_ref, 1 - chip)):
        columns = pl.ds(pl.multiple_of(head * head_size, head_size), head_size)
        out_ref[0:tokens, 0:head_size] = key_ref[:, columns]
        out_ref[0:tokens, head_size:] = value_ref[:, columns]
        out_ref[tokens:, 0:head_size] = table.astype(jnp.bfloat16)
        out_ref[tokens:, head_size:] = jnp.zeros((experts, head_size), jnp.bfloat16)


def pack(chip, queries, keys, values, ids, gates, experts):
    tokens, width = queries.shape
    kv = jax.ShapeDtypeStruct((tokens + experts, keys.shape[1]), jnp.bfloat16)
    return pl.pallas_call(
        pack_kernel,
        in_specs=[pl.BlockSpec(memory_space=pltpu.SMEM)]
        + [pl.BlockSpec(memory_space=pltpu.VMEM)] * 5,
        out_specs=[pl.BlockSpec(memory_space=pltpu.VMEM)] * 3,
        out_shape=[jax.ShapeDtypeStruct((tokens, width // 2), jnp.bfloat16), kv, kv],
        compiler_params=pltpu.CompilerParams(vmem_limit_bytes=VMEM_GRANT),
    )(chip.reshape(1), queries, keys, values, ids, gates)


def attend_kernel(place_ref, query_ref, *refs, scale):
    kv_refs, (w_own_ref, w_other_ref, out_ref, keys, values, heads, w_own, w_other, done) = (
        refs[:4],
        refs[4:],
    )
    fetches = [
        pltpu.make_async_copy(w_own_ref, w_own, done.at[0]),
        pltpu.make_async_copy(w_other_ref, w_other, done.at[1]),
    ]
    for fetch in fetches:
        fetch.start()
    rows = keys.shape[0] // 4
    head_size = keys.shape[1]
    core = place_ref[0]
    query_start = pl.multiple_of(place_ref[1], head_size)
    row_pos = place_ref[2] * rows + lax.broadcasted_iota(jnp.int32, (rows, 1), 0)
    lane = lax.broadcasted_iota(jnp.int32, (1, rows), 1)
    col_pos = jnp.concatenate([place_ref[3 + part] * rows + lane for part in range(4)], axis=1)
    allowed = row_pos >= col_pos
    for part, kv_ref in enumerate(kv_refs):
        keys[part * rows : (part + 1) * rows, :] = kv_ref[0:rows, 0:head_size]
        values[part * rows : (part + 1) * rows, :] = kv_ref[0:rows, head_size:]
    key_block = keys[...]
    value_block = values[...]
    for head in range(heads.shape[1] // head_size):
        query = query_ref[:, pl.ds(query_start + head * head_size, head_size)]
        scores = (
            lax.dot_general(
                query, key_block, (((1,), (1,)), ((), ())), preferred_element_type=jnp.float32
            )
            * scale
        )
        scores = jnp.where(allowed, scores, -1e30)
        weights = jnp.exp(scores - jnp.max(scores, axis=1, keepdims=True))
        probs = (weights / jnp.sum(weights, axis=1, keepdims=True)).astype(jnp.bfloat16)
        heads[:, head * head_size : (head + 1) * head_size] = jnp.dot(
            probs, value_block, preferred_element_type=jnp.float32
        ).astype(jnp.bfloat16)
    for fetch in fetches:
        fetch.wait()
    half = heads.shape[1] // 2
    own = heads[:, pl.ds(pl.multiple_of(core * half, half), half)]
    other = heads[:, pl.ds(pl.multiple_of((1 - core) * half, half), half)]
    out_ref[...] = (
        jnp.dot(own, w_own[...], preferred_element_type=jnp.float32)
        + jnp.dot(other, w_other[...], preferred_element_type=jnp.float32)
    ).astype(out_ref.dtype)


def attend(place, queries, kv_parts, w_own, w_other, dtype):
    tokens = queries.shape[0]
    width = w_own.shape[1]
    chip_width = 2 * w_own.shape[0]
    return pl.pallas_call(
        functools.partial(attend_kernel, scale=1.0 / HD**0.5),
        in_specs=[pl.BlockSpec(memory_space=pltpu.SMEM)]
        + [pl.BlockSpec(memory_space=pltpu.VMEM)] * 5
        + [pl.BlockSpec(memory_space=pl.ANY)] * 2,
        out_specs=pl.BlockSpec(memory_space=pltpu.VMEM),
        out_shape=jax.ShapeDtypeStruct((tokens, width), dtype),
        scratch_shapes=[
            pltpu.VMEM((4 * tokens, HD), jnp.bfloat16),
            pltpu.VMEM((4 * tokens, HD), jnp.bfloat16),
            pltpu.VMEM((tokens, chip_width), jnp.bfloat16),
            pltpu.VMEM(w_own.shape, jnp.bfloat16),
            pltpu.VMEM(w_other.shape, jnp.bfloat16),
            pltpu.SemaphoreType.DMA((2,)),
        ],
        compiler_params=pltpu.CompilerParams(vmem_limit_bytes=VMEM_GRANT),
        cost_estimate=pl.CostEstimate(
            flops=16 * tokens * tokens * chip_width + 2 * tokens * chip_width * width,
            bytes_accessed=4 * w_own.size + 4 * tokens * width,
            transcendentals=4 * tokens * tokens * chip_width // HD,
        ),
    )(place, queries, *kv_parts, w_own, w_other)


def norm_kernel(residual_ref, own_ref, other_ref, gain_ref, hidden_ref, normed_ref):
    hidden = (
        residual_ref[...].astype(jnp.float32) + own_ref[...] + other_ref[...].astype(jnp.float32)
    ).astype(jnp.bfloat16)
    hidden_ref[...] = hidden
    wide = hidden.astype(jnp.float32)
    normed_ref[...] = (
        wide
        * lax.rsqrt(jnp.mean(wide * wide, axis=1, keepdims=True) + 1e-06)
        * gain_ref[...].astype(jnp.float32)
    ).astype(jnp.bfloat16)


def add_and_norm(residual, own, other, gain):
    return pl.pallas_call(
        norm_kernel,
        in_specs=[pl.BlockSpec(memory_space=pltpu.VMEM)] * 4,
        out_specs=[pl.BlockSpec(memory_space=pltpu.VMEM)] * 2,
        out_shape=[jax.ShapeDtypeStruct(residual.shape, jnp.bfloat16)] * 2,
        compiler_params=pltpu.CompilerParams(vmem_limit_bytes=VMEM_GRANT),
    )(residual, own, other, gain)


def pass_kernel(*refs):
    del refs


def meet(*arrays):
    return pl.pallas_call(
        pass_kernel,
        in_specs=[pl.BlockSpec(memory_space=pl.ANY)] * len(arrays),
        out_specs=[pl.BlockSpec(memory_space=pl.ANY)] * len(arrays),
        out_shape=[jax.ShapeDtypeStruct(array.shape, array.dtype) for array in arrays],
        input_output_aliases={index: index for index in range(len(arrays))},
    )(*arrays)


def experts_kernel(gate_ref, *refs, cap):
    row_refs, refs = refs[:4], refs[4:]
    w_gate_ref, w_up_ref, w_down_ref, own_ref, across_ref, other_ref, packed, total = refs
    tokens = row_refs[0].shape[0]
    step = pl.program_id(0)
    gates = gate_ref[...]
    named = gates > 0
    before = (
        lax.broadcasted_iota(jnp.int32, (tokens, tokens), 0)
        < lax.broadcasted_iota(jnp.int32, (tokens, tokens), 1)
    ).astype(jnp.bfloat16)
    rank = jnp.dot(named.astype(jnp.bfloat16), before, preferred_element_type=jnp.float32)
    slot = jnp.where(named, rank.astype(jnp.int32), -1)
    slots = lax.broadcasted_iota(jnp.int32, (cap, tokens), 0)

    def chosen_of(block):
        return slots == slot[block : block + 1, :]

    @pl.when(step == 0)
    def _():
        for block in range(4):
            packed[block * cap : (block + 1) * cap, :] = jnp.dot(
                chosen_of(block).astype(jnp.bfloat16),
                row_refs[block][...],
                preferred_element_type=jnp.float32,
            ).astype(jnp.bfloat16)

    rows = packed[...]
    gate_proj = jnp.dot(rows, w_gate_ref[...], preferred_element_type=jnp.float32)
    up_proj = jnp.dot(rows, w_up_ref[...], preferred_element_type=jnp.float32)
    inner = (gate_proj / (1.0 + jnp.exp(-gate_proj)) * up_proj).astype(jnp.bfloat16)
    result = jnp.dot(inner, w_down_ref[...], preferred_element_type=jnp.float32)

    @pl.when(step == 0)
    def _():
        total[...] = result

    @pl.when(step > 0)
    def _():
        total[...] += result

    @pl.when(step == pl.num_programs(0) - 1)
    def _():
        targets = (
            own_ref.at[...],
            other_ref.at[0:tokens],
            across_ref.at[...],
            other_ref.at[tokens : 2 * tokens],
        )
        for block in range(4):
            chosen = chosen_of(block)
            weights = jnp.sum(
                jnp.where(chosen, gates[block : block + 1, :], 0.0), axis=1, keepdims=True
            )
            part = (total[block * cap : (block + 1) * cap, :] * weights).astype(jnp.bfloat16)
            targets[block][...] = lax.dot_general(
                chosen.astype(jnp.bfloat16),
                part,
                (((0,), (0,)), ((), ())),
                preferred_element_type=jnp.float32,
            ).astype(jnp.bfloat16)


def experts_on_rows(gates, row_blocks, w_gate, w_up, w_down, cap):
    tokens, width = row_blocks[0].shape
    hidden_units = w_gate.shape[1]
    chunk = hidden_units // 3 if hidden_units % 384 == 0 else hidden_units
    whole = pl.BlockSpec((tokens, width), lambda step: (0, 0))
    return pl.pallas_call(
        functools.partial(experts_kernel, cap=cap),
        grid=(hidden_units // chunk,),
        in_specs=[
            pl.BlockSpec((4, tokens), lambda step: (0, 0)),
            whole,
            whole,
            whole,
            whole,
            pl.BlockSpec((width, chunk), lambda step: (0, step)),
            pl.BlockSpec((width, chunk), lambda step: (0, step)),
            pl.BlockSpec((chunk, width), lambda step: (step, 0)),
        ],
        out_specs=[whole, whole, pl.BlockSpec((2 * tokens, width), lambda step: (0, 0))],
        out_shape=[
            jax.ShapeDtypeStruct((tokens, width), jnp.bfloat16),
            jax.ShapeDtypeStruct((tokens, width), jnp.bfloat16),
            jax.ShapeDtypeStruct((2 * tokens, width), jnp.bfloat16),
        ],
        scratch_shapes=[
            pltpu.VMEM((4 * cap, width), jnp.bfloat16),
            pltpu.VMEM((4 * cap, width), jnp.float32),
        ],
        compiler_params=pltpu.CompilerParams(vmem_limit_bytes=VMEM_GRANT),
        cost_estimate=pl.CostEstimate(
            flops=24 * cap * width * hidden_units,
            bytes_accessed=16 * tokens * width + 6 * width * hidden_units,
            transcendentals=4 * cap * hidden_units,
        ),
    )(gates, *row_blocks, w_gate, w_up, w_down)


def gathered_plan(
    query_rows,
    key_rows,
    value_rows,
    residual_in,
    out_proj,
    norm_gain,
    expert_ids,
    gate_weights,
    expert_gate,
    expert_up,
    expert_down,
    cap,
):
    n_seq = lax.axis_size("seq")
    n_sub = lax.axis_size("sub")
    experts = n_seq * n_sub
    place = lax.axis_index("seq")
    core = place % 2
    chip = place // 2
    twin = [(index, index ^ 1) for index in range(n_seq)]
    across = [(index, (index + 2) % n_seq) for index in range(n_seq)]
    diagonal = [(index, (index ^ 1) ^ 2) for index in range(n_seq)]
    order = [0] + list(range(1, n_sub, 2)) + list(reversed(range(2, n_sub, 2)))

    def ring(steps):
        return [(order[at], order[(at + steps) % n_sub]) for at in range(n_sub)]

    queries = query_rows[0]
    chip_width = queries.shape[1] // 2

    tokens = queries.shape[0]
    queries_away, kv_here, kv_away = pack(
        chip,
        queries,
        key_rows[0],
        value_rows[0],
        expert_ids[0].T,
        gate_weights[0].T,
        experts,
    )
    incoming = lax.ppermute(queries_away, "seq", across)
    kv_parts = [
        kv_here,
        lax.ppermute(kv_here, "seq", twin),
        lax.ppermute(kv_away, "seq", across),
        lax.ppermute(kv_away, "seq", diagonal),
    ]
    w_other = lax.ppermute(out_proj, "seq", twin)
    quad = jnp.concatenate([part[tokens:, :tokens] for part in kv_parts], axis=1)
    columns = [place, place ^ 1, place ^ 2, place ^ 3]

    def place_of(query_start, row_block):
        return jnp.stack([core, query_start, row_block] + columns).astype(jnp.int32)

    sent = attend(place_of(0 * place, place ^ 2), incoming, kv_parts, out_proj, w_other, jnp.bfloat16)
    projected_across = lax.ppermute(sent, "seq", across)
    projected = attend(
        place_of(chip * chip_width, place), queries, kv_parts, out_proj, w_other, jnp.float32
    )
    hidden, normed = add_and_norm(residual_in[0], projected, projected_across, norm_gain[None])

    last = n_sub - 1
    mine = place * n_sub + lax.axis_index("sub")

    def gates_of(quad):
        row = lax.dynamic_slice_in_dim(quad, mine, 1, 0)
        return row.reshape(4, tokens).astype(jnp.float32)

    lag = max(n_sub, 4)
    held = {("row", 0): normed, ("quad", 0): quad}

    def move_twin(array):
        return lax.ppermute(array, "seq", twin)

    def move_across(array):
        return lax.ppermute(array, "seq", across)

    def move_on(array):
        return lax.ppermute(array, "sub", ring(1))

    def sum_here(step):
        return (
            held["own", step].astype(jnp.float32)
            + held["met", step][:tokens].astype(jnp.float32)
            + held["back", step].astype(jnp.float32)
        )

    for turn in range(1, lag + n_sub + 1):
        now = {}
        if turn <= n_sub:
            step = turn - 1
            now["across", step] = move_across(held["row", step])
            if step < last:
                now["row", step + 1] = move_on(held["row", step])
            held["twin", step] = move_twin(held["row", step])
        if turn == 1:
            for steps in range(1, n_sub):
                now["quad", steps] = lax.ppermute(quad, "sub", ring(steps))
        if 2 <= turn <= n_sub + 1:
            step = turn - 2
            held["diagonal", step] = move_twin(held["across", step])
        back = turn - lag
        if 1 <= back <= n_sub:
            step = back % n_sub
            now["back", step] = move_across(held["away", step])
        if 2 <= back:
            step = back - 1
            part = sum_here(step)
            if step > 1:
                part = part + held["sum", step - 1].astype(jnp.float32)
            now["sum", step] = move_on(part.astype(jnp.bfloat16))
        step = turn - 2 if turn < lag + n_sub - 2 else 0
        if turn == lag + n_sub - 2 or 1 <= step <= last:
            own, away, other = experts_on_rows(
                gates_of(held["quad", step]),
                [held[name, step] for name in ("row", "twin", "across", "diagonal")],
                expert_gate[0],
                expert_up[0],
                expert_down[0],
                cap,
            )
            now["other", step] = other
            held["own", step] = own
            held["part", step] = away
        step = turn - 3 if turn < lag + n_sub - 1 else 0
        if turn == lag + n_sub - 1 or 1 <= step <= last:
            held["met", step] = move_twin(held["other", step])
            now["away", step] = (
                held["part", step].astype(jnp.float32)
                + held["met", step][tokens:].astype(jnp.float32)
            ).astype(jnp.bfloat16)
        if turn < lag + n_sub:
            now = dict(zip(now.keys(), meet(*now.values())))
        held.update(now)
    total = hidden.astype(jnp.float32) + sum_here(0)
    if last:
        total = total + held["sum", last].astype(jnp.float32)
    return total.astype(jnp.bfloat16)[None]


def per_device(
    query_rows,
    key_rows,
    value_rows,
    residual_in,
    out_proj,
    norm_gain,
    expert_ids,
    gate_weights,
    expert_gate,
    expert_up,
    expert_down,
):
    tokens = query_rows.shape[1]
    n_seq = lax.axis_size("seq")
    n_sub = lax.axis_size("sub")
    experts = n_seq * n_sub
    topk = expert_ids.shape[2]
    cap = max(2, (5 * tokens * topk + 4 * experts - 1) // (4 * experts))
    if n_seq == 2 * KVH and KVH == 2 and tokens == HD and experts <= 2 * topk and cap % 16 == 0:
        return gathered_plan(
            query_rows,
            key_rows,
            value_rows,
            residual_in,
            out_proj,
            norm_gain,
            expert_ids,
            gate_weights,
            expert_gate,
            expert_up,
            expert_down,
            cap,
        )
    heads_here = QH // n_seq
    group = QH // KVH
    query_local = lax.all_to_all(query_rows, "seq", split_axis=2, concat_axis=1, tiled=True)
    key_full, value_full = (
        lax.all_gather(key_rows, "seq", axis=1, tiled=True),
        lax.all_gather(value_rows, "seq", axis=1, tiled=True),
    )
    first_head = lax.axis_index("seq") * heads_here
    key_list = []
    value_list = []
    for head in range(heads_here):
        kv_start = (first_head + head) // group * HD
        key_list.append(lax.dynamic_slice_in_dim(key_full[0], kv_start, HD, 1))
        value_list.append(lax.dynamic_slice_in_dim(value_full[0], kv_start, HD, 1))
    length = query_local.shape[1]
    block = min(length, max(512, length // 8))
    outputs = [
        attend_head(
            query_local[0, :, head * HD : (head + 1) * HD], key_list[head], value_list[head], block
        )
        for head in range(heads_here)
    ]
    head_block = jnp.concatenate(outputs, axis=1)[None]
    attended = lax.all_to_all(head_block, "seq", split_axis=1, concat_axis=2, tiled=True)[0]
    projected = jnp.dot(
        attended,
        lax.all_gather(out_proj, "seq", axis=0, tiled=True),
        preferred_element_type=jnp.float32,
    )
    hidden = (residual_in[0].astype(jnp.float32) + projected).astype(jnp.bfloat16)
    wide = hidden.astype(jnp.float32)
    normed = (
        wide
        * lax.rsqrt(jnp.mean(wide * wide, axis=1, keepdims=True) + 1e-06)
        * norm_gain.astype(jnp.float32)
    ).astype(jnp.bfloat16)
    flat_ids = expert_ids[0].reshape(-1)
    items = flat_ids.shape[0]
    ranks = rank_in_expert(flat_ids, experts)
    slot_of = flat_ids * cap + ranks
    slots_out = experts * cap
    item_of_slot = (
        jnp.full((slots_out,), items, jnp.int32).at[slot_of].set(jnp.arange(items, dtype=jnp.int32))
    )
    padded_rows = jnp.concatenate([normed, jnp.zeros((1, D), jnp.bfloat16)], axis=0)
    padded_gates = jnp.concatenate(
        [gate_weights[0].reshape(-1), jnp.zeros((1,), jnp.bfloat16)], axis=0
    )
    token_of_slot = jnp.where(item_of_slot < items, item_of_slot // topk, tokens)
    send_rows = padded_rows[token_of_slot].reshape(experts, cap, D)
    send_gates = padded_gates[item_of_slot].reshape(experts, cap)
    recv_rows, recv_gates = (
        lax.all_to_all(send_rows, ("seq", "sub"), split_axis=0, concat_axis=0, tiled=True),
        lax.all_to_all(send_gates, ("seq", "sub"), split_axis=0, concat_axis=0, tiled=True),
    )
    slots_in = experts * cap
    valid = recv_gates > 0
    counts = jnp.sum(valid.astype(jnp.int32), axis=1)
    offsets = jnp.cumsum(counts) - counts
    dest = jnp.where(
        valid, offsets[:, None] + jnp.arange(cap, dtype=jnp.int32)[None, :], slots_in
    ).reshape(-1)
    source_of = (
        jnp.full((slots_in + 1,), slots_in, jnp.int32)
        .at[dest]
        .set(jnp.arange(slots_in, dtype=jnp.int32))[:slots_in]
    )
    compact_rows = jnp.concatenate(
        [recv_rows.reshape(slots_in, D), jnp.zeros((1, D), jnp.bfloat16)], axis=0
    )[source_of]
    compact_gates = jnp.concatenate(
        [recv_gates.reshape(-1), jnp.zeros((1,), jnp.bfloat16)], axis=0
    )[source_of].astype(jnp.float32)
    filled = jnp.sum(counts)
    n_blocks = (filled + slots_in - 1) // slots_in
    w_gate = expert_gate[0]
    w_up = expert_up[0]
    w_down = expert_down[0]

    def expert_block(index, results):
        gate_proj = jnp.dot(compact_rows, w_gate, preferred_element_type=jnp.float32)
        up_proj = jnp.dot(compact_rows, w_up, preferred_element_type=jnp.float32)
        inner = (jax.nn.silu(gate_proj) * up_proj).astype(jnp.bfloat16)
        weighted = (
            jnp.dot(inner, w_down, preferred_element_type=jnp.float32) * compact_gates[:, None]
        )
        return weighted.astype(jnp.bfloat16)

    results = lax.fori_loop(0, n_blocks, expert_block, jnp.zeros((slots_in, D), jnp.bfloat16))
    returned = jnp.concatenate([results, jnp.zeros((1, D), jnp.bfloat16)], axis=0)[dest].reshape(
        experts, cap, D
    )
    back = lax.all_to_all(
        returned, ("seq", "sub"), split_axis=0, concat_axis=0, tiled=True
    ).reshape(slots_out, D)
    gathered = back[slot_of].reshape(tokens, topk, D).astype(jnp.float32)
    mixture = jnp.sum(gathered, axis=1)
    return (wide + mixture).astype(jnp.bfloat16)[None]


def solution(mesh):
    placed = (
        P(("grp", "sub"), "seq", None),
        P(("grp", "sub"), "seq", None),
        P(("grp", "sub"), "seq", None),
        P(("grp", "sub"), "seq", None),
        P("seq", None),
        P(),
        P(("grp", "sub"), "seq", None),
        P(("grp", "sub"), "seq", None),
        P(("seq", "sub"), None, None),
        P(("seq", "sub"), None, None),
        P(("seq", "sub"), None, None),
    )
    return jax.shard_map(
        per_device,
        mesh=mesh,
        in_specs=placed,
        out_specs=P(("grp", "sub"), "seq", None),
        check_vma=False,
    )
```

```python
import functools

import jax
import jax.numpy as jnp
from jax import lax
from jax.experimental import pallas as pl
from jax.experimental.pallas import tpu as pltpu
from jax.sharding import PartitionSpec as P

D = 2048
HD = 128
QH = 16
KVH = 2
MIB = 1024 * 1024


def attend_head(queries, keys_one, values_one, block):
    length = queries.shape[0]
    scale = 1.0 / queries.shape[1] ** 0.5
    pieces = []
    for part_index in range(length // block):
        stop = (part_index + 1) * block
        rows_here = queries[part_index * block : stop]
        scores = (
            jnp.einsum("qd,kd->qk", rows_here, keys_one[:stop], preferred_element_type=jnp.float32)
            * scale
        )
        row_pos = part_index * block + jnp.arange(block, dtype=jnp.int32)
        col_pos = jnp.arange(stop, dtype=jnp.int32)
        scores = jnp.where(row_pos[:, None] >= col_pos[None, :], scores, -1e30)
        peak = jnp.max(scores, axis=1, keepdims=True)
        weights = jnp.exp(scores - peak)
        probs = (weights / jnp.sum(weights, axis=1, keepdims=True)).astype(jnp.bfloat16)
        pieces.append(
            jnp.dot(probs, values_one[:stop], preferred_element_type=jnp.float32).astype(
                jnp.bfloat16
            )
        )
    return jnp.concatenate(pieces, axis=0)


def rank_in_expert(flat_ids, experts):
    items = flat_ids.shape[0]
    width = 128
    n_parts = items // width
    onehot = (
        (flat_ids[:, None] == jnp.arange(experts, dtype=jnp.int32)[None, :])
        .astype(jnp.bfloat16)
        .reshape(n_parts, width, experts)
    )
    lower = (
        jnp.arange(width, dtype=jnp.int32)[:, None] > jnp.arange(width, dtype=jnp.int32)[None, :]
    ).astype(jnp.bfloat16)
    within = jnp.einsum("ij,bje->bie", lower, onehot, preferred_element_type=jnp.float32)
    part_counts = jnp.sum(onehot.astype(jnp.float32), axis=1)
    earlier = jnp.cumsum(part_counts, axis=0) - part_counts
    ranks = jnp.sum((within + earlier[:, None, :]) * onehot.astype(jnp.float32), axis=2)
    return ranks.reshape(items).astype(jnp.int32)


def pack_kernel(chip_ref, query_ref, key_ref, value_ref, id_ref, gate_ref, away_ref, here_kv_ref, away_kv_ref):
    tokens = query_ref.shape[0]
    head_size = key_ref.shape[1] // 2
    chip_width = away_ref.shape[1]
    chip = chip_ref[0]
    experts = here_kv_ref.shape[0] - tokens
    away_ref[...] = query_ref[:, pl.ds(pl.multiple_of((1 - chip) * chip_width, chip_width), chip_width)]
    number = lax.broadcasted_iota(jnp.int32, (experts, tokens), 0)
    table = jnp.zeros((experts, tokens), jnp.float32)
    for choice in range(id_ref.shape[0]):
        table += jnp.where(
            number == id_ref[choice : choice + 1, :],
            gate_ref[choice : choice + 1, :].astype(jnp.float32),
            0.0,
        )
    for out_ref, head in ((here_kv_ref, chip), (away_kv_ref, 1 - chip)):
        columns = pl.ds(pl.multiple_of(head * head_size, head_size), head_size)
        out_ref[0:tokens, 0:head_size] = key_ref[:, columns]
        out_ref[0:tokens, head_size:] = value_ref[:, columns]
        out_ref[tokens:, 0:head_size] = table.astype(jnp.bfloat16)
        out_ref[tokens:, head_size:] = jnp.zeros((experts, head_size), jnp.bfloat16)


def pack(chip, queries, keys, values, ids, gates, experts):
    tokens, width = queries.shape
    kv = jax.ShapeDtypeStruct((tokens + experts, keys.shape[1]), jnp.bfloat16)
    return pl.pallas_call(
        pack_kernel,
        in_specs=[pl.BlockSpec(memory_space=pltpu.SMEM)]
        + [pl.BlockSpec(memory_space=pltpu.VMEM)] * 5,
        out_specs=[pl.BlockSpec(memory_space=pltpu.VMEM)] * 3,
        out_shape=[jax.ShapeDtypeStruct((tokens, width // 2), jnp.bfloat16), kv, kv],
        compiler_params=pltpu.CompilerParams(vmem_limit_bytes=6 * MIB),
    )(chip.reshape(1), queries, keys, values, ids, gates)


def attend_kernel(place_ref, query_ref, *refs, scale):
    kv_refs, refs = refs[:4], refs[4:]
    w_own_ref, w_other_ref, out_ref, quad_ref, keys, values, heads, w_own, w_other, done = refs
    fetches = [
        pltpu.make_async_copy(w_own_ref, w_own, done.at[0]),
        pltpu.make_async_copy(w_other_ref, w_other, done.at[1]),
    ]
    for fetch in fetches:
        fetch.start()
    rows = keys.shape[0] // 4
    head_size = keys.shape[1]
    core = place_ref[0]
    query_start = pl.multiple_of(place_ref[1], head_size)
    row_pos = place_ref[2] * rows + lax.broadcasted_iota(jnp.int32, (rows, 1), 0)
    lane = lax.broadcasted_iota(jnp.int32, (1, rows), 1)
    col_pos = jnp.concatenate([place_ref[3 + part] * rows + lane for part in range(4)], axis=1)
    allowed = row_pos >= col_pos
    for part, kv_ref in enumerate(kv_refs):
        keys[part * rows : (part + 1) * rows, :] = kv_ref[0:rows, 0:head_size]
        values[part * rows : (part + 1) * rows, :] = kv_ref[0:rows, head_size:]
        quad_ref[:, part * rows : (part + 1) * rows] = kv_ref[rows:, 0:rows]
    key_block = keys[...]
    value_block = values[...]
    for head in range(heads.shape[1] // head_size):
        query = query_ref[:, pl.ds(query_start + head * head_size, head_size)]
        scores = (
            lax.dot_general(
                query, key_block, (((1,), (1,)), ((), ())), preferred_element_type=jnp.float32
            )
            * scale
        )
        scores = jnp.where(allowed, scores, -1e30)
        weights = jnp.exp(scores - jnp.max(scores, axis=1, keepdims=True))
        probs = (weights / jnp.sum(weights, axis=1, keepdims=True)).astype(jnp.bfloat16)
        heads[:, head * head_size : (head + 1) * head_size] = jnp.dot(
            probs, value_block, preferred_element_type=jnp.float32
        ).astype(jnp.bfloat16)
    for fetch in fetches:
        fetch.wait()
    half = heads.shape[1] // 2
    own = heads[:, pl.ds(pl.multiple_of(core * half, half), half)]
    other = heads[:, pl.ds(pl.multiple_of((1 - core) * half, half), half)]
    out_ref[...] = (
        jnp.dot(own, w_own[...], preferred_element_type=jnp.float32)
        + jnp.dot(other, w_other[...], preferred_element_type=jnp.float32)
    ).astype(out_ref.dtype)


def attend(place, queries, kv_parts, w_own, w_other, dtype):
    tokens = queries.shape[0]
    width = w_own.shape[1]
    chip_width = 2 * w_own.shape[0]
    return pl.pallas_call(
        functools.partial(attend_kernel, scale=1.0 / HD**0.5),
        in_specs=[pl.BlockSpec(memory_space=pltpu.SMEM)]
        + [pl.BlockSpec(memory_space=pltpu.VMEM)] * 5
        + [pl.BlockSpec(memory_space=pl.ANY)] * 2,
        out_specs=[pl.BlockSpec(memory_space=pltpu.VMEM)] * 2,
        out_shape=[
            jax.ShapeDtypeStruct((tokens, width), dtype),
            jax.ShapeDtypeStruct((kv_parts[0].shape[0] - tokens, 4 * tokens), jnp.bfloat16),
        ],
        scratch_shapes=[
            pltpu.VMEM((4 * tokens, HD), jnp.bfloat16),
            pltpu.VMEM((4 * tokens, HD), jnp.bfloat16),
            pltpu.VMEM((tokens, chip_width), jnp.bfloat16),
            pltpu.VMEM(w_own.shape, jnp.bfloat16),
            pltpu.VMEM(w_other.shape, jnp.bfloat16),
            pltpu.SemaphoreType.DMA((2,)),
        ],
        compiler_params=pltpu.CompilerParams(vmem_limit_bytes=16 * MIB),
        cost_estimate=pl.CostEstimate(
            flops=16 * tokens * tokens * chip_width + 2 * tokens * chip_width * width,
            bytes_accessed=4 * w_own.size + 4 * tokens * width,
            transcendentals=4 * tokens * tokens * chip_width // HD,
        ),
    )(place, queries, *kv_parts, w_own, w_other)


def norm_kernel(residual_ref, own_ref, other_ref, gain_ref, hidden_ref, normed_ref):
    hidden = (
        residual_ref[...].astype(jnp.float32) + own_ref[...] + other_ref[...].astype(jnp.float32)
    ).astype(jnp.bfloat16)
    hidden_ref[...] = hidden
    wide = hidden.astype(jnp.float32)
    normed_ref[...] = (
        wide
        * lax.rsqrt(jnp.mean(wide * wide, axis=1, keepdims=True) + 1e-06)
        * gain_ref[...].astype(jnp.float32)
    ).astype(jnp.bfloat16)


def add_and_norm(residual, own, other, gain):
    return pl.pallas_call(
        norm_kernel,
        in_specs=[pl.BlockSpec(memory_space=pltpu.VMEM)] * 4,
        out_specs=[pl.BlockSpec(memory_space=pltpu.VMEM)] * 2,
        out_shape=[jax.ShapeDtypeStruct(residual.shape, jnp.bfloat16)] * 2,
        compiler_params=pltpu.CompilerParams(vmem_limit_bytes=10 * MIB),
    )(residual, own, other, gain)


def pass_kernel(*refs):
    del refs


def meet(*arrays):
    return pl.pallas_call(
        pass_kernel,
        in_specs=[pl.BlockSpec(memory_space=pl.ANY)] * len(arrays),
        out_specs=[pl.BlockSpec(memory_space=pl.ANY)] * len(arrays),
        out_shape=[jax.ShapeDtypeStruct(array.shape, array.dtype) for array in arrays],
        input_output_aliases={index: index for index in range(len(arrays))},
    )(*arrays)


def pass_kernel(*refs):
    del refs


def meet(*arrays):
    return pl.pallas_call(
        pass_kernel,
        in_specs=[pl.BlockSpec(memory_space=pl.ANY)] * len(arrays),
        out_specs=[pl.BlockSpec(memory_space=pl.ANY)] * len(arrays),
        out_shape=[jax.ShapeDtypeStruct(array.shape, array.dtype) for array in arrays],
        input_output_aliases={index: index for index in range(len(arrays))},
        compiler_params=pltpu.CompilerParams(vmem_limit_bytes=MIB),
    )(*arrays)


def experts_kernel(mine_ref, quad_ref, *refs, cap):
    row_refs, refs = refs[:4], refs[4:]
    w_gate_ref, w_up_ref, w_down_ref, own_ref, across_ref, other_ref, packed = refs
    tokens = row_refs[0].shape[0]
    quad = quad_ref[...].astype(jnp.float32)
    expert = lax.broadcasted_iota(jnp.int32, quad.shape, 0)
    line = jnp.sum(jnp.where(expert == mine_ref[0], quad, 0.0), axis=0, keepdims=True)
    gates = jnp.concatenate(
        [line[:, block * tokens : (block + 1) * tokens] for block in range(4)], axis=0
    )
    named = gates > 0
    before = (
        lax.broadcasted_iota(jnp.int32, (tokens, tokens), 0)
        < lax.broadcasted_iota(jnp.int32, (tokens, tokens), 1)
    ).astype(jnp.bfloat16)
    rank = jnp.dot(
        named.astype(jnp.float32).astype(jnp.bfloat16), before, preferred_element_type=jnp.float32
    )
    slot = jnp.where(named, rank.astype(jnp.int32), -1)
    slots = lax.broadcasted_iota(jnp.int32, (cap, tokens), 0)
    picks = []
    weights = []
    for block in range(4):
        chosen = slots == slot[block : block + 1, :]
        picks.append(jnp.where(chosen, 1.0, 0.0).astype(jnp.bfloat16))
        weights.append(
            jnp.sum(jnp.where(chosen, gates[block : block + 1, :], 0.0), axis=1, keepdims=True)
        )
        packed[block * cap : (block + 1) * cap, :] = jnp.dot(
            picks[block], row_refs[block][...], preferred_element_type=jnp.float32
        ).astype(jnp.bfloat16)
    rows = packed[...]
    gate_proj = jnp.dot(rows, w_gate_ref[...], preferred_element_type=jnp.float32)
    up_proj = jnp.dot(rows, w_up_ref[...], preferred_element_type=jnp.float32)
    inner = (gate_proj / (1.0 + jnp.exp(-gate_proj)) * up_proj).astype(jnp.bfloat16)
    result = jnp.dot(inner, w_down_ref[...], preferred_element_type=jnp.float32)
    targets = (
        own_ref.at[...],
        other_ref.at[0:tokens],
        across_ref.at[...],
        other_ref.at[tokens : 2 * tokens],
    )
    for block in range(4):
        part = (result[block * cap : (block + 1) * cap, :] * weights[block]).astype(jnp.bfloat16)
        targets[block][...] = lax.dot_general(
            picks[block], part, (((0,), (0,)), ((), ())), preferred_element_type=jnp.float32
        ).astype(jnp.bfloat16)


def experts_on_rows(mine, quad, row_blocks, w_gate, w_up, w_down, cap):
    tokens, width = row_blocks[0].shape
    hidden_units = w_gate.shape[1]
    return pl.pallas_call(
        functools.partial(experts_kernel, cap=cap),
        in_specs=[pl.BlockSpec(memory_space=pltpu.SMEM)]
        + [pl.BlockSpec(memory_space=pltpu.VMEM)] * 8,
        out_specs=[pl.BlockSpec(memory_space=pltpu.VMEM)] * 3,
        out_shape=[
            jax.ShapeDtypeStruct((tokens, width), jnp.bfloat16),
            jax.ShapeDtypeStruct((tokens, width), jnp.bfloat16),
            jax.ShapeDtypeStruct((2 * tokens, width), jnp.bfloat16),
        ],
        scratch_shapes=[pltpu.VMEM((4 * cap, width), jnp.bfloat16)],
        compiler_params=pltpu.CompilerParams(vmem_limit_bytes=28 * MIB),
        cost_estimate=pl.CostEstimate(
            flops=24 * cap * width * hidden_units,
            bytes_accessed=16 * tokens * width + 6 * width * hidden_units,
            transcendentals=4 * cap * hidden_units,
        ),
    )(mine.reshape(1), quad, *row_blocks, w_gate, w_up, w_down)


def gathered_plan(
    query_rows,
    key_rows,
    value_rows,
    residual_in,
    out_proj,
    norm_gain,
    expert_ids,
    gate_weights,
    expert_gate,
    expert_up,
    expert_down,
    cap,
):
    n_seq = lax.axis_size("seq")
    n_sub = lax.axis_size("sub")
    experts = n_seq * n_sub
    place = lax.axis_index("seq")
    core = place % 2
    chip = place // 2
    twin = [(index, index ^ 1) for index in range(n_seq)]
    across = [(index, (index + 2) % n_seq) for index in range(n_seq)]
    diagonal = [(index, (index ^ 1) ^ 2) for index in range(n_seq)]
    order = [0] + list(range(1, n_sub, 2)) + list(reversed(range(2, n_sub, 2)))

    def ring(steps):
        return [(order[at], order[(at + steps) % n_sub]) for at in range(n_sub)]

    queries = query_rows[0]
    chip_width = queries.shape[1] // 2

    tokens = queries.shape[0]
    queries_away, kv_here, kv_away = pack(
        chip,
        queries,
        key_rows[0],
        value_rows[0],
        expert_ids[0].T,
        gate_weights[0].T,
        experts,
    )
    incoming = lax.ppermute(queries_away, "seq", across)
    kv_parts = [
        kv_here,
        lax.ppermute(kv_here, "seq", twin),
        lax.ppermute(kv_away, "seq", across),
        lax.ppermute(kv_away, "seq", diagonal),
    ]
    w_other = lax.ppermute(out_proj, "seq", twin)
    columns = [place, place ^ 1, place ^ 2, place ^ 3]

    def place_of(query_start, row_block):
        return jnp.stack([core, query_start, row_block] + columns).astype(jnp.int32)

    sent, quad = attend(place_of(0 * place, place ^ 2), incoming, kv_parts, out_proj, w_other, jnp.bfloat16)
    projected_across = lax.ppermute(sent, "seq", across)
    projected, _ = attend(
        place_of(chip * chip_width, place), queries, kv_parts, out_proj, w_other, jnp.float32
    )
    hidden, normed = add_and_norm(residual_in[0], projected, projected_across, norm_gain[None])

    last = n_sub - 1
    mine = place * n_sub + lax.axis_index("sub")

    held = {("row", 0): normed, ("quad", 0): quad}
    ways = {"across": ("seq", across), "twin": ("seq", twin), "on": ("sub", ring(1))}

    def move(array, way):
        return lax.ppermute(array, *ways[way])

    def experts_of(step):
        held["own", step], held["part", step], other = experts_on_rows(
            mine,
            held["quad", step],
            [held[name, step] for name in ("row", "twin", "across", "diagonal")],
            expert_gate[0],
            expert_up[0],
            expert_down[0],
            cap,
        )
        return other

    def twin_sum(step):
        met = move(held["other", step], "twin")
        held["met", step] = met[:tokens]
        return (held["part", step].astype(jnp.float32) + met[tokens:].astype(jnp.float32)).astype(
            jnp.bfloat16
        )

    def sum_of(step, more):
        parts = [held["own", step], held["met", step], held["back", step]] + more
        return sum(part.astype(jnp.float32) for part in parts)

    for turn in range(1, n_sub + 5):
        now = {}
        step = turn - 1
        if step <= last:
            now["across", step] = move(held["row", step], "across")
            if step < last:
                now["row", step + 1] = move(held["row", step], "on")
            held["twin", step] = move(held["row", step], "twin")
        step = turn - 4 if turn < n_sub + 4 else 0
        if 1 <= step <= last or turn == n_sub + 4:
            now["back", step] = move(held["away", step], "across")
        step = turn - 5
        if 1 <= step <= last:
            more = [held["sum", step - 1]] if step > 1 else []
            now["sum", step] = move(sum_of(step, more).astype(jnp.bfloat16), "on")
        step = turn - 2
        if 0 <= step <= last:
            held["diagonal", step] = move(held["across", step], "twin")
            now["other", step] = experts_of(step)
        step = turn - 3 if turn < n_sub + 3 else 0
        if 1 <= step <= last or turn == n_sub + 3:
            now["away", step] = twin_sum(step)
        if turn == 2:
            for steps in range(1, n_sub):
                now["quad", steps] = lax.ppermute(quad, "sub", ring(steps))
        if turn < n_sub + 4:
            now = dict(zip(now.keys(), meet(*now.values())))
        held.update(now)
    total = hidden.astype(jnp.float32) + sum_of(0, [held["sum", last]])
    return total.astype(jnp.bfloat16)[None]


def per_device(
    query_rows,
    key_rows,
    value_rows,
    residual_in,
    out_proj,
    norm_gain,
    expert_ids,
    gate_weights,
    expert_gate,
    expert_up,
    expert_down,
):
    tokens = query_rows.shape[1]
    n_seq = lax.axis_size("seq")
    n_sub = lax.axis_size("sub")
    experts = n_seq * n_sub
    topk = expert_ids.shape[2]
    cap = max(2, (5 * tokens * topk + 4 * experts - 1) // (4 * experts))
    if n_seq == 2 * KVH and KVH == 2 and tokens == HD and n_sub > 2 and experts <= 2 * topk and cap % 16 == 0:
        return gathered_plan(
            query_rows,
            key_rows,
            value_rows,
            residual_in,
            out_proj,
            norm_gain,
            expert_ids,
            gate_weights,
            expert_gate,
            expert_up,
            expert_down,
            cap,
        )
    heads_here = QH // n_seq
    group = QH // KVH
    query_local = lax.all_to_all(query_rows, "seq", split_axis=2, concat_axis=1, tiled=True)
    key_full, value_full = (
        lax.all_gather(key_rows, "seq", axis=1, tiled=True),
        lax.all_gather(value_rows, "seq", axis=1, tiled=True),
    )
    first_head = lax.axis_index("seq") * heads_here
    key_list = []
    value_list = []
    for head in range(heads_here):
        kv_start = (first_head + head) // group * HD
        key_list.append(lax.dynamic_slice_in_dim(key_full[0], kv_start, HD, 1))
        value_list.append(lax.dynamic_slice_in_dim(value_full[0], kv_start, HD, 1))
    length = query_local.shape[1]
    block = min(length, max(512, length // 8))
    outputs = [
        attend_head(
            query_local[0, :, head * HD : (head + 1) * HD], key_list[head], value_list[head], block
        )
        for head in range(heads_here)
    ]
    head_block = jnp.concatenate(outputs, axis=1)[None]
    attended = lax.all_to_all(head_block, "seq", split_axis=1, concat_axis=2, tiled=True)[0]
    projected = jnp.dot(
        attended,
        lax.all_gather(out_proj, "seq", axis=0, tiled=True),
        preferred_element_type=jnp.float32,
    )
    hidden = (residual_in[0].astype(jnp.float32) + projected).astype(jnp.bfloat16)
    wide = hidden.astype(jnp.float32)
    normed = (
        wide
        * lax.rsqrt(jnp.mean(wide * wide, axis=1, keepdims=True) + 1e-06)
        * norm_gain.astype(jnp.float32)
    ).astype(jnp.bfloat16)
    flat_ids = expert_ids[0].reshape(-1)
    items = flat_ids.shape[0]
    ranks = rank_in_expert(flat_ids, experts)
    slot_of = flat_ids * cap + ranks
    slots_out = experts * cap
    item_of_slot = (
        jnp.full((slots_out,), items, jnp.int32).at[slot_of].set(jnp.arange(items, dtype=jnp.int32))
    )
    padded_rows = jnp.concatenate([normed, jnp.zeros((1, D), jnp.bfloat16)], axis=0)
    padded_gates = jnp.concatenate(
        [gate_weights[0].reshape(-1), jnp.zeros((1,), jnp.bfloat16)], axis=0
    )
    token_of_slot = jnp.where(item_of_slot < items, item_of_slot // topk, tokens)
    send_rows = padded_rows[token_of_slot].reshape(experts, cap, D)
    send_gates = padded_gates[item_of_slot].reshape(experts, cap)
    recv_rows, recv_gates = (
        lax.all_to_all(send_rows, ("seq", "sub"), split_axis=0, concat_axis=0, tiled=True),
        lax.all_to_all(send_gates, ("seq", "sub"), split_axis=0, concat_axis=0, tiled=True),
    )
    slots_in = experts * cap
    valid = recv_gates > 0
    counts = jnp.sum(valid.astype(jnp.int32), axis=1)
    offsets = jnp.cumsum(counts) - counts
    dest = jnp.where(
        valid, offsets[:, None] + jnp.arange(cap, dtype=jnp.int32)[None, :], slots_in
    ).reshape(-1)
    source_of = (
        jnp.full((slots_in + 1,), slots_in, jnp.int32)
        .at[dest]
        .set(jnp.arange(slots_in, dtype=jnp.int32))[:slots_in]
    )
    compact_rows = jnp.concatenate(
        [recv_rows.reshape(slots_in, D), jnp.zeros((1, D), jnp.bfloat16)], axis=0
    )[source_of]
    compact_gates = jnp.concatenate(
        [recv_gates.reshape(-1), jnp.zeros((1,), jnp.bfloat16)], axis=0
    )[source_of].astype(jnp.float32)
    filled = jnp.sum(counts)
    n_blocks = (filled + slots_in - 1) // slots_in
    w_gate = expert_gate[0]
    w_up = expert_up[0]
    w_down = expert_down[0]

    def expert_block(index, results):
        gate_proj = jnp.dot(compact_rows, w_gate, preferred_element_type=jnp.float32)
        up_proj = jnp.dot(compact_rows, w_up, preferred_element_type=jnp.float32)
        inner = (jax.nn.silu(gate_proj) * up_proj).astype(jnp.bfloat16)
        weighted = (
            jnp.dot(inner, w_down, preferred_element_type=jnp.float32) * compact_gates[:, None]
        )
        return weighted.astype(jnp.bfloat16)

    results = lax.fori_loop(0, n_blocks, expert_block, jnp.zeros((slots_in, D), jnp.bfloat16))
    returned = jnp.concatenate([results, jnp.zeros((1, D), jnp.bfloat16)], axis=0)[dest].reshape(
        experts, cap, D
    )
    back = lax.all_to_all(
        returned, ("seq", "sub"), split_axis=0, concat_axis=0, tiled=True
    ).reshape(slots_out, D)
    gathered = back[slot_of].reshape(tokens, topk, D).astype(jnp.float32)
    mixture = jnp.sum(gathered, axis=1)
    return (wide + mixture).astype(jnp.bfloat16)[None]


def solution(mesh):
    placed = (
        P(("grp", "sub"), "seq", None),
        P(("grp", "sub"), "seq", None),
        P(("grp", "sub"), "seq", None),
        P(("grp", "sub"), "seq", None),
        P("seq", None),
        P(),
        P(("grp", "sub"), "seq", None),
        P(("grp", "sub"), "seq", None),
        P(("seq", "sub"), None, None),
        P(("seq", "sub"), None, None),
        P(("seq", "sub"), None, None),
    )
    return jax.shard_map(
        per_device,
        mesh=mesh,
        in_specs=placed,
        out_specs=P(("grp", "sub"), "seq", None),
        check_vma=False,
    )
```

```python
import functools

import jax
import jax.numpy as jnp
from jax import lax
from jax.experimental import pallas as pl
from jax.experimental.pallas import tpu as pltpu
from jax.sharding import PartitionSpec as P

D = 2048
HD = 128
QH = 16
KVH = 2
MIB = 1024 * 1024


def attend_head(queries, keys_one, values_one, block):
    length = queries.shape[0]
    scale = 1.0 / queries.shape[1] ** 0.5
    pieces = []
    for part_index in range(length // block):
        stop = (part_index + 1) * block
        rows_here = queries[part_index * block : stop]
        scores = (
            jnp.einsum("qd,kd->qk", rows_here, keys_one[:stop], preferred_element_type=jnp.float32)
            * scale
        )
        row_pos = part_index * block + jnp.arange(block, dtype=jnp.int32)
        col_pos = jnp.arange(stop, dtype=jnp.int32)
        scores = jnp.where(row_pos[:, None] >= col_pos[None, :], scores, -1e30)
        peak = jnp.max(scores, axis=1, keepdims=True)
        weights = jnp.exp(scores - peak)
        probs = (weights / jnp.sum(weights, axis=1, keepdims=True)).astype(jnp.bfloat16)
        pieces.append(
            jnp.dot(probs, values_one[:stop], preferred_element_type=jnp.float32).astype(
                jnp.bfloat16
            )
        )
    return jnp.concatenate(pieces, axis=0)


def rank_in_expert(flat_ids, experts):
    items = flat_ids.shape[0]
    width = 128
    n_parts = items // width
    onehot = (
        (flat_ids[:, None] == jnp.arange(experts, dtype=jnp.int32)[None, :])
        .astype(jnp.bfloat16)
        .reshape(n_parts, width, experts)
    )
    lower = (
        jnp.arange(width, dtype=jnp.int32)[:, None] > jnp.arange(width, dtype=jnp.int32)[None, :]
    ).astype(jnp.bfloat16)
    within = jnp.einsum("ij,bje->bie", lower, onehot, preferred_element_type=jnp.float32)
    part_counts = jnp.sum(onehot.astype(jnp.float32), axis=1)
    earlier = jnp.cumsum(part_counts, axis=0) - part_counts
    ranks = jnp.sum((within + earlier[:, None, :]) * onehot.astype(jnp.float32), axis=2)
    return ranks.reshape(items).astype(jnp.int32)


def pack_kernel(chip_ref, query_ref, key_ref, value_ref, id_ref, gate_ref, away_ref, here_kv_ref, away_kv_ref):
    tokens = query_ref.shape[0]
    head_size = key_ref.shape[1] // 2
    chip_width = away_ref.shape[1]
    chip = chip_ref[0]
    experts = here_kv_ref.shape[0] - tokens
    away_ref[...] = query_ref[:, pl.ds(pl.multiple_of((1 - chip) * chip_width, chip_width), chip_width)]
    number = lax.broadcasted_iota(jnp.int32, (experts, tokens), 0)
    table = jnp.zeros((experts, tokens), jnp.float32)
    for choice in range(id_ref.shape[0]):
        table += jnp.where(
            number == id_ref[choice : choice + 1, :],
            gate_ref[choice : choice + 1, :].astype(jnp.float32),
            0.0,
        )
    for out_ref, head in ((here_kv_ref, chip), (away_kv_ref, 1 - chip)):
        columns = pl.ds(pl.multiple_of(head * head_size, head_size), head_size)
        out_ref[0:tokens, 0:head_size] = key_ref[:, columns]
        out_ref[0:tokens, head_size:] = value_ref[:, columns]
        out_ref[tokens:, 0:head_size] = table.astype(jnp.bfloat16)
        out_ref[tokens:, head_size:] = jnp.zeros((experts, head_size), jnp.bfloat16)


def pack(chip, queries, keys, values, ids, gates, experts):
    tokens, width = queries.shape
    kv = jax.ShapeDtypeStruct((tokens + experts, keys.shape[1]), jnp.bfloat16)
    return pl.pallas_call(
        pack_kernel,
        in_specs=[pl.BlockSpec(memory_space=pltpu.SMEM)]
        + [pl.BlockSpec(memory_space=pltpu.VMEM)] * 5,
        out_specs=[pl.BlockSpec(memory_space=pltpu.VMEM)] * 3,
        out_shape=[jax.ShapeDtypeStruct((tokens, width // 2), jnp.bfloat16), kv, kv],
        compiler_params=pltpu.CompilerParams(vmem_limit_bytes=60 * MIB),
    )(chip.reshape(1), queries, keys, values, ids, gates)


def attend_kernel(place_ref, query_ref, *refs, scale):
    kv_refs, refs = refs[:4], refs[4:]
    base_refs = refs[: len(refs) - 10]
    w_own_ref, w_other_ref, out_ref, quad_ref, keys, values, heads, w_own, w_other, done = refs[-10:]
    fetches = [
        pltpu.make_async_copy(w_own_ref, w_own, done.at[0]),
        pltpu.make_async_copy(w_other_ref, w_other, done.at[1]),
    ]
    for fetch in fetches:
        fetch.start()
    rows = keys.shape[0] // 4
    head_size = keys.shape[1]
    core = place_ref[0]
    query_start = pl.multiple_of(place_ref[1], head_size)
    row_pos = place_ref[2] * rows + lax.broadcasted_iota(jnp.int32, (rows, 1), 0)
    lane = lax.broadcasted_iota(jnp.int32, (1, rows), 1)
    col_pos = jnp.concatenate([place_ref[3 + part] * rows + lane for part in range(4)], axis=1)
    allowed = row_pos >= col_pos
    for part, kv_ref in enumerate(kv_refs):
        keys[part * rows : (part + 1) * rows, :] = kv_ref[0:rows, 0:head_size]
        values[part * rows : (part + 1) * rows, :] = kv_ref[0:rows, head_size:]
        quad_ref[:, part * rows : (part + 1) * rows] = kv_ref[rows:, 0:rows]
    key_block = keys[...]
    value_block = values[...]
    for head in range(heads.shape[1] // head_size):
        query = query_ref[:, pl.ds(query_start + head * head_size, head_size)]
        scores = (
            lax.dot_general(
                query, key_block, (((1,), (1,)), ((), ())), preferred_element_type=jnp.float32
            )
            * scale
        )
        scores = jnp.where(allowed, scores, -1e30)
        weights = jnp.exp(scores - jnp.max(scores, axis=1, keepdims=True))
        probs = (weights / jnp.sum(weights, axis=1, keepdims=True)).astype(jnp.bfloat16)
        heads[:, head * head_size : (head + 1) * head_size] = jnp.dot(
            probs, value_block, preferred_element_type=jnp.float32
        ).astype(jnp.bfloat16)
    for fetch in fetches:
        fetch.wait()
    half = heads.shape[1] // 2
    own = heads[:, pl.ds(pl.multiple_of(core * half, half), half)]
    other = heads[:, pl.ds(pl.multiple_of((1 - core) * half, half), half)]
    total = jnp.dot(own, w_own[...], preferred_element_type=jnp.float32) + jnp.dot(
        other, w_other[...], preferred_element_type=jnp.float32
    )
    for base_ref in base_refs:
        total += base_ref[...].astype(jnp.float32)
    out_ref[...] = total.astype(out_ref.dtype)


def attend(place, queries, kv_parts, bases, w_own, w_other, dtype):
    tokens = queries.shape[0]
    width = w_own.shape[1]
    chip_width = 2 * w_own.shape[0]
    return pl.pallas_call(
        functools.partial(attend_kernel, scale=1.0 / HD**0.5),
        in_specs=[pl.BlockSpec(memory_space=pltpu.SMEM)]
        + [pl.BlockSpec(memory_space=pltpu.VMEM)] * (5 + len(bases))
        + [pl.BlockSpec(memory_space=pl.ANY)] * 2,
        out_specs=[pl.BlockSpec(memory_space=pltpu.VMEM)] * 2,
        out_shape=[
            jax.ShapeDtypeStruct((tokens, width), dtype),
            jax.ShapeDtypeStruct((kv_parts[0].shape[0] - tokens, 4 * tokens), jnp.bfloat16),
        ],
        scratch_shapes=[
            pltpu.VMEM((4 * tokens, HD), jnp.bfloat16),
            pltpu.VMEM((4 * tokens, HD), jnp.bfloat16),
            pltpu.VMEM((tokens, chip_width), jnp.bfloat16),
            pltpu.VMEM(w_own.shape, jnp.bfloat16),
            pltpu.VMEM(w_other.shape, jnp.bfloat16),
            pltpu.SemaphoreType.DMA((2,)),
        ],
        compiler_params=pltpu.CompilerParams(vmem_limit_bytes=16 * MIB),
        cost_estimate=pl.CostEstimate(
            flops=16 * tokens * tokens * chip_width + 2 * tokens * chip_width * width,
            bytes_accessed=4 * w_own.size + 4 * tokens * width,
            transcendentals=4 * tokens * tokens * chip_width // HD,
        ),
    )(place, queries, *kv_parts, *bases, w_own, w_other)


def norm_kernel(own_ref, other_ref, gain_ref, hidden_ref, normed_ref):
    hidden = (own_ref[...] + other_ref[...].astype(jnp.float32)).astype(jnp.bfloat16)
    hidden_ref[...] = hidden
    wide = hidden.astype(jnp.float32)
    normed_ref[...] = (
        wide
        * lax.rsqrt(jnp.mean(wide * wide, axis=1, keepdims=True) + 1e-06)
        * gain_ref[...].astype(jnp.float32)
    ).astype(jnp.bfloat16)


def add_and_norm(own, other, gain):
    return pl.pallas_call(
        norm_kernel,
        in_specs=[pl.BlockSpec(memory_space=pltpu.VMEM)] * 3,
        out_specs=[pl.BlockSpec(memory_space=pltpu.VMEM)] * 2,
        out_shape=[jax.ShapeDtypeStruct(own.shape, jnp.bfloat16)] * 2,
        compiler_params=pltpu.CompilerParams(vmem_limit_bytes=10 * MIB),
    )(own, other, gain)


def pass_kernel(*refs):
    del refs


def meet(*arrays):
    return pl.pallas_call(
        pass_kernel,
        in_specs=[pl.BlockSpec(memory_space=pl.ANY)] * len(arrays),
        out_specs=[pl.BlockSpec(memory_space=pl.ANY)] * len(arrays),
        out_shape=[jax.ShapeDtypeStruct(array.shape, array.dtype) for array in arrays],
        input_output_aliases={index: index for index in range(len(arrays))},
    )(*arrays)


def pass_kernel(*refs):
    del refs


def meet(*arrays):
    return pl.pallas_call(
        pass_kernel,
        in_specs=[pl.BlockSpec(memory_space=pl.ANY)] * len(arrays),
        out_specs=[pl.BlockSpec(memory_space=pl.ANY)] * len(arrays),
        out_shape=[jax.ShapeDtypeStruct(array.shape, array.dtype) for array in arrays],
        input_output_aliases={index: index for index in range(len(arrays))},
        compiler_params=pltpu.CompilerParams(vmem_limit_bytes=MIB),
    )(*arrays)


def experts_kernel(mine_ref, quad_ref, *refs, cap):
    row_refs, refs = refs[:4], refs[4:]
    w_gate_ref, w_up_ref, w_down_ref, own_ref, across_ref, other_ref, packed = refs
    tokens = row_refs[0].shape[0]
    quad = quad_ref[...].astype(jnp.float32)
    expert = lax.broadcasted_iota(jnp.int32, quad.shape, 0)
    line = jnp.sum(jnp.where(expert == mine_ref[0], quad, 0.0), axis=0, keepdims=True)
    gates = jnp.concatenate(
        [line[:, block * tokens : (block + 1) * tokens] for block in range(4)], axis=0
    )
    named = gates > 0
    before = (
        lax.broadcasted_iota(jnp.int32, (tokens, tokens), 0)
        < lax.broadcasted_iota(jnp.int32, (tokens, tokens), 1)
    ).astype(jnp.bfloat16)
    rank = jnp.dot(
        named.astype(jnp.float32).astype(jnp.bfloat16), before, preferred_element_type=jnp.float32
    )
    slot = jnp.where(named, rank.astype(jnp.int32), -1)
    slots = lax.broadcasted_iota(jnp.int32, (cap, tokens), 0)
    picks = []
    weights = []
    for block in range(4):
        chosen = slots == slot[block : block + 1, :]
        picks.append(jnp.where(chosen, 1.0, 0.0).astype(jnp.bfloat16))
        weights.append(
            jnp.sum(jnp.where(chosen, gates[block : block + 1, :], 0.0), axis=1, keepdims=True)
        )
        packed[block * cap : (block + 1) * cap, :] = jnp.dot(
            picks[block], row_refs[block][...], preferred_element_type=jnp.float32
        ).astype(jnp.bfloat16)
    rows = packed[...]
    gate_proj = jnp.dot(rows, w_gate_ref[...], preferred_element_type=jnp.float32)
    up_proj = jnp.dot(rows, w_up_ref[...], preferred_element_type=jnp.float32)
    inner = (gate_proj / (1.0 + jnp.exp(-gate_proj)) * up_proj).astype(jnp.bfloat16)
    result = jnp.dot(inner, w_down_ref[...], preferred_element_type=jnp.float32)
    targets = (
        own_ref.at[...],
        other_ref.at[0:tokens],
        across_ref.at[...],
        other_ref.at[tokens : 2 * tokens],
    )
    for block in range(4):
        part = (result[block * cap : (block + 1) * cap, :] * weights[block]).astype(jnp.bfloat16)
        targets[block][...] = lax.dot_general(
            picks[block], part, (((0,), (0,)), ((), ())), preferred_element_type=jnp.float32
        ).astype(jnp.bfloat16)


def experts_on_rows(mine, quad, row_blocks, w_gate, w_up, w_down, cap):
    tokens, width = row_blocks[0].shape
    hidden_units = w_gate.shape[1]
    return pl.pallas_call(
        functools.partial(experts_kernel, cap=cap),
        in_specs=[pl.BlockSpec(memory_space=pltpu.SMEM)]
        + [pl.BlockSpec(memory_space=pltpu.VMEM)] * 8,
        out_specs=[pl.BlockSpec(memory_space=pltpu.VMEM)] * 3,
        out_shape=[
            jax.ShapeDtypeStruct((tokens, width), jnp.bfloat16),
            jax.ShapeDtypeStruct((tokens, width), jnp.bfloat16),
            jax.ShapeDtypeStruct((2 * tokens, width), jnp.bfloat16),
        ],
        scratch_shapes=[pltpu.VMEM((4 * cap, width), jnp.bfloat16)],
        compiler_params=pltpu.CompilerParams(vmem_limit_bytes=28 * MIB),
        cost_estimate=pl.CostEstimate(
            flops=24 * cap * width * hidden_units,
            bytes_accessed=16 * tokens * width + 6 * width * hidden_units,
            transcendentals=4 * cap * hidden_units,
        ),
    )(mine.reshape(1), quad, *row_blocks, w_gate, w_up, w_down)


def gathered_plan(
    query_rows,
    key_rows,
    value_rows,
    residual_in,
    out_proj,
    norm_gain,
    expert_ids,
    gate_weights,
    expert_gate,
    expert_up,
    expert_down,
    cap,
):
    n_seq = lax.axis_size("seq")
    n_sub = lax.axis_size("sub")
    experts = n_seq * n_sub
    place = lax.axis_index("seq")
    core = place % 2
    chip = place // 2
    twin = [(index, index ^ 1) for index in range(n_seq)]
    across = [(index, (index + 2) % n_seq) for index in range(n_seq)]
    diagonal = [(index, (index ^ 1) ^ 2) for index in range(n_seq)]
    order = [0] + list(range(1, n_sub, 2)) + list(reversed(range(2, n_sub, 2)))

    def ring(steps):
        return [(order[at], order[(at + steps) % n_sub]) for at in range(n_sub)]

    queries = query_rows[0]
    chip_width = queries.shape[1] // 2

    tokens = queries.shape[0]
    queries_away, kv_here, kv_away = pack(
        chip,
        queries,
        key_rows[0],
        value_rows[0],
        expert_ids[0].T,
        gate_weights[0].T,
        experts,
    )
    incoming = lax.ppermute(queries_away, "seq", across)
    kv_parts = [
        kv_here,
        lax.ppermute(kv_here, "seq", twin),
        lax.ppermute(kv_away, "seq", across),
        lax.ppermute(kv_away, "seq", diagonal),
    ]
    w_other = lax.ppermute(out_proj, "seq", twin)
    columns = [place, place ^ 1, place ^ 2, place ^ 3]

    def place_of(query_start, row_block):
        return jnp.stack([core, query_start, row_block] + columns).astype(jnp.int32)

    sent, quad = attend(
        place_of(0 * place, place ^ 2), incoming, kv_parts, [], out_proj, w_other, jnp.bfloat16
    )
    projected_across = lax.ppermute(sent, "seq", across)
    projected, _ = attend(
        place_of(chip * chip_width, place),
        queries,
        kv_parts,
        [residual_in[0]],
        out_proj,
        w_other,
        jnp.float32,
    )
    hidden, normed = add_and_norm(projected, projected_across, norm_gain[None])

    last = n_sub - 1
    mine = place * n_sub + lax.axis_index("sub")

    held = {("row", 0): normed, ("quad", 0): quad}
    ways = {"across": ("seq", across), "twin": ("seq", twin), "on": ("sub", ring(1))}

    def move(array, way):
        return lax.ppermute(array, *ways[way])

    def experts_of(step):
        held["own", step], held["part", step], other = experts_on_rows(
            mine,
            held["quad", step],
            [held[name, step] for name in ("row", "twin", "across", "diagonal")],
            expert_gate[0],
            expert_up[0],
            expert_down[0],
            cap,
        )
        return other

    def twin_sum(step):
        met = move(held["other", step], "twin")
        held["met", step] = met[:tokens]
        return (held["part", step].astype(jnp.float32) + met[tokens:].astype(jnp.float32)).astype(
            jnp.bfloat16
        )

    def sum_of(step, more):
        parts = [held["own", step], held["met", step], held["back", step]] + more
        return sum(part.astype(jnp.float32) for part in parts)

    for turn in range(1, n_sub + 5):
        now = {}
        step = turn - 1
        if step <= last:
            now["across", step] = move(held["row", step], "across")
            if step < last:
                now["row", step + 1] = move(held["row", step], "on")
            held["twin", step] = move(held["row", step], "twin")
        step = turn - 4 if turn < n_sub + 4 else 0
        if 1 <= step <= last or turn == n_sub + 4:
            now["back", step] = move(held["away", step], "across")
        step = turn - 5
        if 1 <= step <= last:
            more = [held["sum", step - 1]] if step > 1 else []
            now["sum", step] = move(sum_of(step, more).astype(jnp.bfloat16), "on")
        step = turn - 2
        if 0 <= step <= last:
            held["diagonal", step] = move(held["across", step], "twin")
        if 1 <= step <= last:
            now["other", step] = experts_of(step)
        if turn == n_sub + 2:
            now["other", 0] = experts_of(0)
        step = turn - 3 if turn < n_sub + 3 else 0
        if 1 <= step <= last or turn == n_sub + 3:
            now["away", step] = twin_sum(step)
        if turn == 1:
            for steps in range(1, n_sub):
                now["quad", steps] = lax.ppermute(quad, "sub", ring(steps))
        if turn < n_sub + 4:
            now = dict(zip(now.keys(), meet(*now.values())))
        held.update(now)
    total = hidden.astype(jnp.float32) + sum_of(0, [held["sum", last]])
    return total.astype(jnp.bfloat16)[None]


def per_device(
    query_rows,
    key_rows,
    value_rows,
    residual_in,
    out_proj,
    norm_gain,
    expert_ids,
    gate_weights,
    expert_gate,
    expert_up,
    expert_down,
):
    tokens = query_rows.shape[1]
    n_seq = lax.axis_size("seq")
    n_sub = lax.axis_size("sub")
    experts = n_seq * n_sub
    topk = expert_ids.shape[2]
    cap = max(2, (5 * tokens * topk + 4 * experts - 1) // (4 * experts))
    if n_seq == 2 * KVH and KVH == 2 and tokens == HD and n_sub > 2 and experts <= 2 * topk and cap % 16 == 0:
        return gathered_plan(
            query_rows,
            key_rows,
            value_rows,
            residual_in,
            out_proj,
            norm_gain,
            expert_ids,
            gate_weights,
            expert_gate,
            expert_up,
            expert_down,
            cap,
        )
    heads_here = QH // n_seq
    group = QH // KVH
    query_local = lax.all_to_all(query_rows, "seq", split_axis=2, concat_axis=1, tiled=True)
    key_full, value_full = (
        lax.all_gather(key_rows, "seq", axis=1, tiled=True),
        lax.all_gather(value_rows, "seq", axis=1, tiled=True),
    )
    first_head = lax.axis_index("seq") * heads_here
    key_list = []
    value_list = []
    for head in range(heads_here):
        kv_start = (first_head + head) // group * HD
        key_list.append(lax.dynamic_slice_in_dim(key_full[0], kv_start, HD, 1))
        value_list.append(lax.dynamic_slice_in_dim(value_full[0], kv_start, HD, 1))
    length = query_local.shape[1]
    block = min(length, max(512, length // 8))
    outputs = [
        attend_head(
            query_local[0, :, head * HD : (head + 1) * HD], key_list[head], value_list[head], block
        )
        for head in range(heads_here)
    ]
    head_block = jnp.concatenate(outputs, axis=1)[None]
    attended = lax.all_to_all(head_block, "seq", split_axis=1, concat_axis=2, tiled=True)[0]
    projected = jnp.dot(
        attended,
        lax.all_gather(out_proj, "seq", axis=0, tiled=True),
        preferred_element_type=jnp.float32,
    )
    hidden = (residual_in[0].astype(jnp.float32) + projected).astype(jnp.bfloat16)
    wide = hidden.astype(jnp.float32)
    normed = (
        wide
        * lax.rsqrt(jnp.mean(wide * wide, axis=1, keepdims=True) + 1e-06)
        * norm_gain.astype(jnp.float32)
    ).astype(jnp.bfloat16)
    flat_ids = expert_ids[0].reshape(-1)
    items = flat_ids.shape[0]
    ranks = rank_in_expert(flat_ids, experts)
    slot_of = flat_ids * cap + ranks
    slots_out = experts * cap
    item_of_slot = (
        jnp.full((slots_out,), items, jnp.int32).at[slot_of].set(jnp.arange(items, dtype=jnp.int32))
    )
    padded_rows = jnp.concatenate([normed, jnp.zeros((1, D), jnp.bfloat16)], axis=0)
    padded_gates = jnp.concatenate(
        [gate_weights[0].reshape(-1), jnp.zeros((1,), jnp.bfloat16)], axis=0
    )
    token_of_slot = jnp.where(item_of_slot < items, item_of_slot // topk, tokens)
    send_rows = padded_rows[token_of_slot].reshape(experts, cap, D)
    send_gates = padded_gates[item_of_slot].reshape(experts, cap)
    recv_rows, recv_gates = (
        lax.all_to_all(send_rows, ("seq", "sub"), split_axis=0, concat_axis=0, tiled=True),
        lax.all_to_all(send_gates, ("seq", "sub"), split_axis=0, concat_axis=0, tiled=True),
    )
    slots_in = experts * cap
    valid = recv_gates > 0
    counts = jnp.sum(valid.astype(jnp.int32), axis=1)
    offsets = jnp.cumsum(counts) - counts
    dest = jnp.where(
        valid, offsets[:, None] + jnp.arange(cap, dtype=jnp.int32)[None, :], slots_in
    ).reshape(-1)
    source_of = (
        jnp.full((slots_in + 1,), slots_in, jnp.int32)
        .at[dest]
        .set(jnp.arange(slots_in, dtype=jnp.int32))[:slots_in]
    )
    compact_rows = jnp.concatenate(
        [recv_rows.reshape(slots_in, D), jnp.zeros((1, D), jnp.bfloat16)], axis=0
    )[source_of]
    compact_gates = jnp.concatenate(
        [recv_gates.reshape(-1), jnp.zeros((1,), jnp.bfloat16)], axis=0
    )[source_of].astype(jnp.float32)
    filled = jnp.sum(counts)
    n_blocks = (filled + slots_in - 1) // slots_in
    w_gate = expert_gate[0]
    w_up = expert_up[0]
    w_down = expert_down[0]

    def expert_block(index, results):
        gate_proj = jnp.dot(compact_rows, w_gate, preferred_element_type=jnp.float32)
        up_proj = jnp.dot(compact_rows, w_up, preferred_element_type=jnp.float32)
        inner = (jax.nn.silu(gate_proj) * up_proj).astype(jnp.bfloat16)
        weighted = (
            jnp.dot(inner, w_down, preferred_element_type=jnp.float32) * compact_gates[:, None]
        )
        return weighted.astype(jnp.bfloat16)

    results = lax.fori_loop(0, n_blocks, expert_block, jnp.zeros((slots_in, D), jnp.bfloat16))
    returned = jnp.concatenate([results, jnp.zeros((1, D), jnp.bfloat16)], axis=0)[dest].reshape(
        experts, cap, D
    )
    back = lax.all_to_all(
        returned, ("seq", "sub"), split_axis=0, concat_axis=0, tiled=True
    ).reshape(slots_out, D)
    gathered = back[slot_of].reshape(tokens, topk, D).astype(jnp.float32)
    mixture = jnp.sum(gathered, axis=1)
    return (wide + mixture).astype(jnp.bfloat16)[None]


def solution(mesh):
    placed = (
        P(("grp", "sub"), "seq", None),
        P(("grp", "sub"), "seq", None),
        P(("grp", "sub"), "seq", None),
        P(("grp", "sub"), "seq", None),
        P("seq", None),
        P(),
        P(("grp", "sub"), "seq", None),
        P(("grp", "sub"), "seq", None),
        P(("seq", "sub"), None, None),
        P(("seq", "sub"), None, None),
        P(("seq", "sub"), None, None),
    )
    return jax.shard_map(
        per_device,
        mesh=mesh,
        in_specs=placed,
        out_specs=P(("grp", "sub"), "seq", None),
        check_vma=False,
    )
```

```python
import functools

import jax
import jax.numpy as jnp
from jax import lax
from jax.experimental import pallas as pl
from jax.experimental.pallas import tpu as pltpu
from jax.sharding import PartitionSpec as P

D = 2048
HD = 128
QH = 16
KVH = 2
MIB = 1024 * 1024


def attend_head(queries, keys_one, values_one, block):
    length = queries.shape[0]
    scale = 1.0 / queries.shape[1] ** 0.5
    pieces = []
    for part_index in range(length // block):
        stop = (part_index + 1) * block
        rows_here = queries[part_index * block : stop]
        scores = (
            jnp.einsum("qd,kd->qk", rows_here, keys_one[:stop], preferred_element_type=jnp.float32)
            * scale
        )
        row_pos = part_index * block + jnp.arange(block, dtype=jnp.int32)
        col_pos = jnp.arange(stop, dtype=jnp.int32)
        scores = jnp.where(row_pos[:, None] >= col_pos[None, :], scores, -1e30)
        peak = jnp.max(scores, axis=1, keepdims=True)
        weights = jnp.exp(scores - peak)
        probs = (weights / jnp.sum(weights, axis=1, keepdims=True)).astype(jnp.bfloat16)
        pieces.append(
            jnp.dot(probs, values_one[:stop], preferred_element_type=jnp.float32).astype(
                jnp.bfloat16
            )
        )
    return jnp.concatenate(pieces, axis=0)


def rank_in_expert(flat_ids, experts):
    items = flat_ids.shape[0]
    width = 128
    n_parts = items // width
    onehot = (
        (flat_ids[:, None] == jnp.arange(experts, dtype=jnp.int32)[None, :])
        .astype(jnp.bfloat16)
        .reshape(n_parts, width, experts)
    )
    lower = (
        jnp.arange(width, dtype=jnp.int32)[:, None] > jnp.arange(width, dtype=jnp.int32)[None, :]
    ).astype(jnp.bfloat16)
    within = jnp.einsum("ij,bje->bie", lower, onehot, preferred_element_type=jnp.float32)
    part_counts = jnp.sum(onehot.astype(jnp.float32), axis=1)
    earlier = jnp.cumsum(part_counts, axis=0) - part_counts
    ranks = jnp.sum((within + earlier[:, None, :]) * onehot.astype(jnp.float32), axis=2)
    return ranks.reshape(items).astype(jnp.int32)


def pack_kernel(chip_ref, query_ref, key_ref, value_ref, id_ref, gate_ref, away_ref, here_kv_ref, away_kv_ref):
    tokens = query_ref.shape[0]
    head_size = key_ref.shape[1] // 2
    chip_width = away_ref.shape[1]
    chip = chip_ref[0]
    experts = here_kv_ref.shape[0] - tokens
    away_ref[...] = query_ref[:, pl.ds(pl.multiple_of((1 - chip) * chip_width, chip_width), chip_width)]
    number = lax.broadcasted_iota(jnp.int32, (experts, tokens), 0)
    table = jnp.zeros((experts, tokens), jnp.float32)
    for choice in range(id_ref.shape[0]):
        table += jnp.where(
            number == id_ref[choice : choice + 1, :],
            gate_ref[choice : choice + 1, :].astype(jnp.float32),
            0.0,
        )
    for out_ref, head in ((here_kv_ref, chip), (away_kv_ref, 1 - chip)):
        columns = pl.ds(pl.multiple_of(head * head_size, head_size), head_size)
        out_ref[0:tokens, 0:head_size] = key_ref[:, columns]
        out_ref[0:tokens, head_size:] = value_ref[:, columns]
        out_ref[tokens:, 0:head_size] = table.astype(jnp.bfloat16)
        out_ref[tokens:, head_size:] = jnp.zeros((experts, head_size), jnp.bfloat16)


def pack(chip, queries, keys, values, ids, gates, experts):
    tokens, width = queries.shape
    kv = jax.ShapeDtypeStruct((tokens + experts, keys.shape[1]), jnp.bfloat16)
    return pl.pallas_call(
        pack_kernel,
        in_specs=[pl.BlockSpec(memory_space=pltpu.SMEM)]
        + [pl.BlockSpec(memory_space=pltpu.VMEM)] * 5,
        out_specs=[pl.BlockSpec(memory_space=pltpu.VMEM)] * 3,
        out_shape=[jax.ShapeDtypeStruct((tokens, width // 2), jnp.bfloat16), kv, kv],
        compiler_params=pltpu.CompilerParams(vmem_limit_bytes=60 * MIB),
    )(chip.reshape(1), queries, keys, values, ids, gates)


def attend_kernel(place_ref, query_ref, *refs, scale):
    kv_refs, refs = refs[:4], refs[4:]
    base_refs = refs[: len(refs) - 10]
    w_own_ref, w_other_ref, out_ref, quad_ref, keys, values, heads, w_own, w_other, done = refs[-10:]
    fetches = [
        pltpu.make_async_copy(w_own_ref, w_own, done.at[0]),
        pltpu.make_async_copy(w_other_ref, w_other, done.at[1]),
    ]
    for fetch in fetches:
        fetch.start()
    rows = keys.shape[0] // 4
    head_size = keys.shape[1]
    core = place_ref[0]
    query_start = pl.multiple_of(place_ref[1], head_size)
    row_pos = place_ref[2] * rows + lax.broadcasted_iota(jnp.int32, (rows, 1), 0)
    lane = lax.broadcasted_iota(jnp.int32, (1, rows), 1)
    col_pos = jnp.concatenate([place_ref[3 + part] * rows + lane for part in range(4)], axis=1)
    allowed = row_pos >= col_pos
    for part, kv_ref in enumerate(kv_refs):
        keys[part * rows : (part + 1) * rows, :] = kv_ref[0:rows, 0:head_size]
        values[part * rows : (part + 1) * rows, :] = kv_ref[0:rows, head_size:]
        quad_ref[:, part * rows : (part + 1) * rows] = kv_ref[rows:, 0:rows]
    key_block = keys[...]
    value_block = values[...]
    for head in range(heads.shape[1] // head_size):
        query = query_ref[:, pl.ds(query_start + head * head_size, head_size)]
        scores = (
            lax.dot_general(
                query, key_block, (((1,), (1,)), ((), ())), preferred_element_type=jnp.float32
            )
            * scale
        )
        scores = jnp.where(allowed, scores, -1e30)
        weights = jnp.exp(scores - jnp.max(scores, axis=1, keepdims=True))
        probs = (weights / jnp.sum(weights, axis=1, keepdims=True)).astype(jnp.bfloat16)
        heads[:, head * head_size : (head + 1) * head_size] = jnp.dot(
            probs, value_block, preferred_element_type=jnp.float32
        ).astype(jnp.bfloat16)
    for fetch in fetches:
        fetch.wait()
    half = heads.shape[1] // 2
    own = heads[:, pl.ds(pl.multiple_of(core * half, half), half)]
    other = heads[:, pl.ds(pl.multiple_of((1 - core) * half, half), half)]
    total = jnp.dot(own, w_own[...], preferred_element_type=jnp.float32) + jnp.dot(
        other, w_other[...], preferred_element_type=jnp.float32
    )
    for base_ref in base_refs:
        total += base_ref[...].astype(jnp.float32)
    out_ref[...] = total.astype(out_ref.dtype)


def attend(place, queries, kv_parts, bases, w_own, w_other, dtype):
    tokens = queries.shape[0]
    width = w_own.shape[1]
    chip_width = 2 * w_own.shape[0]
    return pl.pallas_call(
        functools.partial(attend_kernel, scale=1.0 / HD**0.5),
        in_specs=[pl.BlockSpec(memory_space=pltpu.SMEM)]
        + [pl.BlockSpec(memory_space=pltpu.VMEM)] * (5 + len(bases))
        + [pl.BlockSpec(memory_space=pl.ANY)] * 2,
        out_specs=[pl.BlockSpec(memory_space=pltpu.VMEM)] * 2,
        out_shape=[
            jax.ShapeDtypeStruct((tokens, width), dtype),
            jax.ShapeDtypeStruct((kv_parts[0].shape[0] - tokens, 4 * tokens), jnp.bfloat16),
        ],
        scratch_shapes=[
            pltpu.VMEM((4 * tokens, HD), jnp.bfloat16),
            pltpu.VMEM((4 * tokens, HD), jnp.bfloat16),
            pltpu.VMEM((tokens, chip_width), jnp.bfloat16),
            pltpu.VMEM(w_own.shape, jnp.bfloat16),
            pltpu.VMEM(w_other.shape, jnp.bfloat16),
            pltpu.SemaphoreType.DMA((2,)),
        ],
        compiler_params=pltpu.CompilerParams(vmem_limit_bytes=60 * MIB),
        cost_estimate=pl.CostEstimate(
            flops=16 * tokens * tokens * chip_width + 2 * tokens * chip_width * width,
            bytes_accessed=4 * w_own.size + 4 * tokens * width,
            transcendentals=4 * tokens * tokens * chip_width // HD,
        ),
    )(place, queries, *kv_parts, *bases, w_own, w_other)


def norm_kernel(own_ref, other_ref, gain_ref, *refs):
    hidden_ref, normed_ref = refs[-2:]
    hidden = (own_ref[...] + other_ref[...].astype(jnp.float32)).astype(jnp.bfloat16)
    hidden_ref[...] = hidden
    wide = hidden.astype(jnp.float32)
    normed_ref[...] = (
        wide
        * lax.rsqrt(jnp.mean(wide * wide, axis=1, keepdims=True) + 1e-06)
        * gain_ref[...].astype(jnp.float32)
    ).astype(jnp.bfloat16)


def add_and_norm(own, other, gain, present):
    return pl.pallas_call(
        norm_kernel,
        in_specs=[pl.BlockSpec(memory_space=pltpu.VMEM)] * 3
        + [pl.BlockSpec(memory_space=pl.ANY)] * len(present),
        out_specs=[pl.BlockSpec(memory_space=pltpu.VMEM)] * 2,
        out_shape=[jax.ShapeDtypeStruct(own.shape, jnp.bfloat16)] * 2,
        compiler_params=pltpu.CompilerParams(vmem_limit_bytes=60 * MIB),
    )(own, other, gain, *present)


def pass_kernel(*refs):
    del refs


def meet(*arrays):
    return pl.pallas_call(
        pass_kernel,
        in_specs=[pl.BlockSpec(memory_space=pl.ANY)] * len(arrays),
        out_specs=[pl.BlockSpec(memory_space=pl.ANY)] * len(arrays),
        out_shape=[jax.ShapeDtypeStruct(array.shape, array.dtype) for array in arrays],
        input_output_aliases={index: index for index in range(len(arrays))},
    )(*arrays)


def pass_kernel(*refs):
    del refs


def meet(*arrays):
    return pl.pallas_call(
        pass_kernel,
        in_specs=[pl.BlockSpec(memory_space=pl.ANY)] * len(arrays),
        out_specs=[pl.BlockSpec(memory_space=pl.ANY)] * len(arrays),
        out_shape=[jax.ShapeDtypeStruct(array.shape, array.dtype) for array in arrays],
        input_output_aliases={index: index for index in range(len(arrays))},
        compiler_params=pltpu.CompilerParams(vmem_limit_bytes=MIB),
    )(*arrays)


def experts_kernel(mine_ref, quad_ref, *refs, cap):
    row_refs, refs = refs[:4], refs[4:]
    w_gate_ref, w_up_ref, w_down_ref, own_ref, across_ref, other_ref, packed = refs
    tokens = row_refs[0].shape[0]
    quad = quad_ref[...].astype(jnp.float32)
    expert = lax.broadcasted_iota(jnp.int32, quad.shape, 0)
    line = jnp.sum(jnp.where(expert == mine_ref[0], quad, 0.0), axis=0, keepdims=True)
    gates = jnp.concatenate(
        [line[:, block * tokens : (block + 1) * tokens] for block in range(4)], axis=0
    )
    named = gates > 0
    before = (
        lax.broadcasted_iota(jnp.int32, (tokens, tokens), 0)
        < lax.broadcasted_iota(jnp.int32, (tokens, tokens), 1)
    ).astype(jnp.bfloat16)
    rank = jnp.dot(
        named.astype(jnp.float32).astype(jnp.bfloat16), before, preferred_element_type=jnp.float32
    )
    slot = jnp.where(named, rank.astype(jnp.int32), -1)
    slots = lax.broadcasted_iota(jnp.int32, (cap, tokens), 0)
    picks = []
    weights = []
    for block in range(4):
        chosen = slots == slot[block : block + 1, :]
        picks.append(jnp.where(chosen, 1.0, 0.0).astype(jnp.bfloat16))
        weights.append(
            jnp.sum(jnp.where(chosen, gates[block : block + 1, :], 0.0), axis=1, keepdims=True)
        )
        packed[block * cap : (block + 1) * cap, :] = jnp.dot(
            picks[block], row_refs[block][...], preferred_element_type=jnp.float32
        ).astype(jnp.bfloat16)
    rows = packed[...]
    gate_proj = jnp.dot(rows, w_gate_ref[...], preferred_element_type=jnp.float32)
    up_proj = jnp.dot(rows, w_up_ref[...], preferred_element_type=jnp.float32)
    inner = (gate_proj / (1.0 + jnp.exp(-gate_proj)) * up_proj).astype(jnp.bfloat16)
    result = jnp.dot(inner, w_down_ref[...], preferred_element_type=jnp.float32)
    targets = (
        own_ref.at[...],
        other_ref.at[0:tokens],
        across_ref.at[...],
        other_ref.at[tokens : 2 * tokens],
    )
    for block in range(4):
        part = (result[block * cap : (block + 1) * cap, :] * weights[block]).astype(jnp.bfloat16)
        targets[block][...] = lax.dot_general(
            picks[block], part, (((0,), (0,)), ((), ())), preferred_element_type=jnp.float32
        ).astype(jnp.bfloat16)


def experts_on_rows(mine, quad, row_blocks, w_gate, w_up, w_down, cap):
    tokens, width = row_blocks[0].shape
    hidden_units = w_gate.shape[1]
    return pl.pallas_call(
        functools.partial(experts_kernel, cap=cap),
        in_specs=[pl.BlockSpec(memory_space=pltpu.SMEM)]
        + [pl.BlockSpec(memory_space=pltpu.VMEM)] * 8,
        out_specs=[pl.BlockSpec(memory_space=pltpu.VMEM)] * 3,
        out_shape=[
            jax.ShapeDtypeStruct((tokens, width), jnp.bfloat16),
            jax.ShapeDtypeStruct((tokens, width), jnp.bfloat16),
            jax.ShapeDtypeStruct((2 * tokens, width), jnp.bfloat16),
        ],
        scratch_shapes=[pltpu.VMEM((4 * cap, width), jnp.bfloat16)],
        compiler_params=pltpu.CompilerParams(vmem_limit_bytes=28 * MIB),
        cost_estimate=pl.CostEstimate(
            flops=24 * cap * width * hidden_units,
            bytes_accessed=16 * tokens * width + 6 * width * hidden_units,
            transcendentals=4 * cap * hidden_units,
        ),
    )(mine.reshape(1), quad, *row_blocks, w_gate, w_up, w_down)


def gathered_plan(
    query_rows,
    key_rows,
    value_rows,
    residual_in,
    out_proj,
    norm_gain,
    expert_ids,
    gate_weights,
    expert_gate,
    expert_up,
    expert_down,
    cap,
):
    n_seq = lax.axis_size("seq")
    n_sub = lax.axis_size("sub")
    experts = n_seq * n_sub
    place = lax.axis_index("seq")
    core = place % 2
    chip = place // 2
    twin = [(index, index ^ 1) for index in range(n_seq)]
    across = [(index, (index + 2) % n_seq) for index in range(n_seq)]
    diagonal = [(index, (index ^ 1) ^ 2) for index in range(n_seq)]
    order = [0] + list(range(1, n_sub, 2)) + list(reversed(range(2, n_sub, 2)))

    def ring(steps):
        return [(order[at], order[(at + steps) % n_sub]) for at in range(n_sub)]

    queries = query_rows[0]
    chip_width = queries.shape[1] // 2

    tokens = queries.shape[0]
    queries_away, kv_here, kv_away = pack(
        chip,
        queries,
        key_rows[0],
        value_rows[0],
        expert_ids[0].T,
        gate_weights[0].T,
        experts,
    )
    incoming = lax.ppermute(queries_away, "seq", across)
    kv_parts = [
        kv_here,
        lax.ppermute(kv_here, "seq", twin),
        lax.ppermute(kv_away, "seq", across),
        lax.ppermute(kv_away, "seq", diagonal),
    ]
    w_other = lax.ppermute(out_proj, "seq", twin)
    columns = [place, place ^ 1, place ^ 2, place ^ 3]

    def place_of(query_start, row_block):
        return jnp.stack([core, query_start, row_block] + columns).astype(jnp.int32)

    sent, quad = attend(
        place_of(0 * place, place ^ 2), incoming, kv_parts, [], out_proj, w_other, jnp.bfloat16
    )
    projected_across = lax.ppermute(sent, "seq", across)
    projected, _ = attend(
        place_of(chip * chip_width, place),
        queries,
        kv_parts,
        [residual_in[0]],
        out_proj,
        w_other,
        jnp.float32,
    )
    quads = [lax.ppermute(quad, "sub", ring(steps)) for steps in range(1, n_sub)]
    hidden, normed = add_and_norm(projected, projected_across, norm_gain[None], quads)

    last = n_sub - 1
    mine = place * n_sub + lax.axis_index("sub")

    held = {("row", 0): normed, ("quad", 0): quad}
    held.update({("quad", steps): moved for steps, moved in enumerate(quads, 1)})
    ways = {"across": ("seq", across), "twin": ("seq", twin), "on": ("sub", ring(1))}

    def move(array, way):
        return lax.ppermute(array, *ways[way])

    def experts_of(step):
        held["own", step], held["part", step], other = experts_on_rows(
            mine,
            held["quad", step],
            [held[name, step] for name in ("row", "twin", "across", "diagonal")],
            expert_gate[0],
            expert_up[0],
            expert_down[0],
            cap,
        )
        return other

    def twin_sum(step):
        met = move(held["other", step], "twin")
        held["met", step] = met[:tokens]
        return (held["part", step].astype(jnp.float32) + met[tokens:].astype(jnp.float32)).astype(
            jnp.bfloat16
        )

    def sum_of(step, more):
        parts = [held["own", step], held["met", step], held["back", step]] + more
        return sum(part.astype(jnp.float32) for part in parts)

    for turn in range(1, n_sub + 5):
        now = {}
        step = turn - 1
        if step <= last:
            now["across", step] = move(held["row", step], "across")
            if step < last:
                now["row", step + 1] = move(held["row", step], "on")
            held["twin", step] = move(held["row", step], "twin")
        step = turn - 4 if turn < n_sub + 4 else 0
        if 1 <= step <= last or turn == n_sub + 4:
            now["back", step] = move(held["away", step], "across")
        step = turn - 5
        if 1 <= step <= last:
            more = [held["sum", step - 1]] if step > 1 else []
            now["sum", step] = move(sum_of(step, more).astype(jnp.bfloat16), "on")
        step = turn - 2
        if 0 <= step <= last:
            held["diagonal", step] = move(held["across", step], "twin")
        if 1 <= step <= last:
            now["other", step] = experts_of(step)
        if turn == n_sub + 2:
            now["other", 0] = experts_of(0)
        step = turn - 3 if turn < n_sub + 3 else 0
        if 1 <= step <= last or turn == n_sub + 3:
            now["away", step] = twin_sum(step)
        if turn < n_sub + 4:
            now = dict(zip(now.keys(), meet(*now.values())))
        held.update(now)
    total = hidden.astype(jnp.float32) + sum_of(0, [held["sum", last]])
    return total.astype(jnp.bfloat16)[None]


def per_device(
    query_rows,
    key_rows,
    value_rows,
    residual_in,
    out_proj,
    norm_gain,
    expert_ids,
    gate_weights,
    expert_gate,
    expert_up,
    expert_down,
):
    tokens = query_rows.shape[1]
    n_seq = lax.axis_size("seq")
    n_sub = lax.axis_size("sub")
    experts = n_seq * n_sub
    topk = expert_ids.shape[2]
    cap = max(2, (5 * tokens * topk + 4 * experts - 1) // (4 * experts))
    if n_seq == 2 * KVH and KVH == 2 and tokens == HD and n_sub > 2 and experts <= 2 * topk and cap % 16 == 0:
        return gathered_plan(
            query_rows,
            key_rows,
            value_rows,
            residual_in,
            out_proj,
            norm_gain,
            expert_ids,
            gate_weights,
            expert_gate,
            expert_up,
            expert_down,
            cap,
        )
    heads_here = QH // n_seq
    group = QH // KVH
    query_local = lax.all_to_all(query_rows, "seq", split_axis=2, concat_axis=1, tiled=True)
    key_full, value_full = (
        lax.all_gather(key_rows, "seq", axis=1, tiled=True),
        lax.all_gather(value_rows, "seq", axis=1, tiled=True),
    )
    first_head = lax.axis_index("seq") * heads_here
    key_list = []
    value_list = []
    for head in range(heads_here):
        kv_start = (first_head + head) // group * HD
        key_list.append(lax.dynamic_slice_in_dim(key_full[0], kv_start, HD, 1))
        value_list.append(lax.dynamic_slice_in_dim(value_full[0], kv_start, HD, 1))
    length = query_local.shape[1]
    block = min(length, max(512, length // 8))
    outputs = [
        attend_head(
            query_local[0, :, head * HD : (head + 1) * HD], key_list[head], value_list[head], block
        )
        for head in range(heads_here)
    ]
    head_block = jnp.concatenate(outputs, axis=1)[None]
    attended = lax.all_to_all(head_block, "seq", split_axis=1, concat_axis=2, tiled=True)[0]
    projected = jnp.dot(
        attended,
        lax.all_gather(out_proj, "seq", axis=0, tiled=True),
        preferred_element_type=jnp.float32,
    )
    hidden = (residual_in[0].astype(jnp.float32) + projected).astype(jnp.bfloat16)
    wide = hidden.astype(jnp.float32)
    normed = (
        wide
        * lax.rsqrt(jnp.mean(wide * wide, axis=1, keepdims=True) + 1e-06)
        * norm_gain.astype(jnp.float32)
    ).astype(jnp.bfloat16)
    flat_ids = expert_ids[0].reshape(-1)
    items = flat_ids.shape[0]
    ranks = rank_in_expert(flat_ids, experts)
    slot_of = flat_ids * cap + ranks
    slots_out = experts * cap
    item_of_slot = (
        jnp.full((slots_out,), items, jnp.int32).at[slot_of].set(jnp.arange(items, dtype=jnp.int32))
    )
    padded_rows = jnp.concatenate([normed, jnp.zeros((1, D), jnp.bfloat16)], axis=0)
    padded_gates = jnp.concatenate(
        [gate_weights[0].reshape(-1), jnp.zeros((1,), jnp.bfloat16)], axis=0
    )
    token_of_slot = jnp.where(item_of_slot < items, item_of_slot // topk, tokens)
    send_rows = padded_rows[token_of_slot].reshape(experts, cap, D)
    send_gates = padded_gates[item_of_slot].reshape(experts, cap)
    recv_rows, recv_gates = (
        lax.all_to_all(send_rows, ("seq", "sub"), split_axis=0, concat_axis=0, tiled=True),
        lax.all_to_all(send_gates, ("seq", "sub"), split_axis=0, concat_axis=0, tiled=True),
    )
    slots_in = experts * cap
    valid = recv_gates > 0
    counts = jnp.sum(valid.astype(jnp.int32), axis=1)
    offsets = jnp.cumsum(counts) - counts
    dest = jnp.where(
        valid, offsets[:, None] + jnp.arange(cap, dtype=jnp.int32)[None, :], slots_in
    ).reshape(-1)
    source_of = (
        jnp.full((slots_in + 1,), slots_in, jnp.int32)
        .at[dest]
        .set(jnp.arange(slots_in, dtype=jnp.int32))[:slots_in]
    )
    compact_rows = jnp.concatenate(
        [recv_rows.reshape(slots_in, D), jnp.zeros((1, D), jnp.bfloat16)], axis=0
    )[source_of]
    compact_gates = jnp.concatenate(
        [recv_gates.reshape(-1), jnp.zeros((1,), jnp.bfloat16)], axis=0
    )[source_of].astype(jnp.float32)
    filled = jnp.sum(counts)
    n_blocks = (filled + slots_in - 1) // slots_in
    w_gate = expert_gate[0]
    w_up = expert_up[0]
    w_down = expert_down[0]

    def expert_block(index, results):
        gate_proj = jnp.dot(compact_rows, w_gate, preferred_element_type=jnp.float32)
        up_proj = jnp.dot(compact_rows, w_up, preferred_element_type=jnp.float32)
        inner = (jax.nn.silu(gate_proj) * up_proj).astype(jnp.bfloat16)
        weighted = (
            jnp.dot(inner, w_down, preferred_element_type=jnp.float32) * compact_gates[:, None]
        )
        return weighted.astype(jnp.bfloat16)

    results = lax.fori_loop(0, n_blocks, expert_block, jnp.zeros((slots_in, D), jnp.bfloat16))
    returned = jnp.concatenate([results, jnp.zeros((1, D), jnp.bfloat16)], axis=0)[dest].reshape(
        experts, cap, D
    )
    back = lax.all_to_all(
        returned, ("seq", "sub"), split_axis=0, concat_axis=0, tiled=True
    ).reshape(slots_out, D)
    gathered = back[slot_of].reshape(tokens, topk, D).astype(jnp.float32)
    mixture = jnp.sum(gathered, axis=1)
    return (wide + mixture).astype(jnp.bfloat16)[None]


def solution(mesh):
    placed = (
        P(("grp", "sub"), "seq", None),
        P(("grp", "sub"), "seq", None),
        P(("grp", "sub"), "seq", None),
        P(("grp", "sub"), "seq", None),
        P("seq", None),
        P(),
        P(("grp", "sub"), "seq", None),
        P(("grp", "sub"), "seq", None),
        P(("seq", "sub"), None, None),
        P(("seq", "sub"), None, None),
        P(("seq", "sub"), None, None),
    )
    return jax.shard_map(
        per_device,
        mesh=mesh,
        in_specs=placed,
        out_specs=P(("grp", "sub"), "seq", None),
        check_vma=False,
    )
```

```python
import functools

import jax
import jax.numpy as jnp
from jax import lax
from jax.experimental import pallas as pl
from jax.experimental.pallas import tpu as pltpu
from jax.sharding import PartitionSpec as P

D = 2048
HD = 128
QH = 16
KVH = 2
MIB = 1024 * 1024


def attend_head(queries, keys_one, values_one, block):
    length = queries.shape[0]
    scale = 1.0 / queries.shape[1] ** 0.5
    pieces = []
    for part_index in range(length // block):
        stop = (part_index + 1) * block
        rows_here = queries[part_index * block : stop]
        scores = (
            jnp.einsum("qd,kd->qk", rows_here, keys_one[:stop], preferred_element_type=jnp.float32)
            * scale
        )
        row_pos = part_index * block + jnp.arange(block, dtype=jnp.int32)
        col_pos = jnp.arange(stop, dtype=jnp.int32)
        scores = jnp.where(row_pos[:, None] >= col_pos[None, :], scores, -1e30)
        peak = jnp.max(scores, axis=1, keepdims=True)
        weights = jnp.exp(scores - peak)
        probs = (weights / jnp.sum(weights, axis=1, keepdims=True)).astype(jnp.bfloat16)
        pieces.append(
            jnp.dot(probs, values_one[:stop], preferred_element_type=jnp.float32).astype(
                jnp.bfloat16
            )
        )
    return jnp.concatenate(pieces, axis=0)


def rank_in_expert(flat_ids, experts):
    items = flat_ids.shape[0]
    width = 128
    n_parts = items // width
    onehot = (
        (flat_ids[:, None] == jnp.arange(experts, dtype=jnp.int32)[None, :])
        .astype(jnp.bfloat16)
        .reshape(n_parts, width, experts)
    )
    lower = (
        jnp.arange(width, dtype=jnp.int32)[:, None] > jnp.arange(width, dtype=jnp.int32)[None, :]
    ).astype(jnp.bfloat16)
    within = jnp.einsum("ij,bje->bie", lower, onehot, preferred_element_type=jnp.float32)
    part_counts = jnp.sum(onehot.astype(jnp.float32), axis=1)
    earlier = jnp.cumsum(part_counts, axis=0) - part_counts
    ranks = jnp.sum((within + earlier[:, None, :]) * onehot.astype(jnp.float32), axis=2)
    return ranks.reshape(items).astype(jnp.int32)


def pack_kernel(chip_ref, query_ref, key_ref, value_ref, id_ref, gate_ref, away_ref, here_kv_ref, away_kv_ref):
    tokens = query_ref.shape[0]
    head_size = key_ref.shape[1] // 2
    chip_width = away_ref.shape[1]
    chip = chip_ref[0]
    experts = here_kv_ref.shape[0] - tokens
    away_ref[...] = query_ref[:, pl.ds(pl.multiple_of((1 - chip) * chip_width, chip_width), chip_width)]
    number = lax.broadcasted_iota(jnp.int32, (experts, tokens), 0)
    table = jnp.zeros((experts, tokens), jnp.float32)
    for choice in range(id_ref.shape[0]):
        table += jnp.where(
            number == id_ref[choice : choice + 1, :],
            gate_ref[choice : choice + 1, :].astype(jnp.float32),
            0.0,
        )
    for out_ref, head in ((here_kv_ref, chip), (away_kv_ref, 1 - chip)):
        columns = pl.ds(pl.multiple_of(head * head_size, head_size), head_size)
        out_ref[0:tokens, 0:head_size] = key_ref[:, columns]
        out_ref[0:tokens, head_size:] = value_ref[:, columns]
        out_ref[tokens:, 0:head_size] = table.astype(jnp.bfloat16)
        out_ref[tokens:, head_size:] = jnp.zeros((experts, head_size), jnp.bfloat16)


def pack(chip, queries, keys, values, ids, gates, experts):
    tokens, width = queries.shape
    kv = jax.ShapeDtypeStruct((tokens + experts, keys.shape[1]), jnp.bfloat16)
    return pl.pallas_call(
        pack_kernel,
        in_specs=[pl.BlockSpec(memory_space=pltpu.SMEM)]
        + [pl.BlockSpec(memory_space=pltpu.VMEM)] * 5,
        out_specs=[pl.BlockSpec(memory_space=pltpu.VMEM)] * 3,
        out_shape=[jax.ShapeDtypeStruct((tokens, width // 2), jnp.bfloat16), kv, kv],
        compiler_params=pltpu.CompilerParams(vmem_limit_bytes=60 * MIB),
    )(chip.reshape(1), queries, keys, values, ids, gates)


def attend_kernel(place_ref, query_ref, *refs, scale):
    kv_refs, refs = refs[:4], refs[4:]
    base_refs = refs[: len(refs) - 10]
    w_own_ref, w_other_ref, out_ref, quad_ref, keys, values, heads, w_own, w_other, done = refs[-10:]
    fetches = [
        pltpu.make_async_copy(w_own_ref, w_own, done.at[0]),
        pltpu.make_async_copy(w_other_ref, w_other, done.at[1]),
    ]
    for fetch in fetches:
        fetch.start()
    rows = keys.shape[0] // 4
    head_size = keys.shape[1]
    core = place_ref[0]
    query_start = pl.multiple_of(place_ref[1], head_size)
    row_pos = place_ref[2] * rows + lax.broadcasted_iota(jnp.int32, (rows, 1), 0)
    lane = lax.broadcasted_iota(jnp.int32, (1, rows), 1)
    col_pos = jnp.concatenate([place_ref[3 + part] * rows + lane for part in range(4)], axis=1)
    allowed = row_pos >= col_pos
    for part, kv_ref in enumerate(kv_refs):
        keys[part * rows : (part + 1) * rows, :] = kv_ref[0:rows, 0:head_size]
        values[part * rows : (part + 1) * rows, :] = kv_ref[0:rows, head_size:]
        quad_ref[:, part * rows : (part + 1) * rows] = kv_ref[rows:, 0:rows]
    key_block = keys[...]
    value_block = values[...]
    for head in range(heads.shape[1] // head_size):
        query = query_ref[:, pl.ds(query_start + head * head_size, head_size)]
        scores = (
            lax.dot_general(
                query, key_block, (((1,), (1,)), ((), ())), preferred_element_type=jnp.float32
            )
            * scale
        )
        scores = jnp.where(allowed, scores, -1e30)
        weights = jnp.exp(scores - jnp.max(scores, axis=1, keepdims=True))
        probs = (weights / jnp.sum(weights, axis=1, keepdims=True)).astype(jnp.bfloat16)
        heads[:, head * head_size : (head + 1) * head_size] = jnp.dot(
            probs, value_block, preferred_element_type=jnp.float32
        ).astype(jnp.bfloat16)
    for fetch in fetches:
        fetch.wait()
    half = heads.shape[1] // 2
    own = heads[:, pl.ds(pl.multiple_of(core * half, half), half)]
    other = heads[:, pl.ds(pl.multiple_of((1 - core) * half, half), half)]
    total = jnp.dot(own, w_own[...], preferred_element_type=jnp.float32) + jnp.dot(
        other, w_other[...], preferred_element_type=jnp.float32
    )
    for base_ref in base_refs:
        total += base_ref[...].astype(jnp.float32)
    out_ref[...] = total.astype(out_ref.dtype)


def attend(place, queries, kv_parts, bases, w_own, w_other, dtype):
    tokens = queries.shape[0]
    width = w_own.shape[1]
    chip_width = 2 * w_own.shape[0]
    return pl.pallas_call(
        functools.partial(attend_kernel, scale=1.0 / HD**0.5),
        in_specs=[pl.BlockSpec(memory_space=pltpu.SMEM)]
        + [pl.BlockSpec(memory_space=pltpu.VMEM)] * (5 + len(bases))
        + [pl.BlockSpec(memory_space=pl.ANY)] * 2,
        out_specs=[pl.BlockSpec(memory_space=pltpu.VMEM)] * 2,
        out_shape=[
            jax.ShapeDtypeStruct((tokens, width), dtype),
            jax.ShapeDtypeStruct((kv_parts[0].shape[0] - tokens, 4 * tokens), jnp.bfloat16),
        ],
        scratch_shapes=[
            pltpu.VMEM((4 * tokens, HD), jnp.bfloat16),
            pltpu.VMEM((4 * tokens, HD), jnp.bfloat16),
            pltpu.VMEM((tokens, chip_width), jnp.bfloat16),
            pltpu.VMEM(w_own.shape, jnp.bfloat16),
            pltpu.VMEM(w_other.shape, jnp.bfloat16),
            pltpu.SemaphoreType.DMA((2,)),
        ],
        compiler_params=pltpu.CompilerParams(vmem_limit_bytes=60 * MIB),
        cost_estimate=pl.CostEstimate(
            flops=16 * tokens * tokens * chip_width + 2 * tokens * chip_width * width,
            bytes_accessed=4 * w_own.size + 4 * tokens * width,
            transcendentals=4 * tokens * tokens * chip_width // HD,
        ),
    )(place, queries, *kv_parts, *bases, w_own, w_other)


def norm_kernel(own_ref, other_ref, gain_ref, hidden_ref, normed_ref):
    hidden = (own_ref[...] + other_ref[...].astype(jnp.float32)).astype(jnp.bfloat16)
    hidden_ref[...] = hidden
    wide = hidden.astype(jnp.float32)
    normed_ref[...] = (
        wide
        * lax.rsqrt(jnp.mean(wide * wide, axis=1, keepdims=True) + 1e-06)
        * gain_ref[...].astype(jnp.float32)
    ).astype(jnp.bfloat16)


def add_and_norm(own, other, gain):
    tokens, width = own.shape
    rows = tokens // 4
    block = pl.BlockSpec((rows, width), lambda step: (step, 0))
    return pl.pallas_call(
        norm_kernel,
        grid=(4,),
        in_specs=[block, block, pl.BlockSpec((1, width), lambda step: (0, 0))],
        out_specs=[block, block],
        out_shape=[jax.ShapeDtypeStruct(own.shape, jnp.bfloat16)] * 2,
        compiler_params=pltpu.CompilerParams(vmem_limit_bytes=60 * MIB),
    )(own, other, gain)


def pass_kernel(*refs):
    del refs


def meet(*arrays):
    return pl.pallas_call(
        pass_kernel,
        in_specs=[pl.BlockSpec(memory_space=pl.ANY)] * len(arrays),
        out_specs=[pl.BlockSpec(memory_space=pl.ANY)] * len(arrays),
        out_shape=[jax.ShapeDtypeStruct(array.shape, array.dtype) for array in arrays],
        input_output_aliases={index: index for index in range(len(arrays))},
    )(*arrays)


def pass_kernel(*refs):
    del refs


def meet(*arrays):
    return pl.pallas_call(
        pass_kernel,
        in_specs=[pl.BlockSpec(memory_space=pl.ANY)] * len(arrays),
        out_specs=[pl.BlockSpec(memory_space=pl.ANY)] * len(arrays),
        out_shape=[jax.ShapeDtypeStruct(array.shape, array.dtype) for array in arrays],
        input_output_aliases={index: index for index in range(len(arrays))},
        compiler_params=pltpu.CompilerParams(vmem_limit_bytes=MIB),
    )(*arrays)


def experts_kernel(mine_ref, quad_ref, *refs, cap, pieces):
    row_refs = []
    for count in pieces:
        row_refs.append(refs[:count])
        refs = refs[count:]
    w_gate_ref, w_up_ref, w_down_ref, own_ref, across_ref, other_ref, packed = refs
    tokens = row_refs[0][0].shape[0]
    quad = quad_ref[...].astype(jnp.float32)
    expert = lax.broadcasted_iota(jnp.int32, quad.shape, 0)
    line = jnp.sum(jnp.where(expert == mine_ref[0], quad, 0.0), axis=0, keepdims=True)
    gates = jnp.concatenate(
        [line[:, block * tokens : (block + 1) * tokens] for block in range(4)], axis=0
    )
    named = gates > 0
    before = (
        lax.broadcasted_iota(jnp.int32, (tokens, tokens), 0)
        < lax.broadcasted_iota(jnp.int32, (tokens, tokens), 1)
    ).astype(jnp.bfloat16)
    rank = jnp.dot(
        named.astype(jnp.float32).astype(jnp.bfloat16), before, preferred_element_type=jnp.float32
    )
    slot = jnp.where(named, rank.astype(jnp.int32), -1)
    slots = lax.broadcasted_iota(jnp.int32, (cap, tokens), 0)
    picks = []
    weights = []
    for block in range(4):
        chosen = slots == slot[block : block + 1, :]
        picks.append(jnp.where(chosen, 1.0, 0.0).astype(jnp.bfloat16))
        weights.append(
            jnp.sum(jnp.where(chosen, gates[block : block + 1, :], 0.0), axis=1, keepdims=True)
        )
        start = 0
        for row_ref in row_refs[block]:
            stop = start + row_ref.shape[1]
            packed[block * cap : (block + 1) * cap, start:stop] = jnp.dot(
                picks[block], row_ref[...], preferred_element_type=jnp.float32
            ).astype(jnp.bfloat16)
            start = stop
    rows = packed[...]
    gate_proj = jnp.dot(rows, w_gate_ref[...], preferred_element_type=jnp.float32)
    up_proj = jnp.dot(rows, w_up_ref[...], preferred_element_type=jnp.float32)
    inner = (gate_proj / (1.0 + jnp.exp(-gate_proj)) * up_proj).astype(jnp.bfloat16)
    result = jnp.dot(inner, w_down_ref[...], preferred_element_type=jnp.float32)
    targets = (
        own_ref.at[...],
        other_ref.at[0:tokens],
        across_ref.at[...],
        other_ref.at[tokens : 2 * tokens],
    )
    for block in range(4):
        part = (result[block * cap : (block + 1) * cap, :] * weights[block]).astype(jnp.bfloat16)
        targets[block][...] = lax.dot_general(
            picks[block], part, (((0,), (0,)), ((), ())), preferred_element_type=jnp.float32
        ).astype(jnp.bfloat16)


def experts_on_rows(mine, quad, row_blocks, w_gate, w_up, w_down, cap):
    tokens = row_blocks[0][0].shape[0]
    width, hidden_units = w_gate.shape
    pieces = tuple(len(block) for block in row_blocks)
    return pl.pallas_call(
        functools.partial(experts_kernel, cap=cap, pieces=pieces),
        in_specs=[pl.BlockSpec(memory_space=pltpu.SMEM)]
        + [pl.BlockSpec(memory_space=pltpu.VMEM)] * (4 + sum(pieces)),
        out_specs=[pl.BlockSpec(memory_space=pltpu.VMEM)] * 3,
        out_shape=[
            jax.ShapeDtypeStruct((tokens, width), jnp.bfloat16),
            jax.ShapeDtypeStruct((tokens, width), jnp.bfloat16),
            jax.ShapeDtypeStruct((2 * tokens, width), jnp.bfloat16),
        ],
        scratch_shapes=[pltpu.VMEM((4 * cap, width), jnp.bfloat16)],
        compiler_params=pltpu.CompilerParams(vmem_limit_bytes=28 * MIB),
        cost_estimate=pl.CostEstimate(
            flops=24 * cap * width * hidden_units,
            bytes_accessed=16 * tokens * width + 6 * width * hidden_units,
            transcendentals=4 * cap * hidden_units,
        ),
    )(mine.reshape(1), quad, *sum(row_blocks, []), w_gate, w_up, w_down)


def gathered_plan(
    query_rows,
    key_rows,
    value_rows,
    residual_in,
    out_proj,
    norm_gain,
    expert_ids,
    gate_weights,
    expert_gate,
    expert_up,
    expert_down,
    cap,
):
    n_seq = lax.axis_size("seq")
    n_sub = lax.axis_size("sub")
    experts = n_seq * n_sub
    place = lax.axis_index("seq")
    core = place % 2
    chip = place // 2
    twin = [(index, index ^ 1) for index in range(n_seq)]
    across = [(index, (index + 2) % n_seq) for index in range(n_seq)]
    diagonal = [(index, (index ^ 1) ^ 2) for index in range(n_seq)]
    order = [0] + list(range(1, n_sub, 2)) + list(reversed(range(2, n_sub, 2)))

    def ring(steps):
        return [(order[at], order[(at + steps) % n_sub]) for at in range(n_sub)]

    queries = query_rows[0]
    chip_width = queries.shape[1] // 2

    tokens = queries.shape[0]
    queries_away, kv_here, kv_away = pack(
        chip,
        queries,
        key_rows[0],
        value_rows[0],
        expert_ids[0].T,
        gate_weights[0].T,
        experts,
    )
    incoming = lax.ppermute(queries_away, "seq", across)
    kv_parts = [
        kv_here,
        lax.ppermute(kv_here, "seq", twin),
        lax.ppermute(kv_away, "seq", across),
        lax.ppermute(kv_away, "seq", diagonal),
    ]
    w_other = lax.ppermute(out_proj, "seq", twin)
    columns = [place, place ^ 1, place ^ 2, place ^ 3]

    def place_of(query_start, row_block):
        return jnp.stack([core, query_start, row_block] + columns).astype(jnp.int32)

    sent, quad = attend(
        place_of(0 * place, place ^ 2), incoming, kv_parts, [], out_proj, w_other, jnp.bfloat16
    )
    projected_across = lax.ppermute(sent, "seq", across)
    projected, _ = attend(
        place_of(chip * chip_width, place),
        queries,
        kv_parts,
        [residual_in[0]],
        out_proj,
        w_other,
        jnp.float32,
    )
    hidden, normed = add_and_norm(projected, projected_across, norm_gain[None])

    last = n_sub - 1
    mine = place * n_sub + lax.axis_index("sub")

    held = {("row", 0): normed, ("quad", 0): quad}
    half = normed.shape[1] // 2
    ways = {"across": ("seq", across), "twin": ("seq", twin), "on": ("sub", ring(1))}

    def move(array, way):
        return lax.ppermute(array, *ways[way])

    def experts_of(step):
        held["own", step], held["part", step], other = experts_on_rows(
            mine,
            held["quad", step],
            [
                [held[name, step]] if (name, step) in held else list(held[name, step, "pieces"])
                for name in ("row", "twin", "across", "diagonal")
            ],
            expert_gate[0],
            expert_up[0],
            expert_down[0],
            cap,
        )
        return other

    def twin_sum(step):
        met = move(held["other", step], "twin")
        held["met", step] = met[:tokens]
        return (held["part", step].astype(jnp.float32) + met[tokens:].astype(jnp.float32)).astype(
            jnp.bfloat16
        )

    def sum_of(step, more):
        parts = [held["own", step], held["met", step], held["back", step]] + more
        return sum(part.astype(jnp.float32) for part in parts)

    for turn in range(1, n_sub + 5):
        now = {}
        step = turn - 1
        if step < last:
            now["across", step] = move(held["row", step], "across")
            now["row", step + 1] = move(held["row", step], "on")
            now["quad", step + 1] = move(held["quad", step], "on")
        if step == last:
            now["half", 0] = move(held["row", step][:, :half], "across")
            now["half", 1] = move(held["across", step - 1][:, half:], "on")
        if step <= last:
            held["twin", step] = move(held["row", step], "twin")
        step = turn - 4 if turn < n_sub + 4 else 0
        if 1 <= step <= last or turn == n_sub + 4:
            now["back", step] = move(held["away", step], "across")
        step = turn - 5
        if 1 <= step <= last:
            more = [held["sum", step - 1]] if step > 1 else []
            now["sum", step] = move(sum_of(step, more).astype(jnp.bfloat16), "on")
        step = turn - 2
        if 0 <= step < last:
            held["diagonal", step] = move(held["across", step], "twin")
        if step == last:
            held["across", step, "pieces"] = [held["half", side] for side in range(2)]
            held["diagonal", step, "pieces"] = [
                move(held["half", side], "twin") for side in range(2)
            ]
        if 1 <= step <= last:
            now["other", step] = experts_of(step)
        if turn == n_sub + 2:
            now["other", 0] = experts_of(0)
        step = turn - 3 if turn < n_sub + 3 else 0
        if 1 <= step <= last or turn == n_sub + 3:
            now["away", step] = twin_sum(step)
        if turn < n_sub + 4:
            now = dict(zip(now.keys(), meet(*now.values())))
        held.update(now)
    total = hidden.astype(jnp.float32) + sum_of(0, [held["sum", last]])
    return total.astype(jnp.bfloat16)[None]


def per_device(
    query_rows,
    key_rows,
    value_rows,
    residual_in,
    out_proj,
    norm_gain,
    expert_ids,
    gate_weights,
    expert_gate,
    expert_up,
    expert_down,
):
    tokens = query_rows.shape[1]
    n_seq = lax.axis_size("seq")
    n_sub = lax.axis_size("sub")
    experts = n_seq * n_sub
    topk = expert_ids.shape[2]
    cap = max(2, (5 * tokens * topk + 4 * experts - 1) // (4 * experts))
    if n_seq == 2 * KVH and KVH == 2 and tokens == HD and n_sub > 2 and experts <= 2 * topk and cap % 16 == 0:
        return gathered_plan(
            query_rows,
            key_rows,
            value_rows,
            residual_in,
            out_proj,
            norm_gain,
            expert_ids,
            gate_weights,
            expert_gate,
            expert_up,
            expert_down,
            cap,
        )
    heads_here = QH // n_seq
    group = QH // KVH
    query_local = lax.all_to_all(query_rows, "seq", split_axis=2, concat_axis=1, tiled=True)
    key_full, value_full = (
        lax.all_gather(key_rows, "seq", axis=1, tiled=True),
        lax.all_gather(value_rows, "seq", axis=1, tiled=True),
    )
    first_head = lax.axis_index("seq") * heads_here
    key_list = []
    value_list = []
    for head in range(heads_here):
        kv_start = (first_head + head) // group * HD
        key_list.append(lax.dynamic_slice_in_dim(key_full[0], kv_start, HD, 1))
        value_list.append(lax.dynamic_slice_in_dim(value_full[0], kv_start, HD, 1))
    length = query_local.shape[1]
    block = min(length, max(512, length // 8))
    outputs = [
        attend_head(
            query_local[0, :, head * HD : (head + 1) * HD], key_list[head], value_list[head], block
        )
        for head in range(heads_here)
    ]
    head_block = jnp.concatenate(outputs, axis=1)[None]
    attended = lax.all_to_all(head_block, "seq", split_axis=1, concat_axis=2, tiled=True)[0]
    projected = jnp.dot(
        attended,
        lax.all_gather(out_proj, "seq", axis=0, tiled=True),
        preferred_element_type=jnp.float32,
    )
    hidden = (residual_in[0].astype(jnp.float32) + projected).astype(jnp.bfloat16)
    wide = hidden.astype(jnp.float32)
    normed = (
        wide
        * lax.rsqrt(jnp.mean(wide * wide, axis=1, keepdims=True) + 1e-06)
        * norm_gain.astype(jnp.float32)
    ).astype(jnp.bfloat16)
    flat_ids = expert_ids[0].reshape(-1)
    items = flat_ids.shape[0]
    ranks = rank_in_expert(flat_ids, experts)
    slot_of = flat_ids * cap + ranks
    slots_out = experts * cap
    item_of_slot = (
        jnp.full((slots_out,), items, jnp.int32).at[slot_of].set(jnp.arange(items, dtype=jnp.int32))
    )
    padded_rows = jnp.concatenate([normed, jnp.zeros((1, D), jnp.bfloat16)], axis=0)
    padded_gates = jnp.concatenate(
        [gate_weights[0].reshape(-1), jnp.zeros((1,), jnp.bfloat16)], axis=0
    )
    token_of_slot = jnp.where(item_of_slot < items, item_of_slot // topk, tokens)
    send_rows = padded_rows[token_of_slot].reshape(experts, cap, D)
    send_gates = padded_gates[item_of_slot].reshape(experts, cap)
    recv_rows, recv_gates = (
        lax.all_to_all(send_rows, ("seq", "sub"), split_axis=0, concat_axis=0, tiled=True),
        lax.all_to_all(send_gates, ("seq", "sub"), split_axis=0, concat_axis=0, tiled=True),
    )
    slots_in = experts * cap
    valid = recv_gates > 0
    counts = jnp.sum(valid.astype(jnp.int32), axis=1)
    offsets = jnp.cumsum(counts) - counts
    dest = jnp.where(
        valid, offsets[:, None] + jnp.arange(cap, dtype=jnp.int32)[None, :], slots_in
    ).reshape(-1)
    source_of = (
        jnp.full((slots_in + 1,), slots_in, jnp.int32)
        .at[dest]
        .set(jnp.arange(slots_in, dtype=jnp.int32))[:slots_in]
    )
    compact_rows = jnp.concatenate(
        [recv_rows.reshape(slots_in, D), jnp.zeros((1, D), jnp.bfloat16)], axis=0
    )[source_of]
    compact_gates = jnp.concatenate(
        [recv_gates.reshape(-1), jnp.zeros((1,), jnp.bfloat16)], axis=0
    )[source_of].astype(jnp.float32)
    filled = jnp.sum(counts)
    n_blocks = (filled + slots_in - 1) // slots_in
    w_gate = expert_gate[0]
    w_up = expert_up[0]
    w_down = expert_down[0]

    def expert_block(index, results):
        gate_proj = jnp.dot(compact_rows, w_gate, preferred_element_type=jnp.float32)
        up_proj = jnp.dot(compact_rows, w_up, preferred_element_type=jnp.float32)
        inner = (jax.nn.silu(gate_proj) * up_proj).astype(jnp.bfloat16)
        weighted = (
            jnp.dot(inner, w_down, preferred_element_type=jnp.float32) * compact_gates[:, None]
        )
        return weighted.astype(jnp.bfloat16)

    results = lax.fori_loop(0, n_blocks, expert_block, jnp.zeros((slots_in, D), jnp.bfloat16))
    returned = jnp.concatenate([results, jnp.zeros((1, D), jnp.bfloat16)], axis=0)[dest].reshape(
        experts, cap, D
    )
    back = lax.all_to_all(
        returned, ("seq", "sub"), split_axis=0, concat_axis=0, tiled=True
    ).reshape(slots_out, D)
    gathered = back[slot_of].reshape(tokens, topk, D).astype(jnp.float32)
    mixture = jnp.sum(gathered, axis=1)
    return (wide + mixture).astype(jnp.bfloat16)[None]


def solution(mesh):
    placed = (
        P(("grp", "sub"), "seq", None),
        P(("grp", "sub"), "seq", None),
        P(("grp", "sub"), "seq", None),
        P(("grp", "sub"), "seq", None),
        P("seq", None),
        P(),
        P(("grp", "sub"), "seq", None),
        P(("grp", "sub"), "seq", None),
        P(("seq", "sub"), None, None),
        P(("seq", "sub"), None, None),
        P(("seq", "sub"), None, None),
    )
    return jax.shard_map(
        per_device,
        mesh=mesh,
        in_specs=placed,
        out_specs=P(("grp", "sub"), "seq", None),
        check_vma=False,
    )
```

```python
import functools

import jax
import jax.numpy as jnp
from jax import lax
from jax.experimental import pallas as pl
from jax.experimental.pallas import tpu as pltpu
from jax.sharding import PartitionSpec as P

D = 2048
HD = 128
QH = 16
KVH = 2
MIB = 1024 * 1024


def attend_head(queries, keys_one, values_one, block):
    length = queries.shape[0]
    scale = 1.0 / queries.shape[1] ** 0.5
    pieces = []
    for part_index in range(length // block):
        stop = (part_index + 1) * block
        rows_here = queries[part_index * block : stop]
        scores = (
            jnp.einsum("qd,kd->qk", rows_here, keys_one[:stop], preferred_element_type=jnp.float32)
            * scale
        )
        row_pos = part_index * block + jnp.arange(block, dtype=jnp.int32)
        col_pos = jnp.arange(stop, dtype=jnp.int32)
        scores = jnp.where(row_pos[:, None] >= col_pos[None, :], scores, -1e30)
        peak = jnp.max(scores, axis=1, keepdims=True)
        weights = jnp.exp(scores - peak)
        probs = (weights / jnp.sum(weights, axis=1, keepdims=True)).astype(jnp.bfloat16)
        pieces.append(
            jnp.dot(probs, values_one[:stop], preferred_element_type=jnp.float32).astype(
                jnp.bfloat16
            )
        )
    return jnp.concatenate(pieces, axis=0)


def rank_in_expert(flat_ids, experts):
    items = flat_ids.shape[0]
    width = 128
    n_parts = items // width
    onehot = (
        (flat_ids[:, None] == jnp.arange(experts, dtype=jnp.int32)[None, :])
        .astype(jnp.bfloat16)
        .reshape(n_parts, width, experts)
    )
    lower = (
        jnp.arange(width, dtype=jnp.int32)[:, None] > jnp.arange(width, dtype=jnp.int32)[None, :]
    ).astype(jnp.bfloat16)
    within = jnp.einsum("ij,bje->bie", lower, onehot, preferred_element_type=jnp.float32)
    part_counts = jnp.sum(onehot.astype(jnp.float32), axis=1)
    earlier = jnp.cumsum(part_counts, axis=0) - part_counts
    ranks = jnp.sum((within + earlier[:, None, :]) * onehot.astype(jnp.float32), axis=2)
    return ranks.reshape(items).astype(jnp.int32)


def pack_kernel(chip_ref, query_ref, key_ref, value_ref, id_ref, gate_ref, away_ref, here_kv_ref, away_kv_ref):
    tokens = query_ref.shape[0]
    head_size = key_ref.shape[1] // 2
    chip_width = away_ref.shape[1]
    chip = chip_ref[0]
    experts = here_kv_ref.shape[0] - tokens
    away_ref[...] = query_ref[:, pl.ds(pl.multiple_of((1 - chip) * chip_width, chip_width), chip_width)]
    number = lax.broadcasted_iota(jnp.int32, (experts, tokens), 0)
    table = jnp.zeros((experts, tokens), jnp.float32)
    for choice in range(id_ref.shape[0]):
        table += jnp.where(
            number == id_ref[choice : choice + 1, :],
            gate_ref[choice : choice + 1, :].astype(jnp.float32),
            0.0,
        )
    for out_ref, head in ((here_kv_ref, chip), (away_kv_ref, 1 - chip)):
        columns = pl.ds(pl.multiple_of(head * head_size, head_size), head_size)
        out_ref[0:tokens, 0:head_size] = key_ref[:, columns]
        out_ref[0:tokens, head_size:] = value_ref[:, columns]
        out_ref[tokens:, 0:head_size] = table.astype(jnp.bfloat16)
        out_ref[tokens:, head_size:] = jnp.zeros((experts, head_size), jnp.bfloat16)


def pack(chip, queries, keys, values, ids, gates, experts):
    tokens, width = queries.shape
    kv = jax.ShapeDtypeStruct((tokens + experts, keys.shape[1]), jnp.bfloat16)
    return pl.pallas_call(
        pack_kernel,
        in_specs=[pl.BlockSpec(memory_space=pltpu.SMEM)]
        + [pl.BlockSpec(memory_space=pltpu.VMEM)] * 5,
        out_specs=[pl.BlockSpec(memory_space=pltpu.VMEM)] * 3,
        out_shape=[jax.ShapeDtypeStruct((tokens, width // 2), jnp.bfloat16), kv, kv],
        compiler_params=pltpu.CompilerParams(vmem_limit_bytes=60 * MIB),
    )(chip.reshape(1), queries, keys, values, ids, gates)


def attend_kernel(place_ref, query_ref, *refs, scale):
    kv_refs, refs = refs[:4], refs[4:]
    base_refs = refs[: len(refs) - 10]
    w_own_ref, w_other_ref, out_ref, quad_ref, keys, values, heads, w_own, w_other, done = refs[-10:]
    fetches = [
        pltpu.make_async_copy(w_own_ref, w_own, done.at[0]),
        pltpu.make_async_copy(w_other_ref, w_other, done.at[1]),
    ]
    for fetch in fetches:
        fetch.start()
    rows = keys.shape[0] // 4
    head_size = keys.shape[1]
    core = place_ref[0]
    query_start = pl.multiple_of(place_ref[1], head_size)
    row_pos = place_ref[2] * rows + lax.broadcasted_iota(jnp.int32, (rows, 1), 0)
    lane = lax.broadcasted_iota(jnp.int32, (1, rows), 1)
    col_pos = jnp.concatenate([place_ref[3 + part] * rows + lane for part in range(4)], axis=1)
    allowed = row_pos >= col_pos
    for part, kv_ref in enumerate(kv_refs):
        keys[part * rows : (part + 1) * rows, :] = kv_ref[0:rows, 0:head_size]
        values[part * rows : (part + 1) * rows, :] = kv_ref[0:rows, head_size:]
        quad_ref[:, part * rows : (part + 1) * rows] = kv_ref[rows:, 0:rows]
    key_block = keys[...]
    value_block = values[...]
    for head in range(heads.shape[1] // head_size):
        query = query_ref[:, pl.ds(query_start + head * head_size, head_size)]
        scores = (
            lax.dot_general(
                query, key_block, (((1,), (1,)), ((), ())), preferred_element_type=jnp.float32
            )
            * scale
        )
        scores = jnp.where(allowed, scores, -1e30)
        weights = jnp.exp(scores - jnp.max(scores, axis=1, keepdims=True))
        probs = (weights * (1.0 / jnp.sum(weights, axis=1, keepdims=True))).astype(jnp.bfloat16)
        heads[:, head * head_size : (head + 1) * head_size] = jnp.dot(
            probs, value_block, preferred_element_type=jnp.float32
        ).astype(jnp.bfloat16)
    for fetch in fetches:
        fetch.wait()
    half = heads.shape[1] // 2
    own = heads[:, pl.ds(pl.multiple_of(core * half, half), half)]
    other = heads[:, pl.ds(pl.multiple_of((1 - core) * half, half), half)]
    total = jnp.dot(own, w_own[...], preferred_element_type=jnp.float32) + jnp.dot(
        other, w_other[...], preferred_element_type=jnp.float32
    )
    for base_ref in base_refs:
        total += base_ref[...].astype(jnp.float32)
    out_ref[...] = total.astype(out_ref.dtype)


def attend(place, queries, kv_parts, bases, w_own, w_other, dtype):
    tokens = queries.shape[0]
    width = w_own.shape[1]
    chip_width = 2 * w_own.shape[0]
    return pl.pallas_call(
        functools.partial(attend_kernel, scale=1.0 / HD**0.5),
        in_specs=[pl.BlockSpec(memory_space=pltpu.SMEM)]
        + [pl.BlockSpec(memory_space=pltpu.VMEM)] * (5 + len(bases))
        + [pl.BlockSpec(memory_space=pl.ANY)] * 2,
        out_specs=[pl.BlockSpec(memory_space=pltpu.VMEM)] * 2,
        out_shape=[
            jax.ShapeDtypeStruct((tokens, width), dtype),
            jax.ShapeDtypeStruct((kv_parts[0].shape[0] - tokens, 4 * tokens), jnp.bfloat16),
        ],
        scratch_shapes=[
            pltpu.VMEM((4 * tokens, HD), jnp.bfloat16),
            pltpu.VMEM((4 * tokens, HD), jnp.bfloat16),
            pltpu.VMEM((tokens, chip_width), jnp.bfloat16),
            pltpu.VMEM(w_own.shape, jnp.bfloat16),
            pltpu.VMEM(w_other.shape, jnp.bfloat16),
            pltpu.SemaphoreType.DMA((2,)),
        ],
        compiler_params=pltpu.CompilerParams(vmem_limit_bytes=60 * MIB),
        cost_estimate=pl.CostEstimate(
            flops=16 * tokens * tokens * chip_width + 2 * tokens * chip_width * width,
            bytes_accessed=4 * w_own.size + 4 * tokens * width,
            transcendentals=4 * tokens * tokens * chip_width // HD,
        ),
    )(place, queries, *kv_parts, *bases, w_own, w_other)


def norm_kernel(own_ref, other_ref, gain_ref, *refs):
    hidden_ref, normed_ref = refs[-2:]
    hidden = (own_ref[...] + other_ref[...].astype(jnp.float32)).astype(jnp.bfloat16)
    hidden_ref[...] = hidden
    wide = hidden.astype(jnp.float32)
    normed_ref[...] = (
        wide
        * lax.rsqrt(jnp.mean(wide * wide, axis=1, keepdims=True) + 1e-06)
        * gain_ref[...].astype(jnp.float32)
    ).astype(jnp.bfloat16)


def add_and_norm(own, other, gain, present):
    return pl.pallas_call(
        norm_kernel,
        in_specs=[pl.BlockSpec(memory_space=pltpu.VMEM)] * 3
        + [pl.BlockSpec(memory_space=pl.ANY)] * len(present),
        out_specs=[pl.BlockSpec(memory_space=pltpu.VMEM)] * 2,
        out_shape=[jax.ShapeDtypeStruct(own.shape, jnp.bfloat16)] * 2,
        compiler_params=pltpu.CompilerParams(vmem_limit_bytes=60 * MIB),
    )(own, other, gain, *present)


def pass_kernel(*refs):
    del refs


def meet(arrays, present):
    return pl.pallas_call(
        pass_kernel,
        in_specs=[pl.BlockSpec(memory_space=pl.ANY)] * (len(arrays) + len(present)),
        out_specs=[pl.BlockSpec(memory_space=pl.ANY)] * len(arrays),
        out_shape=[jax.ShapeDtypeStruct(array.shape, array.dtype) for array in arrays],
        input_output_aliases={index: index for index in range(len(arrays))},
    )(*arrays)


def pass_kernel(*refs):
    del refs


def meet(arrays, present):
    return pl.pallas_call(
        pass_kernel,
        in_specs=[pl.BlockSpec(memory_space=pl.ANY)] * (len(arrays) + len(present)),
        out_specs=[pl.BlockSpec(memory_space=pl.ANY)] * len(arrays),
        out_shape=[jax.ShapeDtypeStruct(array.shape, array.dtype) for array in arrays],
        input_output_aliases={index: index for index in range(len(arrays))},
        compiler_params=pltpu.CompilerParams(vmem_limit_bytes=MIB),
    )(*arrays, *present)


def experts_kernel(mine_ref, quad_ref, *refs, cap, pieces):
    row_refs = []
    for count in pieces:
        row_refs.append(refs[:count])
        refs = refs[count:]
    w_gate_ref, w_up_ref, w_down_ref, own_ref, across_ref, other_ref, packed = refs
    tokens = row_refs[0][0].shape[0]
    quad = quad_ref[...].astype(jnp.float32)
    expert = lax.broadcasted_iota(jnp.int32, quad.shape, 0)
    line = jnp.sum(jnp.where(expert == mine_ref[0], quad, 0.0), axis=0, keepdims=True)
    gates = jnp.concatenate(
        [line[:, block * tokens : (block + 1) * tokens] for block in range(4)], axis=0
    )
    named = gates > 0
    before = (
        lax.broadcasted_iota(jnp.int32, (tokens, tokens), 0)
        < lax.broadcasted_iota(jnp.int32, (tokens, tokens), 1)
    ).astype(jnp.bfloat16)
    rank = jnp.dot(
        named.astype(jnp.float32).astype(jnp.bfloat16), before, preferred_element_type=jnp.float32
    )
    slot = jnp.where(named, rank.astype(jnp.int32), -1)
    slots = lax.broadcasted_iota(jnp.int32, (cap, tokens), 0)
    picks = []
    weights = []
    for block in range(4):
        chosen = slots == slot[block : block + 1, :]
        picks.append(jnp.where(chosen, 1.0, 0.0).astype(jnp.bfloat16))
        weights.append(
            jnp.sum(jnp.where(chosen, gates[block : block + 1, :], 0.0), axis=1, keepdims=True)
        )
        start = 0
        for row_ref in row_refs[block]:
            stop = start + row_ref.shape[1]
            packed[block * cap : (block + 1) * cap, start:stop] = jnp.dot(
                picks[block], row_ref[...], preferred_element_type=jnp.float32
            ).astype(jnp.bfloat16)
            start = stop
    rows = packed[...]
    gate_proj = jnp.dot(rows, w_gate_ref[...], preferred_element_type=jnp.float32)
    up_proj = jnp.dot(rows, w_up_ref[...], preferred_element_type=jnp.float32)
    inner = (gate_proj / (1.0 + jnp.exp(-gate_proj)) * up_proj).astype(jnp.bfloat16)
    result = jnp.dot(inner, w_down_ref[...], preferred_element_type=jnp.float32)
    targets = (
        own_ref.at[...],
        other_ref.at[0:tokens],
        across_ref.at[...],
        other_ref.at[tokens : 2 * tokens],
    )
    for block in range(4):
        part = (result[block * cap : (block + 1) * cap, :] * weights[block]).astype(jnp.bfloat16)
        targets[block][...] = lax.dot_general(
            picks[block], part, (((0,), (0,)), ((), ())), preferred_element_type=jnp.float32
        ).astype(jnp.bfloat16)


def experts_on_rows(mine, quad, row_blocks, w_gate, w_up, w_down, cap):
    tokens = row_blocks[0][0].shape[0]
    width, hidden_units = w_gate.shape
    pieces = tuple(len(block) for block in row_blocks)
    return pl.pallas_call(
        functools.partial(experts_kernel, cap=cap, pieces=pieces),
        in_specs=[pl.BlockSpec(memory_space=pltpu.SMEM)]
        + [pl.BlockSpec(memory_space=pltpu.VMEM)] * (4 + sum(pieces)),
        out_specs=[pl.BlockSpec(memory_space=pltpu.VMEM)] * 3,
        out_shape=[
            jax.ShapeDtypeStruct((tokens, width), jnp.bfloat16),
            jax.ShapeDtypeStruct((tokens, width), jnp.bfloat16),
            jax.ShapeDtypeStruct((2 * tokens, width), jnp.bfloat16),
        ],
        scratch_shapes=[pltpu.VMEM((4 * cap, width), jnp.bfloat16)],
        compiler_params=pltpu.CompilerParams(vmem_limit_bytes=28 * MIB),
        cost_estimate=pl.CostEstimate(
            flops=24 * cap * width * hidden_units,
            bytes_accessed=16 * tokens * width + 6 * width * hidden_units,
            transcendentals=4 * cap * hidden_units,
        ),
    )(mine.reshape(1), quad, *sum(row_blocks, []), w_gate, w_up, w_down)


def gathered_plan(
    query_rows,
    key_rows,
    value_rows,
    residual_in,
    out_proj,
    norm_gain,
    expert_ids,
    gate_weights,
    expert_gate,
    expert_up,
    expert_down,
    cap,
):
    n_seq = lax.axis_size("seq")
    n_sub = lax.axis_size("sub")
    experts = n_seq * n_sub
    place = lax.axis_index("seq")
    core = place % 2
    chip = place // 2
    twin = [(index, index ^ 1) for index in range(n_seq)]
    across = [(index, (index + 2) % n_seq) for index in range(n_seq)]
    diagonal = [(index, (index ^ 1) ^ 2) for index in range(n_seq)]
    order = [0] + list(range(1, n_sub, 2)) + list(reversed(range(2, n_sub, 2)))

    def ring(steps):
        return [(order[at], order[(at + steps) % n_sub]) for at in range(n_sub)]

    queries = query_rows[0]
    chip_width = queries.shape[1] // 2

    tokens = queries.shape[0]
    queries_away, kv_here, kv_away = pack(
        chip,
        queries,
        key_rows[0],
        value_rows[0],
        expert_ids[0].T,
        gate_weights[0].T,
        experts,
    )
    incoming = lax.ppermute(queries_away, "seq", across)
    kv_parts = [
        kv_here,
        lax.ppermute(kv_here, "seq", twin),
        lax.ppermute(kv_away, "seq", across),
        lax.ppermute(kv_away, "seq", diagonal),
    ]
    w_other = lax.ppermute(out_proj, "seq", twin)
    columns = [place, place ^ 1, place ^ 2, place ^ 3]

    def place_of(query_start, row_block):
        return jnp.stack([core, query_start, row_block] + columns).astype(jnp.int32)

    sent, quad = attend(
        place_of(0 * place, place ^ 2), incoming, kv_parts, [], out_proj, w_other, jnp.bfloat16
    )
    projected_across = lax.ppermute(sent, "seq", across)
    projected, _ = attend(
        place_of(chip * chip_width, place),
        queries,
        kv_parts,
        [residual_in[0]],
        out_proj,
        w_other,
        jnp.float32,
    )
    quads = [lax.ppermute(quad, "sub", ring(steps)) for steps in range(1, n_sub)]
    hidden, normed = add_and_norm(projected, projected_across, norm_gain[None], quads)

    last = n_sub - 1
    mine = place * n_sub + lax.axis_index("sub")

    held = {("row", 0): normed, ("quad", 0): quad}
    held.update({("quad", steps): moved for steps, moved in enumerate(quads, 1)})
    half = normed.shape[1] // 2
    ways = {"across": ("seq", across), "twin": ("seq", twin), "on": ("sub", ring(1))}

    def move(array, way):
        return lax.ppermute(array, *ways[way])

    def experts_of(step):
        held["own", step], held["part", step], other = experts_on_rows(
            mine,
            held["quad", step],
            [
                [held[name, step]] if (name, step) in held else list(held[name, step, "pieces"])
                for name in ("row", "twin", "across", "diagonal")
            ],
            expert_gate[0],
            expert_up[0],
            expert_down[0],
            cap,
        )
        return other

    def twin_sum(step):
        met = move(held["other", step], "twin")
        held["met", step] = met[:tokens]
        return (held["part", step].astype(jnp.float32) + met[tokens:].astype(jnp.float32)).astype(
            jnp.bfloat16
        )

    def sum_of(step, more):
        parts = [held["own", step], held["met", step], held["back", step]] + more
        return sum(part.astype(jnp.float32) for part in parts)

    for turn in range(1, n_sub + 5):
        now = {}
        step = turn - 1
        if step < last:
            now["across", step] = move(held["row", step], "across")
            now["row", step + 1] = move(held["row", step], "on")
        if step == last:
            now["half", 0] = move(held["row", step][:, :half], "across")
            now["half", 1] = move(held["across", step - 1][:, half:], "on")
        if step <= last:
            held["twin", step] = move(held["row", step], "twin")
        step = turn - 4 if turn < n_sub + 4 else 0
        if 1 <= step <= last or turn == n_sub + 4:
            now["back", step] = move(held["away", step], "across")
        step = turn - 5
        if 1 <= step <= last:
            more = [held["sum", step - 1]] if step > 1 else []
            now["sum", step] = move(sum_of(step, more).astype(jnp.bfloat16), "on")
        step = turn - 2
        if 0 <= step < last:
            held["diagonal", step] = move(held["across", step], "twin")
        if step == last:
            held["across", step, "pieces"] = [held["half", side] for side in range(2)]
            held["diagonal", step, "pieces"] = [
                move(held["half", side], "twin") for side in range(2)
            ]
        if 1 <= step <= last:
            now["other", step] = experts_of(step)
        if turn == n_sub + 2:
            now["other", 0] = experts_of(0)
        step = turn - 3 if turn < n_sub + 3 else 0
        if 1 <= step <= last or turn == n_sub + 3:
            now["away", step] = twin_sum(step)
        if turn < n_sub + 4:
            weights = [expert_gate[0], expert_up[0], expert_down[0]] if turn == 1 else []
            now = dict(zip(now.keys(), meet(list(now.values()), weights)))
        held.update(now)
    total = hidden.astype(jnp.float32) + sum_of(0, [held["sum", last]])
    return total.astype(jnp.bfloat16)[None]


def per_device(
    query_rows,
    key_rows,
    value_rows,
    residual_in,
    out_proj,
    norm_gain,
    expert_ids,
    gate_weights,
    expert_gate,
    expert_up,
    expert_down,
):
    tokens = query_rows.shape[1]
    n_seq = lax.axis_size("seq")
    n_sub = lax.axis_size("sub")
    experts = n_seq * n_sub
    topk = expert_ids.shape[2]
    cap = max(2, (5 * tokens * topk + 4 * experts - 1) // (4 * experts))
    if n_seq == 2 * KVH and KVH == 2 and tokens == HD and n_sub > 2 and experts <= 2 * topk and cap % 16 == 0:
        return gathered_plan(
            query_rows,
            key_rows,
            value_rows,
            residual_in,
            out_proj,
            norm_gain,
            expert_ids,
            gate_weights,
            expert_gate,
            expert_up,
            expert_down,
            cap,
        )
    heads_here = QH // n_seq
    group = QH // KVH
    query_local = lax.all_to_all(query_rows, "seq", split_axis=2, concat_axis=1, tiled=True)
    key_full, value_full = (
        lax.all_gather(key_rows, "seq", axis=1, tiled=True),
        lax.all_gather(value_rows, "seq", axis=1, tiled=True),
    )
    first_head = lax.axis_index("seq") * heads_here
    key_list = []
    value_list = []
    for head in range(heads_here):
        kv_start = (first_head + head) // group * HD
        key_list.append(lax.dynamic_slice_in_dim(key_full[0], kv_start, HD, 1))
        value_list.append(lax.dynamic_slice_in_dim(value_full[0], kv_start, HD, 1))
    length = query_local.shape[1]
    block = min(length, max(512, length // 8))
    outputs = [
        attend_head(
            query_local[0, :, head * HD : (head + 1) * HD], key_list[head], value_list[head], block
        )
        for head in range(heads_here)
    ]
    head_block = jnp.concatenate(outputs, axis=1)[None]
    attended = lax.all_to_all(head_block, "seq", split_axis=1, concat_axis=2, tiled=True)[0]
    projected = jnp.dot(
        attended,
        lax.all_gather(out_proj, "seq", axis=0, tiled=True),
        preferred_element_type=jnp.float32,
    )
    hidden = (residual_in[0].astype(jnp.float32) + projected).astype(jnp.bfloat16)
    wide = hidden.astype(jnp.float32)
    normed = (
        wide
        * lax.rsqrt(jnp.mean(wide * wide, axis=1, keepdims=True) + 1e-06)
        * norm_gain.astype(jnp.float32)
    ).astype(jnp.bfloat16)
    flat_ids = expert_ids[0].reshape(-1)
    items = flat_ids.shape[0]
    ranks = rank_in_expert(flat_ids, experts)
    slot_of = flat_ids * cap + ranks
    slots_out = experts * cap
    item_of_slot = (
        jnp.full((slots_out,), items, jnp.int32).at[slot_of].set(jnp.arange(items, dtype=jnp.int32))
    )
    padded_rows = jnp.concatenate([normed, jnp.zeros((1, D), jnp.bfloat16)], axis=0)
    padded_gates = jnp.concatenate(
        [gate_weights[0].reshape(-1), jnp.zeros((1,), jnp.bfloat16)], axis=0
    )
    token_of_slot = jnp.where(item_of_slot < items, item_of_slot // topk, tokens)
    send_rows = padded_rows[token_of_slot].reshape(experts, cap, D)
    send_gates = padded_gates[item_of_slot].reshape(experts, cap)
    recv_rows, recv_gates = (
        lax.all_to_all(send_rows, ("seq", "sub"), split_axis=0, concat_axis=0, tiled=True),
        lax.all_to_all(send_gates, ("seq", "sub"), split_axis=0, concat_axis=0, tiled=True),
    )
    slots_in = experts * cap
    valid = recv_gates > 0
    counts = jnp.sum(valid.astype(jnp.int32), axis=1)
    offsets = jnp.cumsum(counts) - counts
    dest = jnp.where(
        valid, offsets[:, None] + jnp.arange(cap, dtype=jnp.int32)[None, :], slots_in
    ).reshape(-1)
    source_of = (
        jnp.full((slots_in + 1,), slots_in, jnp.int32)
        .at[dest]
        .set(jnp.arange(slots_in, dtype=jnp.int32))[:slots_in]
    )
    compact_rows = jnp.concatenate(
        [recv_rows.reshape(slots_in, D), jnp.zeros((1, D), jnp.bfloat16)], axis=0
    )[source_of]
    compact_gates = jnp.concatenate(
        [recv_gates.reshape(-1), jnp.zeros((1,), jnp.bfloat16)], axis=0
    )[source_of].astype(jnp.float32)
    filled = jnp.sum(counts)
    n_blocks = (filled + slots_in - 1) // slots_in
    w_gate = expert_gate[0]
    w_up = expert_up[0]
    w_down = expert_down[0]

    def expert_block(index, results):
        gate_proj = jnp.dot(compact_rows, w_gate, preferred_element_type=jnp.float32)
        up_proj = jnp.dot(compact_rows, w_up, preferred_element_type=jnp.float32)
        inner = (jax.nn.silu(gate_proj) * up_proj).astype(jnp.bfloat16)
        weighted = (
            jnp.dot(inner, w_down, preferred_element_type=jnp.float32) * compact_gates[:, None]
        )
        return weighted.astype(jnp.bfloat16)

    results = lax.fori_loop(0, n_blocks, expert_block, jnp.zeros((slots_in, D), jnp.bfloat16))
    returned = jnp.concatenate([results, jnp.zeros((1, D), jnp.bfloat16)], axis=0)[dest].reshape(
        experts, cap, D
    )
    back = lax.all_to_all(
        returned, ("seq", "sub"), split_axis=0, concat_axis=0, tiled=True
    ).reshape(slots_out, D)
    gathered = back[slot_of].reshape(tokens, topk, D).astype(jnp.float32)
    mixture = jnp.sum(gathered, axis=1)
    return (wide + mixture).astype(jnp.bfloat16)[None]


def solution(mesh):
    placed = (
        P(("grp", "sub"), "seq", None),
        P(("grp", "sub"), "seq", None),
        P(("grp", "sub"), "seq", None),
        P(("grp", "sub"), "seq", None),
        P("seq", None),
        P(),
        P(("grp", "sub"), "seq", None),
        P(("grp", "sub"), "seq", None),
        P(("seq", "sub"), None, None),
        P(("seq", "sub"), None, None),
        P(("seq", "sub"), None, None),
    )
    return jax.shard_map(
        per_device,
        mesh=mesh,
        in_specs=placed,
        out_specs=P(("grp", "sub"), "seq", None),
        check_vma=False,
    )
```

```python
import functools

import jax
import jax.numpy as jnp
from jax import lax
from jax.experimental import pallas as pl
from jax.experimental.pallas import tpu as pltpu
from jax.sharding import PartitionSpec as P

D = 2048
HD = 128
QH = 16
KVH = 2
MIB = 1024 * 1024


def attend_head(queries, keys_one, values_one, block):
    length = queries.shape[0]
    scale = 1.0 / queries.shape[1] ** 0.5
    pieces = []
    for part_index in range(length // block):
        stop = (part_index + 1) * block
        rows_here = queries[part_index * block : stop]
        scores = (
            jnp.einsum("qd,kd->qk", rows_here, keys_one[:stop], preferred_element_type=jnp.float32)
            * scale
        )
        row_pos = part_index * block + jnp.arange(block, dtype=jnp.int32)
        col_pos = jnp.arange(stop, dtype=jnp.int32)
        scores = jnp.where(row_pos[:, None] >= col_pos[None, :], scores, -1e30)
        peak = jnp.max(scores, axis=1, keepdims=True)
        weights = jnp.exp(scores - peak)
        probs = (weights / jnp.sum(weights, axis=1, keepdims=True)).astype(jnp.bfloat16)
        pieces.append(
            jnp.dot(probs, values_one[:stop], preferred_element_type=jnp.float32).astype(
                jnp.bfloat16
            )
        )
    return jnp.concatenate(pieces, axis=0)


def rank_in_expert(flat_ids, experts):
    items = flat_ids.shape[0]
    width = 128
    n_parts = items // width
    onehot = (
        (flat_ids[:, None] == jnp.arange(experts, dtype=jnp.int32)[None, :])
        .astype(jnp.bfloat16)
        .reshape(n_parts, width, experts)
    )
    lower = (
        jnp.arange(width, dtype=jnp.int32)[:, None] > jnp.arange(width, dtype=jnp.int32)[None, :]
    ).astype(jnp.bfloat16)
    within = jnp.einsum("ij,bje->bie", lower, onehot, preferred_element_type=jnp.float32)
    part_counts = jnp.sum(onehot.astype(jnp.float32), axis=1)
    earlier = jnp.cumsum(part_counts, axis=0) - part_counts
    ranks = jnp.sum((within + earlier[:, None, :]) * onehot.astype(jnp.float32), axis=2)
    return ranks.reshape(items).astype(jnp.int32)


def pack_kernel(chip_ref, query_ref, key_ref, value_ref, id_ref, gate_ref, away_ref, here_kv_ref, away_kv_ref):
    tokens = query_ref.shape[0]
    head_size = key_ref.shape[1] // 2
    chip_width = away_ref.shape[1]
    chip = chip_ref[0]
    experts = here_kv_ref.shape[0] - tokens
    away_ref[...] = query_ref[:, pl.ds(pl.multiple_of((1 - chip) * chip_width, chip_width), chip_width)]
    number = lax.broadcasted_iota(jnp.int32, (experts, tokens), 0)
    table = jnp.zeros((experts, tokens), jnp.float32)
    for choice in range(id_ref.shape[0]):
        table += jnp.where(
            number == id_ref[choice : choice + 1, :],
            gate_ref[choice : choice + 1, :].astype(jnp.float32),
            0.0,
        )
    for out_ref, head in ((here_kv_ref, chip), (away_kv_ref, 1 - chip)):
        columns = pl.ds(pl.multiple_of(head * head_size, head_size), head_size)
        out_ref[0:tokens, 0:head_size] = key_ref[:, columns]
        out_ref[0:tokens, head_size:] = value_ref[:, columns]
        out_ref[tokens:, 0:head_size] = table.astype(jnp.bfloat16)
        out_ref[tokens:, head_size:] = jnp.zeros((experts, head_size), jnp.bfloat16)


def pack(chip, queries, keys, values, ids, gates, experts):
    tokens, width = queries.shape
    kv = jax.ShapeDtypeStruct((tokens + experts, keys.shape[1]), jnp.bfloat16)
    return pl.pallas_call(
        pack_kernel,
        in_specs=[pl.BlockSpec(memory_space=pltpu.SMEM)]
        + [pl.BlockSpec(memory_space=pltpu.VMEM)] * 5,
        out_specs=[pl.BlockSpec(memory_space=pltpu.VMEM)] * 3,
        out_shape=[jax.ShapeDtypeStruct((tokens, width // 2), jnp.bfloat16), kv, kv],
        compiler_params=pltpu.CompilerParams(vmem_limit_bytes=60 * MIB),
    )(chip.reshape(1), queries, keys, values, ids, gates)


def attend_kernel(place_ref, query_ref, *refs, scale):
    kv_refs, refs = refs[:4], refs[4:]
    base_refs = refs[: len(refs) - 10]
    w_own_ref, w_other_ref, out_ref, quad_ref, keys, values, heads, w_own, w_other, done = refs[-10:]
    fetches = [
        pltpu.make_async_copy(w_own_ref, w_own, done.at[0]),
        pltpu.make_async_copy(w_other_ref, w_other, done.at[1]),
    ]
    for fetch in fetches:
        fetch.start()
    rows = keys.shape[0] // 4
    head_size = keys.shape[1]
    core = place_ref[0]
    query_start = pl.multiple_of(place_ref[1], head_size)
    row_pos = place_ref[2] * rows + lax.broadcasted_iota(jnp.int32, (rows, 1), 0)
    lane = lax.broadcasted_iota(jnp.int32, (1, rows), 1)
    col_pos = jnp.concatenate([place_ref[3 + part] * rows + lane for part in range(4)], axis=1)
    allowed = row_pos >= col_pos
    for part, kv_ref in enumerate(kv_refs):
        keys[part * rows : (part + 1) * rows, :] = kv_ref[0:rows, 0:head_size]
        values[part * rows : (part + 1) * rows, :] = kv_ref[0:rows, head_size:]
        quad_ref[:, part * rows : (part + 1) * rows] = kv_ref[rows:, 0:rows]
    key_block = keys[...]
    value_block = values[...]
    for head in range(heads.shape[1] // head_size):
        query = query_ref[:, pl.ds(query_start + head * head_size, head_size)]
        scores = (
            lax.dot_general(
                query, key_block, (((1,), (1,)), ((), ())), preferred_element_type=jnp.float32
            )
            * scale
        )
        scores = jnp.where(allowed, scores, -1e30)
        weights = jnp.exp(scores - jnp.max(scores, axis=1, keepdims=True))
        probs = (weights * (1.0 / jnp.sum(weights, axis=1, keepdims=True))).astype(jnp.bfloat16)
        heads[:, head * head_size : (head + 1) * head_size] = jnp.dot(
            probs, value_block, preferred_element_type=jnp.float32
        ).astype(jnp.bfloat16)
    for fetch in fetches:
        fetch.wait()
    half = heads.shape[1] // 2
    own = heads[:, pl.ds(pl.multiple_of(core * half, half), half)]
    other = heads[:, pl.ds(pl.multiple_of((1 - core) * half, half), half)]
    total = jnp.dot(own, w_own[...], preferred_element_type=jnp.float32) + jnp.dot(
        other, w_other[...], preferred_element_type=jnp.float32
    )
    for base_ref in base_refs:
        total += base_ref[...].astype(jnp.float32)
    out_ref[...] = total.astype(out_ref.dtype)


def attend(place, queries, kv_parts, bases, w_own, w_other, dtype):
    tokens = queries.shape[0]
    width = w_own.shape[1]
    chip_width = 2 * w_own.shape[0]
    return pl.pallas_call(
        functools.partial(attend_kernel, scale=1.0 / HD**0.5),
        in_specs=[pl.BlockSpec(memory_space=pltpu.SMEM)]
        + [pl.BlockSpec(memory_space=pltpu.VMEM)] * (5 + len(bases))
        + [pl.BlockSpec(memory_space=pl.ANY)] * 2,
        out_specs=[pl.BlockSpec(memory_space=pltpu.VMEM)] * 2,
        out_shape=[
            jax.ShapeDtypeStruct((tokens, width), dtype),
            jax.ShapeDtypeStruct((kv_parts[0].shape[0] - tokens, 4 * tokens), jnp.bfloat16),
        ],
        scratch_shapes=[
            pltpu.VMEM((4 * tokens, HD), jnp.bfloat16),
            pltpu.VMEM((4 * tokens, HD), jnp.bfloat16),
            pltpu.VMEM((tokens, chip_width), jnp.bfloat16),
            pltpu.VMEM(w_own.shape, jnp.bfloat16),
            pltpu.VMEM(w_other.shape, jnp.bfloat16),
            pltpu.SemaphoreType.DMA((2,)),
        ],
        compiler_params=pltpu.CompilerParams(vmem_limit_bytes=60 * MIB),
        cost_estimate=pl.CostEstimate(
            flops=16 * tokens * tokens * chip_width + 2 * tokens * chip_width * width,
            bytes_accessed=4 * w_own.size + 4 * tokens * width,
            transcendentals=4 * tokens * tokens * chip_width // HD,
        ),
    )(place, queries, *kv_parts, *bases, w_own, w_other)


def norm_kernel(own_ref, other_ref, gain_ref, *refs):
    hidden_ref, normed_ref = refs[-2:]
    hidden = (own_ref[...] + other_ref[...].astype(jnp.float32)).astype(jnp.bfloat16)
    hidden_ref[...] = hidden
    wide = hidden.astype(jnp.float32)
    normed_ref[...] = (
        wide
        * lax.rsqrt(jnp.mean(wide * wide, axis=1, keepdims=True) + 1e-06)
        * gain_ref[...].astype(jnp.float32)
    ).astype(jnp.bfloat16)


def add_and_norm(own, other, gain, present):
    return pl.pallas_call(
        norm_kernel,
        in_specs=[pl.BlockSpec(memory_space=pltpu.VMEM)] * 3
        + [pl.BlockSpec(memory_space=pl.ANY)] * len(present),
        out_specs=[pl.BlockSpec(memory_space=pltpu.VMEM)] * 2,
        out_shape=[jax.ShapeDtypeStruct(own.shape, jnp.bfloat16)] * 2,
        compiler_params=pltpu.CompilerParams(vmem_limit_bytes=60 * MIB),
    )(own, other, gain, *present)


def pass_kernel(*refs):
    del refs


def meet(arrays, flops):
    return pl.pallas_call(
        pass_kernel,
        in_specs=[pl.BlockSpec(memory_space=pl.ANY)] * len(arrays),
        out_specs=[pl.BlockSpec(memory_space=pl.ANY)] * len(arrays),
        out_shape=[jax.ShapeDtypeStruct(array.shape, array.dtype) for array in arrays],
        input_output_aliases={index: index for index in range(len(arrays))},
    )(*arrays)


def pass_kernel(*refs):
    del refs


def meet(arrays, flops):
    return pl.pallas_call(
        pass_kernel,
        in_specs=[pl.BlockSpec(memory_space=pl.ANY)] * len(arrays),
        out_specs=[pl.BlockSpec(memory_space=pl.ANY)] * len(arrays),
        out_shape=[jax.ShapeDtypeStruct(array.shape, array.dtype) for array in arrays],
        input_output_aliases={index: index for index in range(len(arrays))},
        compiler_params=pltpu.CompilerParams(vmem_limit_bytes=MIB),
        cost_estimate=pl.CostEstimate(flops=flops, bytes_accessed=0, transcendentals=0),
    )(*arrays)


def experts_kernel(mine_ref, quad_ref, *refs, cap, pieces):
    row_refs = []
    for count in pieces:
        row_refs.append(refs[:count])
        refs = refs[count:]
    w_gate_ref, w_up_ref, w_down_ref, own_ref, across_ref, other_ref, packed = refs
    tokens = row_refs[0][0].shape[0]
    quad = quad_ref[...].astype(jnp.float32)
    expert = lax.broadcasted_iota(jnp.int32, quad.shape, 0)
    line = jnp.sum(jnp.where(expert == mine_ref[0], quad, 0.0), axis=0, keepdims=True)
    gates = jnp.concatenate(
        [line[:, block * tokens : (block + 1) * tokens] for block in range(4)], axis=0
    )
    named = gates > 0
    before = (
        lax.broadcasted_iota(jnp.int32, (tokens, tokens), 0)
        < lax.broadcasted_iota(jnp.int32, (tokens, tokens), 1)
    ).astype(jnp.bfloat16)
    rank = jnp.dot(
        named.astype(jnp.float32).astype(jnp.bfloat16), before, preferred_element_type=jnp.float32
    )
    slot = jnp.where(named, rank.astype(jnp.int32), -1)
    slots = lax.broadcasted_iota(jnp.int32, (cap, tokens), 0)
    picks = []
    weights = []
    for block in range(4):
        chosen = slots == slot[block : block + 1, :]
        picks.append(jnp.where(chosen, 1.0, 0.0).astype(jnp.bfloat16))
        weights.append(
            jnp.sum(jnp.where(chosen, gates[block : block + 1, :], 0.0), axis=1, keepdims=True)
        )
        start = 0
        for row_ref in row_refs[block]:
            stop = start + row_ref.shape[1]
            packed[block * cap : (block + 1) * cap, start:stop] = jnp.dot(
                picks[block], row_ref[...], preferred_element_type=jnp.float32
            ).astype(jnp.bfloat16)
            start = stop
    rows = packed[...]
    gate_proj = jnp.dot(rows, w_gate_ref[...], preferred_element_type=jnp.float32)
    up_proj = jnp.dot(rows, w_up_ref[...], preferred_element_type=jnp.float32)
    inner = (gate_proj / (1.0 + jnp.exp(-gate_proj)) * up_proj).astype(jnp.bfloat16)
    result = jnp.dot(inner, w_down_ref[...], preferred_element_type=jnp.float32)
    targets = (
        own_ref.at[...],
        other_ref.at[0:tokens],
        across_ref.at[...],
        other_ref.at[tokens : 2 * tokens],
    )
    for block in range(4):
        part = (result[block * cap : (block + 1) * cap, :] * weights[block]).astype(jnp.bfloat16)
        targets[block][...] = lax.dot_general(
            picks[block], part, (((0,), (0,)), ((), ())), preferred_element_type=jnp.float32
        ).astype(jnp.bfloat16)


def experts_on_rows(mine, quad, row_blocks, w_gate, w_up, w_down, cap):
    tokens = row_blocks[0][0].shape[0]
    width, hidden_units = w_gate.shape
    pieces = tuple(len(block) for block in row_blocks)
    return pl.pallas_call(
        functools.partial(experts_kernel, cap=cap, pieces=pieces),
        in_specs=[pl.BlockSpec(memory_space=pltpu.SMEM)]
        + [pl.BlockSpec(memory_space=pltpu.VMEM)] * (4 + sum(pieces)),
        out_specs=[pl.BlockSpec(memory_space=pltpu.VMEM)] * 3,
        out_shape=[
            jax.ShapeDtypeStruct((tokens, width), jnp.bfloat16),
            jax.ShapeDtypeStruct((tokens, width), jnp.bfloat16),
            jax.ShapeDtypeStruct((2 * tokens, width), jnp.bfloat16),
        ],
        scratch_shapes=[pltpu.VMEM((4 * cap, width), jnp.bfloat16)],
        compiler_params=pltpu.CompilerParams(vmem_limit_bytes=28 * MIB),
        cost_estimate=pl.CostEstimate(
            flops=24 * cap * width * hidden_units,
            bytes_accessed=16 * tokens * width + 6 * width * hidden_units,
            transcendentals=4 * cap * hidden_units,
        ),
    )(mine.reshape(1), quad, *sum(row_blocks, []), w_gate, w_up, w_down)


def gathered_plan(
    query_rows,
    key_rows,
    value_rows,
    residual_in,
    out_proj,
    norm_gain,
    expert_ids,
    gate_weights,
    expert_gate,
    expert_up,
    expert_down,
    cap,
):
    n_seq = lax.axis_size("seq")
    n_sub = lax.axis_size("sub")
    experts = n_seq * n_sub
    place = lax.axis_index("seq")
    core = place % 2
    chip = place // 2
    twin = [(index, index ^ 1) for index in range(n_seq)]
    across = [(index, (index + 2) % n_seq) for index in range(n_seq)]
    diagonal = [(index, (index ^ 1) ^ 2) for index in range(n_seq)]
    order = [0] + list(range(1, n_sub, 2)) + list(reversed(range(2, n_sub, 2)))

    def ring(steps):
        return [(order[at], order[(at + steps) % n_sub]) for at in range(n_sub)]

    queries = query_rows[0]
    chip_width = queries.shape[1] // 2

    tokens = queries.shape[0]
    queries_away, kv_here, kv_away = pack(
        chip,
        queries,
        key_rows[0],
        value_rows[0],
        expert_ids[0].T,
        gate_weights[0].T,
        experts,
    )
    incoming = lax.ppermute(queries_away, "seq", across)
    kv_parts = [
        kv_here,
        lax.ppermute(kv_here, "seq", twin),
        lax.ppermute(kv_away, "seq", across),
        lax.ppermute(kv_away, "seq", diagonal),
    ]
    w_other = lax.ppermute(out_proj, "seq", twin)
    columns = [place, place ^ 1, place ^ 2, place ^ 3]

    def place_of(query_start, row_block):
        return jnp.stack([core, query_start, row_block] + columns).astype(jnp.int32)

    sent, quad = attend(
        place_of(0 * place, place ^ 2), incoming, kv_parts, [], out_proj, w_other, jnp.bfloat16
    )
    projected_across = lax.ppermute(sent, "seq", across)
    projected, _ = attend(
        place_of(chip * chip_width, place),
        queries,
        kv_parts,
        [residual_in[0]],
        out_proj,
        w_other,
        jnp.float32,
    )
    quads = [lax.ppermute(quad, "sub", ring(steps)) for steps in range(1, n_sub)]
    hidden, normed = add_and_norm(projected, projected_across, norm_gain[None], quads)

    last = n_sub - 1
    mine = place * n_sub + lax.axis_index("sub")

    held = {("row", 0): normed, ("quad", 0): quad}
    held.update({("quad", steps): moved for steps, moved in enumerate(quads, 1)})
    half = normed.shape[1] // 2
    ways = {"across": ("seq", across), "twin": ("seq", twin), "on": ("sub", ring(1))}

    def move(array, way):
        return lax.ppermute(array, *ways[way])

    def experts_of(step):
        held["own", step], held["part", step], other = experts_on_rows(
            mine,
            held["quad", step],
            [
                [held[name, step]] if (name, step) in held else list(held[name, step, "pieces"])
                for name in ("row", "twin", "across", "diagonal")
            ],
            expert_gate[0],
            expert_up[0],
            expert_down[0],
            cap,
        )
        return other

    def twin_sum(step):
        met = move(held["other", step], "twin")
        held["met", step] = met[:tokens]
        return (held["part", step].astype(jnp.float32) + met[tokens:].astype(jnp.float32)).astype(
            jnp.bfloat16
        )

    def sum_of(step, more):
        parts = [held["own", step], held["met", step], held["back", step]] + more
        if held["back", step].shape[1] == half:
            left = sum(part[:, :half].astype(jnp.float32) for part in parts)
            right = sum(part[:, half:].astype(jnp.float32) for part in parts if part.shape[1] > half)
            return jnp.concatenate([left, right], axis=1)
        return sum(part.astype(jnp.float32) for part in parts)

    for turn in range(1, n_sub + 5):
        now = {}
        step = turn - 1
        if step < last:
            now["across", step] = move(held["row", step], "across")
            now["row", step + 1] = move(held["row", step], "on")
        if step == last:
            now["half", 0] = move(held["row", step][:, :half], "across")
            now["half", 1] = move(held["across", step - 1][:, half:], "on")
        if step <= last:
            held["twin", step] = move(held["row", step], "twin")
        step = turn - 4 if turn < n_sub + 4 else 0
        if 1 <= step <= last or turn == n_sub + 4:
            if step == 1 and last > 1:
                now["back", step] = move(held["away", step][:, :half], "across")
                now["late", step] = move(held["away", step][:, half:], "on")
            elif step == 2:
                away = held["away", step]
                added = away[:, half:].astype(jnp.float32) + held["late", 1].astype(jnp.float32)
                now["back", step] = move(
                    jnp.concatenate([away[:, :half], added.astype(jnp.bfloat16)], axis=1), "across"
                )
            else:
                now["back", step] = move(held["away", step], "across")
        step = turn - 5
        if 1 <= step <= last:
            more = [held["sum", step - 1]] if step > 1 else []
            now["sum", step] = move(sum_of(step, more).astype(jnp.bfloat16), "on")
        step = turn - 2
        if 0 <= step < last:
            held["diagonal", step] = move(held["across", step], "twin")
        if step == last:
            held["across", step, "pieces"] = [held["half", side] for side in range(2)]
            held["diagonal", step, "pieces"] = [
                move(held["half", side], "twin") for side in range(2)
            ]
        if 1 <= step <= last:
            now["other", step] = experts_of(step)
        if turn == n_sub + 2:
            now["other", 0] = experts_of(0)
        step = turn - 3 if turn < n_sub + 3 else 0
        if 1 <= step <= last or turn == n_sub + 3:
            now["away", step] = twin_sum(step)
        if turn < n_sub + 4:
            wait = 10_000_000_000 if turn <= 2 else 0
            now = dict(zip(now.keys(), meet(list(now.values()), wait)))
        held.update(now)
    total = hidden.astype(jnp.float32) + sum_of(0, [held["sum", last]])
    return total.astype(jnp.bfloat16)[None]


def per_device(
    query_rows,
    key_rows,
    value_rows,
    residual_in,
    out_proj,
    norm_gain,
    expert_ids,
    gate_weights,
    expert_gate,
    expert_up,
    expert_down,
):
    tokens = query_rows.shape[1]
    n_seq = lax.axis_size("seq")
    n_sub = lax.axis_size("sub")
    experts = n_seq * n_sub
    topk = expert_ids.shape[2]
    cap = max(2, (5 * tokens * topk + 4 * experts - 1) // (4 * experts))
    if n_seq == 2 * KVH and KVH == 2 and tokens == HD and n_sub > 2 and experts <= 2 * topk and cap % 16 == 0:
        return gathered_plan(
            query_rows,
            key_rows,
            value_rows,
            residual_in,
            out_proj,
            norm_gain,
            expert_ids,
            gate_weights,
            expert_gate,
            expert_up,
            expert_down,
            cap,
        )
    heads_here = QH // n_seq
    group = QH // KVH
    query_local = lax.all_to_all(query_rows, "seq", split_axis=2, concat_axis=1, tiled=True)
    key_full, value_full = (
        lax.all_gather(key_rows, "seq", axis=1, tiled=True),
        lax.all_gather(value_rows, "seq", axis=1, tiled=True),
    )
    first_head = lax.axis_index("seq") * heads_here
    key_list = []
    value_list = []
    for head in range(heads_here):
        kv_start = (first_head + head) // group * HD
        key_list.append(lax.dynamic_slice_in_dim(key_full[0], kv_start, HD, 1))
        value_list.append(lax.dynamic_slice_in_dim(value_full[0], kv_start, HD, 1))
    length = query_local.shape[1]
    block = min(length, max(512, length // 8))
    outputs = [
        attend_head(
            query_local[0, :, head * HD : (head + 1) * HD], key_list[head], value_list[head], block
        )
        for head in range(heads_here)
    ]
    head_block = jnp.concatenate(outputs, axis=1)[None]
    attended = lax.all_to_all(head_block, "seq", split_axis=1, concat_axis=2, tiled=True)[0]
    projected = jnp.dot(
        attended,
        lax.all_gather(out_proj, "seq", axis=0, tiled=True),
        preferred_element_type=jnp.float32,
    )
    hidden = (residual_in[0].astype(jnp.float32) + projected).astype(jnp.bfloat16)
    wide = hidden.astype(jnp.float32)
    normed = (
        wide
        * lax.rsqrt(jnp.mean(wide * wide, axis=1, keepdims=True) + 1e-06)
        * norm_gain.astype(jnp.float32)
    ).astype(jnp.bfloat16)
    flat_ids = expert_ids[0].reshape(-1)
    items = flat_ids.shape[0]
    ranks = rank_in_expert(flat_ids, experts)
    slot_of = flat_ids * cap + ranks
    slots_out = experts * cap
    item_of_slot = (
        jnp.full((slots_out,), items, jnp.int32).at[slot_of].set(jnp.arange(items, dtype=jnp.int32))
    )
    padded_rows = jnp.concatenate([normed, jnp.zeros((1, D), jnp.bfloat16)], axis=0)
    padded_gates = jnp.concatenate(
        [gate_weights[0].reshape(-1), jnp.zeros((1,), jnp.bfloat16)], axis=0
    )
    token_of_slot = jnp.where(item_of_slot < items, item_of_slot // topk, tokens)
    send_rows = padded_rows[token_of_slot].reshape(experts, cap, D)
    send_gates = padded_gates[item_of_slot].reshape(experts, cap)
    recv_rows, recv_gates = (
        lax.all_to_all(send_rows, ("seq", "sub"), split_axis=0, concat_axis=0, tiled=True),
        lax.all_to_all(send_gates, ("seq", "sub"), split_axis=0, concat_axis=0, tiled=True),
    )
    slots_in = experts * cap
    valid = recv_gates > 0
    counts = jnp.sum(valid.astype(jnp.int32), axis=1)
    offsets = jnp.cumsum(counts) - counts
    dest = jnp.where(
        valid, offsets[:, None] + jnp.arange(cap, dtype=jnp.int32)[None, :], slots_in
    ).reshape(-1)
    source_of = (
        jnp.full((slots_in + 1,), slots_in, jnp.int32)
        .at[dest]
        .set(jnp.arange(slots_in, dtype=jnp.int32))[:slots_in]
    )
    compact_rows = jnp.concatenate(
        [recv_rows.reshape(slots_in, D), jnp.zeros((1, D), jnp.bfloat16)], axis=0
    )[source_of]
    compact_gates = jnp.concatenate(
        [recv_gates.reshape(-1), jnp.zeros((1,), jnp.bfloat16)], axis=0
    )[source_of].astype(jnp.float32)
    filled = jnp.sum(counts)
    n_blocks = (filled + slots_in - 1) // slots_in
    w_gate = expert_gate[0]
    w_up = expert_up[0]
    w_down = expert_down[0]

    def expert_block(index, results):
        gate_proj = jnp.dot(compact_rows, w_gate, preferred_element_type=jnp.float32)
        up_proj = jnp.dot(compact_rows, w_up, preferred_element_type=jnp.float32)
        inner = (jax.nn.silu(gate_proj) * up_proj).astype(jnp.bfloat16)
        weighted = (
            jnp.dot(inner, w_down, preferred_element_type=jnp.float32) * compact_gates[:, None]
        )
        return weighted.astype(jnp.bfloat16)

    results = lax.fori_loop(0, n_blocks, expert_block, jnp.zeros((slots_in, D), jnp.bfloat16))
    returned = jnp.concatenate([results, jnp.zeros((1, D), jnp.bfloat16)], axis=0)[dest].reshape(
        experts, cap, D
    )
    back = lax.all_to_all(
        returned, ("seq", "sub"), split_axis=0, concat_axis=0, tiled=True
    ).reshape(slots_out, D)
    gathered = back[slot_of].reshape(tokens, topk, D).astype(jnp.float32)
    mixture = jnp.sum(gathered, axis=1)
    return (wide + mixture).astype(jnp.bfloat16)[None]


def solution(mesh):
    placed = (
        P(("grp", "sub"), "seq", None),
        P(("grp", "sub"), "seq", None),
        P(("grp", "sub"), "seq", None),
        P(("grp", "sub"), "seq", None),
        P("seq", None),
        P(),
        P(("grp", "sub"), "seq", None),
        P(("grp", "sub"), "seq", None),
        P(("seq", "sub"), None, None),
        P(("seq", "sub"), None, None),
        P(("seq", "sub"), None, None),
    )
    return jax.shard_map(
        per_device,
        mesh=mesh,
        in_specs=placed,
        out_specs=P(("grp", "sub"), "seq", None),
        check_vma=False,
    )
```

```python
import functools

import jax
import jax.numpy as jnp
from jax import lax
from jax.experimental import pallas as pl
from jax.experimental.pallas import tpu as pltpu
from jax.sharding import PartitionSpec as P

D = 2048
HD = 128
QH = 16
KVH = 2
MIB = 1024 * 1024


def attend_head(queries, keys_one, values_one, block):
    length = queries.shape[0]
    scale = 1.0 / queries.shape[1] ** 0.5
    pieces = []
    for part_index in range(length // block):
        stop = (part_index + 1) * block
        rows_here = queries[part_index * block : stop]
        scores = (
            jnp.einsum("qd,kd->qk", rows_here, keys_one[:stop], preferred_element_type=jnp.float32)
            * scale
        )
        row_pos = part_index * block + jnp.arange(block, dtype=jnp.int32)
        col_pos = jnp.arange(stop, dtype=jnp.int32)
        scores = jnp.where(row_pos[:, None] >= col_pos[None, :], scores, -1e30)
        peak = jnp.max(scores, axis=1, keepdims=True)
        weights = jnp.exp(scores - peak)
        probs = (weights / jnp.sum(weights, axis=1, keepdims=True)).astype(jnp.bfloat16)
        pieces.append(
            jnp.dot(probs, values_one[:stop], preferred_element_type=jnp.float32).astype(
                jnp.bfloat16
            )
        )
    return jnp.concatenate(pieces, axis=0)


def rank_in_expert(flat_ids, experts):
    items = flat_ids.shape[0]
    width = 128
    n_parts = items // width
    onehot = (
        (flat_ids[:, None] == jnp.arange(experts, dtype=jnp.int32)[None, :])
        .astype(jnp.bfloat16)
        .reshape(n_parts, width, experts)
    )
    lower = (
        jnp.arange(width, dtype=jnp.int32)[:, None] > jnp.arange(width, dtype=jnp.int32)[None, :]
    ).astype(jnp.bfloat16)
    within = jnp.einsum("ij,bje->bie", lower, onehot, preferred_element_type=jnp.float32)
    part_counts = jnp.sum(onehot.astype(jnp.float32), axis=1)
    earlier = jnp.cumsum(part_counts, axis=0) - part_counts
    ranks = jnp.sum((within + earlier[:, None, :]) * onehot.astype(jnp.float32), axis=2)
    return ranks.reshape(items).astype(jnp.int32)


def pack_kernel(chip_ref, query_ref, key_ref, value_ref, id_ref, gate_ref, away_ref, here_kv_ref, away_kv_ref):
    tokens = query_ref.shape[0]
    head_size = key_ref.shape[1] // 2
    chip_width = away_ref.shape[1]
    chip = chip_ref[0]
    experts = here_kv_ref.shape[0] - tokens
    away_ref[...] = query_ref[:, pl.ds(pl.multiple_of((1 - chip) * chip_width, chip_width), chip_width)]
    number = lax.broadcasted_iota(jnp.int32, (experts, tokens), 0)
    table = jnp.zeros((experts, tokens), jnp.float32)
    for choice in range(id_ref.shape[0]):
        table += jnp.where(
            number == id_ref[choice : choice + 1, :],
            gate_ref[choice : choice + 1, :].astype(jnp.float32),
            0.0,
        )
    for out_ref, head in ((here_kv_ref, chip), (away_kv_ref, 1 - chip)):
        columns = pl.ds(pl.multiple_of(head * head_size, head_size), head_size)
        out_ref[0:tokens, 0:head_size] = key_ref[:, columns]
        out_ref[0:tokens, head_size:] = value_ref[:, columns]
        out_ref[tokens:, 0:head_size] = table.astype(jnp.bfloat16)
        out_ref[tokens:, head_size:] = jnp.zeros((experts, head_size), jnp.bfloat16)


def pack(chip, queries, keys, values, ids, gates, experts):
    tokens, width = queries.shape
    kv = jax.ShapeDtypeStruct((tokens + experts, keys.shape[1]), jnp.bfloat16)
    return pl.pallas_call(
        pack_kernel,
        in_specs=[pl.BlockSpec(memory_space=pltpu.SMEM)]
        + [pl.BlockSpec(memory_space=pltpu.VMEM)] * 5,
        out_specs=[pl.BlockSpec(memory_space=pltpu.VMEM)] * 3,
        out_shape=[jax.ShapeDtypeStruct((tokens, width // 2), jnp.bfloat16), kv, kv],
        compiler_params=pltpu.CompilerParams(vmem_limit_bytes=60 * MIB),
    )(chip.reshape(1), queries, keys, values, ids, gates)


def attend_kernel(place_ref, query_ref, *refs, scale):
    kv_refs, refs = refs[:4], refs[4:]
    base_refs = refs[: len(refs) - 10]
    w_own_ref, w_other_ref, out_ref, quad_ref, keys, values, heads, w_own, w_other, done = refs[-10:]
    fetches = [
        pltpu.make_async_copy(w_own_ref, w_own, done.at[0]),
        pltpu.make_async_copy(w_other_ref, w_other, done.at[1]),
    ]
    for fetch in fetches:
        fetch.start()
    rows = keys.shape[0] // 4
    head_size = keys.shape[1]
    core = place_ref[0]
    query_start = pl.multiple_of(place_ref[1], head_size)
    lane = lax.broadcasted_iota(jnp.int32, (1, rows), 1)
    col_pos = jnp.concatenate([place_ref[3 + part] * rows + lane for part in range(4)], axis=1)
    for part, kv_ref in enumerate(kv_refs):
        keys[part * rows : (part + 1) * rows, :] = kv_ref[0:rows, 0:head_size]
        values[part * rows : (part + 1) * rows, :] = kv_ref[0:rows, head_size:]
        quad_ref[:, part * rows : (part + 1) * rows] = kv_ref[rows:, 0:rows]
    key_block = keys[...]
    value_block = values[...]
    part = rows // 2
    for start in range(0, rows, part):
        row_pos = (
            place_ref[2] * rows + start + lax.broadcasted_iota(jnp.int32, (part, 1), 0)
        )
        allowed = row_pos >= col_pos
        for head in range(heads.shape[1] // head_size):
            query = query_ref[
                start : start + part, pl.ds(query_start + head * head_size, head_size)
            ]
            scores = (
                lax.dot_general(
                    query, key_block, (((1,), (1,)), ((), ())), preferred_element_type=jnp.float32
                )
                * scale
            )
            scores = jnp.where(allowed, scores, -1e30)
            weights = jnp.exp(scores - jnp.max(scores, axis=1, keepdims=True))
            probs = (weights * (1.0 / jnp.sum(weights, axis=1, keepdims=True))).astype(jnp.bfloat16)
            heads[start : start + part, head * head_size : (head + 1) * head_size] = jnp.dot(
                probs, value_block, preferred_element_type=jnp.float32
            ).astype(jnp.bfloat16)
    for fetch in fetches:
        fetch.wait()
    half = heads.shape[1] // 2
    own = heads[:, pl.ds(pl.multiple_of(core * half, half), half)]
    other = heads[:, pl.ds(pl.multiple_of((1 - core) * half, half), half)]
    total = jnp.dot(own, w_own[...], preferred_element_type=jnp.float32) + jnp.dot(
        other, w_other[...], preferred_element_type=jnp.float32
    )
    for base_ref in base_refs:
        total += base_ref[...].astype(jnp.float32)
    out_ref[...] = total.astype(out_ref.dtype)


def attend(place, queries, kv_parts, bases, w_own, w_other, dtype):
    tokens = queries.shape[0]
    width = w_own.shape[1]
    chip_width = 2 * w_own.shape[0]
    return pl.pallas_call(
        functools.partial(attend_kernel, scale=1.0 / HD**0.5),
        in_specs=[pl.BlockSpec(memory_space=pltpu.SMEM)]
        + [pl.BlockSpec(memory_space=pltpu.VMEM)] * (5 + len(bases))
        + [pl.BlockSpec(memory_space=pl.ANY)] * 2,
        out_specs=[pl.BlockSpec(memory_space=pltpu.VMEM)] * 2,
        out_shape=[
            jax.ShapeDtypeStruct((tokens, width), dtype),
            jax.ShapeDtypeStruct((kv_parts[0].shape[0] - tokens, 4 * tokens), jnp.bfloat16),
        ],
        scratch_shapes=[
            pltpu.VMEM((4 * tokens, HD), jnp.bfloat16),
            pltpu.VMEM((4 * tokens, HD), jnp.bfloat16),
            pltpu.VMEM((tokens, chip_width), jnp.bfloat16),
            pltpu.VMEM(w_own.shape, jnp.bfloat16),
            pltpu.VMEM(w_other.shape, jnp.bfloat16),
            pltpu.SemaphoreType.DMA((2,)),
        ],
        compiler_params=pltpu.CompilerParams(vmem_limit_bytes=60 * MIB),
        cost_estimate=pl.CostEstimate(
            flops=16 * tokens * tokens * chip_width + 2 * tokens * chip_width * width,
            bytes_accessed=4 * w_own.size + 4 * tokens * width,
            transcendentals=4 * tokens * tokens * chip_width // HD,
        ),
    )(place, queries, *kv_parts, *bases, w_own, w_other)


def norm_kernel(own_ref, other_ref, gain_ref, *refs):
    hidden_ref, normed_ref = refs[-2:]
    gain = gain_ref[...].astype(jnp.float32)
    rows = 16
    for start in range(0, own_ref.shape[0], rows):
        part = slice(start, start + rows)
        hidden = (own_ref[part, :] + other_ref[part, :].astype(jnp.float32)).astype(jnp.bfloat16)
        hidden_ref[part, :] = hidden
        wide = hidden.astype(jnp.float32)
        normed_ref[part, :] = (
            wide * lax.rsqrt(jnp.mean(wide * wide, axis=1, keepdims=True) + 1e-06) * gain
        ).astype(jnp.bfloat16)


def add_and_norm(own, other, gain, present):
    return pl.pallas_call(
        norm_kernel,
        in_specs=[pl.BlockSpec(memory_space=pltpu.VMEM)] * 3
        + [pl.BlockSpec(memory_space=pl.ANY)] * len(present),
        out_specs=[pl.BlockSpec(memory_space=pltpu.VMEM)] * 2,
        out_shape=[jax.ShapeDtypeStruct(own.shape, jnp.bfloat16)] * 2,
        compiler_params=pltpu.CompilerParams(vmem_limit_bytes=60 * MIB),
    )(own, other, gain, *present)


def pass_kernel(*refs):
    del refs


def meet(arrays, flops):
    return pl.pallas_call(
        pass_kernel,
        in_specs=[pl.BlockSpec(memory_space=pl.ANY)] * len(arrays),
        out_specs=[pl.BlockSpec(memory_space=pl.ANY)] * len(arrays),
        out_shape=[jax.ShapeDtypeStruct(array.shape, array.dtype) for array in arrays],
        input_output_aliases={index: index for index in range(len(arrays))},
    )(*arrays)


def pass_kernel(*refs):
    del refs


def meet(arrays, flops):
    return pl.pallas_call(
        pass_kernel,
        in_specs=[pl.BlockSpec(memory_space=pl.ANY)] * len(arrays),
        out_specs=[pl.BlockSpec(memory_space=pl.ANY)] * len(arrays),
        out_shape=[jax.ShapeDtypeStruct(array.shape, array.dtype) for array in arrays],
        input_output_aliases={index: index for index in range(len(arrays))},
        compiler_params=pltpu.CompilerParams(vmem_limit_bytes=MIB),
        cost_estimate=pl.CostEstimate(flops=flops, bytes_accessed=0, transcendentals=0),
    )(*arrays)


def experts_kernel(mine_ref, quad_ref, *refs, cap, pieces):
    row_refs = []
    for count in pieces:
        row_refs.append(refs[:count])
        refs = refs[count:]
    w_gate_ref, w_up_ref, w_down_ref, own_ref, across_ref, other_ref, packed = refs
    tokens = row_refs[0][0].shape[0]
    quad = quad_ref[...].astype(jnp.float32)
    expert = lax.broadcasted_iota(jnp.int32, quad.shape, 0)
    line = jnp.sum(jnp.where(expert == mine_ref[0], quad, 0.0), axis=0, keepdims=True)
    gates = jnp.concatenate(
        [line[:, block * tokens : (block + 1) * tokens] for block in range(4)], axis=0
    )
    named = gates > 0
    before = (
        lax.broadcasted_iota(jnp.int32, (tokens, tokens), 0)
        < lax.broadcasted_iota(jnp.int32, (tokens, tokens), 1)
    ).astype(jnp.bfloat16)
    rank = jnp.dot(
        named.astype(jnp.float32).astype(jnp.bfloat16), before, preferred_element_type=jnp.float32
    )
    slot = jnp.where(named, rank.astype(jnp.int32), -1)
    slots = lax.broadcasted_iota(jnp.int32, (cap, tokens), 0)
    picks = []
    weights = []
    for block in range(4):
        chosen = slots == slot[block : block + 1, :]
        picks.append(jnp.where(chosen, 1.0, 0.0).astype(jnp.bfloat16))
        weights.append(
            jnp.sum(jnp.where(chosen, gates[block : block + 1, :], 0.0), axis=1, keepdims=True)
        )
        start = 0
        for row_ref in row_refs[block]:
            stop = start + row_ref.shape[1]
            packed[block * cap : (block + 1) * cap, start:stop] = jnp.dot(
                picks[block], row_ref[...], preferred_element_type=jnp.float32
            ).astype(jnp.bfloat16)
            start = stop
    rows = packed[...]
    gate_proj = jnp.dot(rows, w_gate_ref[...], preferred_element_type=jnp.float32)
    up_proj = jnp.dot(rows, w_up_ref[...], preferred_element_type=jnp.float32)
    inner = (gate_proj / (1.0 + jnp.exp(-gate_proj)) * up_proj).astype(jnp.bfloat16)
    result = jnp.dot(inner, w_down_ref[...], preferred_element_type=jnp.float32)
    targets = (
        own_ref.at[...],
        other_ref.at[0:tokens],
        across_ref.at[...],
        other_ref.at[tokens : 2 * tokens],
    )
    for block in range(4):
        part = (result[block * cap : (block + 1) * cap, :] * weights[block]).astype(jnp.bfloat16)
        targets[block][...] = lax.dot_general(
            picks[block], part, (((0,), (0,)), ((), ())), preferred_element_type=jnp.float32
        ).astype(jnp.bfloat16)


def experts_on_rows(mine, quad, row_blocks, w_gate, w_up, w_down, cap):
    tokens = row_blocks[0][0].shape[0]
    width, hidden_units = w_gate.shape
    pieces = tuple(len(block) for block in row_blocks)
    return pl.pallas_call(
        functools.partial(experts_kernel, cap=cap, pieces=pieces),
        in_specs=[pl.BlockSpec(memory_space=pltpu.SMEM)]
        + [pl.BlockSpec(memory_space=pltpu.VMEM)] * (4 + sum(pieces)),
        out_specs=[pl.BlockSpec(memory_space=pltpu.VMEM)] * 3,
        out_shape=[
            jax.ShapeDtypeStruct((tokens, width), jnp.bfloat16),
            jax.ShapeDtypeStruct((tokens, width), jnp.bfloat16),
            jax.ShapeDtypeStruct((2 * tokens, width), jnp.bfloat16),
        ],
        scratch_shapes=[pltpu.VMEM((4 * cap, width), jnp.bfloat16)],
        compiler_params=pltpu.CompilerParams(vmem_limit_bytes=28 * MIB),
        cost_estimate=pl.CostEstimate(
            flops=24 * cap * width * hidden_units,
            bytes_accessed=16 * tokens * width + 6 * width * hidden_units,
            transcendentals=4 * cap * hidden_units,
        ),
    )(mine.reshape(1), quad, *sum(row_blocks, []), w_gate, w_up, w_down)


def gathered_plan(
    query_rows,
    key_rows,
    value_rows,
    residual_in,
    out_proj,
    norm_gain,
    expert_ids,
    gate_weights,
    expert_gate,
    expert_up,
    expert_down,
    cap,
):
    n_seq = lax.axis_size("seq")
    n_sub = lax.axis_size("sub")
    experts = n_seq * n_sub
    place = lax.axis_index("seq")
    core = place % 2
    chip = place // 2
    twin = [(index, index ^ 1) for index in range(n_seq)]
    across = [(index, (index + 2) % n_seq) for index in range(n_seq)]
    order = [0] + list(range(1, n_sub, 2)) + list(reversed(range(2, n_sub, 2)))

    def ring(steps):
        return [(order[at], order[(at + steps) % n_sub]) for at in range(n_sub)]

    queries = query_rows[0]
    chip_width = queries.shape[1] // 2

    tokens = queries.shape[0]
    queries_away, kv_here, kv_away = pack(
        chip,
        queries,
        key_rows[0],
        value_rows[0],
        expert_ids[0].T,
        gate_weights[0].T,
        experts,
    )
    incoming = lax.ppermute(queries_away, "seq", across)
    kv_across = lax.ppermute(kv_away, "seq", across)
    kv_parts = [
        kv_here,
        lax.ppermute(kv_here, "seq", twin),
        kv_across,
        lax.ppermute(kv_across, "seq", twin),
    ]
    w_other = lax.ppermute(out_proj, "seq", twin)
    columns = [place, place ^ 1, place ^ 2, place ^ 3]

    def place_of(query_start, row_block):
        return jnp.stack([core, query_start, row_block] + columns).astype(jnp.int32)

    sent, quad = attend(
        place_of(0 * place, place ^ 2), incoming, kv_parts, [], out_proj, w_other, jnp.bfloat16
    )
    projected_across = lax.ppermute(sent, "seq", across)
    projected, _ = attend(
        place_of(chip * chip_width, place),
        queries,
        kv_parts,
        [residual_in[0]],
        out_proj,
        w_other,
        jnp.float32,
    )
    quads = [lax.ppermute(quad, "sub", ring(steps)) for steps in range(1, n_sub)]
    hidden, normed = add_and_norm(projected, projected_across, norm_gain[None], quads)

    last = n_sub - 1
    mine = place * n_sub + lax.axis_index("sub")

    held = {("row", 0): normed, ("quad", 0): quad}
    held.update({("quad", steps): moved for steps, moved in enumerate(quads, 1)})
    half = normed.shape[1] // 2
    ways = {"across": ("seq", across), "twin": ("seq", twin), "on": ("sub", ring(1))}

    def move(array, way):
        return lax.ppermute(array, *ways[way])

    def experts_of(step):
        held["own", step], held["part", step], other = experts_on_rows(
            mine,
            held["quad", step],
            [
                [held[name, step]] if (name, step) in held else list(held[name, step, "pieces"])
                for name in ("row", "twin", "across", "diagonal")
            ],
            expert_gate[0],
            expert_up[0],
            expert_down[0],
            cap,
        )
        return other

    def twin_sum(step):
        met = move(held["other", step], "twin")
        held["met", step] = met[:tokens]
        return (held["part", step].astype(jnp.float32) + met[tokens:].astype(jnp.float32)).astype(
            jnp.bfloat16
        )

    def sum_of(step, more):
        parts = [held["own", step], held["met", step], held["back", step]] + more
        if held["back", step].shape[1] == half:
            left = sum(part[:, :half].astype(jnp.float32) for part in parts)
            right = sum(part[:, half:].astype(jnp.float32) for part in parts if part.shape[1] > half)
            return jnp.concatenate([left, right], axis=1)
        return sum(part.astype(jnp.float32) for part in parts)

    for turn in range(1, n_sub + 5):
        now = {}
        step = turn - 1
        if step < last:
            now["across", step] = move(held["row", step], "across")
            now["row", step + 1] = move(held["row", step], "on")
        if step == last:
            now["half", 0] = move(held["row", step][:, :half], "across")
            now["half", 1] = move(held["across", step - 1][:, half:], "on")
        if step <= last:
            held["twin", step] = move(held["row", step], "twin")
        step = turn - 4 if turn < n_sub + 4 else 0
        if 1 <= step <= last or turn == n_sub + 4:
            if step == 1 and last > 1:
                now["back", step] = move(held["away", step][:, :half], "across")
                now["late", step] = move(held["away", step][:, half:], "on")
            elif step == 2:
                away = held["away", step]
                added = away[:, half:].astype(jnp.float32) + held["late", 1].astype(jnp.float32)
                now["back", step] = move(
                    jnp.concatenate([away[:, :half], added.astype(jnp.bfloat16)], axis=1), "across"
                )
            else:
                now["back", step] = move(held["away", step], "across")
        step = turn - 5
        if 1 <= step <= last:
            more = [held["sum", step - 1]] if step > 1 else []
            now["sum", step] = move(sum_of(step, more).astype(jnp.bfloat16), "on")
        step = turn - 2
        if 0 <= step < last:
            held["diagonal", step] = move(held["across", step], "twin")
        if step == last:
            held["across", step, "pieces"] = [held["half", side] for side in range(2)]
            held["diagonal", step, "pieces"] = [
                move(held["half", side], "twin") for side in range(2)
            ]
        if 1 <= step <= last:
            now["other", step] = experts_of(step)
        if turn == n_sub + 2:
            now["other", 0] = experts_of(0)
        step = turn - 3 if turn < n_sub + 3 else 0
        if 1 <= step <= last or turn == n_sub + 3:
            now["away", step] = twin_sum(step)
        if turn < n_sub + 4:
            wait = 10_000_000_000 if turn <= 2 else 0
            now = dict(zip(now.keys(), meet(list(now.values()), wait)))
        held.update(now)
    total = hidden.astype(jnp.float32) + sum_of(0, [held["sum", last]])
    return total.astype(jnp.bfloat16)[None]


def per_device(
    query_rows,
    key_rows,
    value_rows,
    residual_in,
    out_proj,
    norm_gain,
    expert_ids,
    gate_weights,
    expert_gate,
    expert_up,
    expert_down,
):
    tokens = query_rows.shape[1]
    n_seq = lax.axis_size("seq")
    n_sub = lax.axis_size("sub")
    experts = n_seq * n_sub
    topk = expert_ids.shape[2]
    cap = max(2, (5 * tokens * topk + 4 * experts - 1) // (4 * experts))
    if n_seq == 2 * KVH and KVH == 2 and tokens == HD and n_sub > 2 and experts <= 2 * topk and cap % 16 == 0:
        return gathered_plan(
            query_rows,
            key_rows,
            value_rows,
            residual_in,
            out_proj,
            norm_gain,
            expert_ids,
            gate_weights,
            expert_gate,
            expert_up,
            expert_down,
            cap,
        )
    heads_here = QH // n_seq
    group = QH // KVH
    query_local = lax.all_to_all(query_rows, "seq", split_axis=2, concat_axis=1, tiled=True)
    key_full, value_full = (
        lax.all_gather(key_rows, "seq", axis=1, tiled=True),
        lax.all_gather(value_rows, "seq", axis=1, tiled=True),
    )
    first_head = lax.axis_index("seq") * heads_here
    key_list = []
    value_list = []
    for head in range(heads_here):
        kv_start = (first_head + head) // group * HD
        key_list.append(lax.dynamic_slice_in_dim(key_full[0], kv_start, HD, 1))
        value_list.append(lax.dynamic_slice_in_dim(value_full[0], kv_start, HD, 1))
    length = query_local.shape[1]
    block = min(length, max(512, length // 8))
    outputs = [
        attend_head(
            query_local[0, :, head * HD : (head + 1) * HD], key_list[head], value_list[head], block
        )
        for head in range(heads_here)
    ]
    head_block = jnp.concatenate(outputs, axis=1)[None]
    attended = lax.all_to_all(head_block, "seq", split_axis=1, concat_axis=2, tiled=True)[0]
    projected = jnp.dot(
        attended,
        lax.all_gather(out_proj, "seq", axis=0, tiled=True),
        preferred_element_type=jnp.float32,
    )
    hidden = (residual_in[0].astype(jnp.float32) + projected).astype(jnp.bfloat16)
    wide = hidden.astype(jnp.float32)
    normed = (
        wide
        * lax.rsqrt(jnp.mean(wide * wide, axis=1, keepdims=True) + 1e-06)
        * norm_gain.astype(jnp.float32)
    ).astype(jnp.bfloat16)
    flat_ids = expert_ids[0].reshape(-1)
    items = flat_ids.shape[0]
    ranks = rank_in_expert(flat_ids, experts)
    slot_of = flat_ids * cap + ranks
    slots_out = experts * cap
    item_of_slot = (
        jnp.full((slots_out,), items, jnp.int32).at[slot_of].set(jnp.arange(items, dtype=jnp.int32))
    )
    padded_rows = jnp.concatenate([normed, jnp.zeros((1, D), jnp.bfloat16)], axis=0)
    padded_gates = jnp.concatenate(
        [gate_weights[0].reshape(-1), jnp.zeros((1,), jnp.bfloat16)], axis=0
    )
    token_of_slot = jnp.where(item_of_slot < items, item_of_slot // topk, tokens)
    send_rows = padded_rows[token_of_slot].reshape(experts, cap, D)
    send_gates = padded_gates[item_of_slot].reshape(experts, cap)
    recv_rows, recv_gates = (
        lax.all_to_all(send_rows, ("seq", "sub"), split_axis=0, concat_axis=0, tiled=True),
        lax.all_to_all(send_gates, ("seq", "sub"), split_axis=0, concat_axis=0, tiled=True),
    )
    slots_in = experts * cap
    valid = recv_gates > 0
    counts = jnp.sum(valid.astype(jnp.int32), axis=1)
    offsets = jnp.cumsum(counts) - counts
    dest = jnp.where(
        valid, offsets[:, None] + jnp.arange(cap, dtype=jnp.int32)[None, :], slots_in
    ).reshape(-1)
    source_of = (
        jnp.full((slots_in + 1,), slots_in, jnp.int32)
        .at[dest]
        .set(jnp.arange(slots_in, dtype=jnp.int32))[:slots_in]
    )
    compact_rows = jnp.concatenate(
        [recv_rows.reshape(slots_in, D), jnp.zeros((1, D), jnp.bfloat16)], axis=0
    )[source_of]
    compact_gates = jnp.concatenate(
        [recv_gates.reshape(-1), jnp.zeros((1,), jnp.bfloat16)], axis=0
    )[source_of].astype(jnp.float32)
    filled = jnp.sum(counts)
    n_blocks = (filled + slots_in - 1) // slots_in
    w_gate = expert_gate[0]
    w_up = expert_up[0]
    w_down = expert_down[0]

    def expert_block(index, results):
        gate_proj = jnp.dot(compact_rows, w_gate, preferred_element_type=jnp.float32)
        up_proj = jnp.dot(compact_rows, w_up, preferred_element_type=jnp.float32)
        inner = (jax.nn.silu(gate_proj) * up_proj).astype(jnp.bfloat16)
        weighted = (
            jnp.dot(inner, w_down, preferred_element_type=jnp.float32) * compact_gates[:, None]
        )
        return weighted.astype(jnp.bfloat16)

    results = lax.fori_loop(0, n_blocks, expert_block, jnp.zeros((slots_in, D), jnp.bfloat16))
    returned = jnp.concatenate([results, jnp.zeros((1, D), jnp.bfloat16)], axis=0)[dest].reshape(
        experts, cap, D
    )
    back = lax.all_to_all(
        returned, ("seq", "sub"), split_axis=0, concat_axis=0, tiled=True
    ).reshape(slots_out, D)
    gathered = back[slot_of].reshape(tokens, topk, D).astype(jnp.float32)
    mixture = jnp.sum(gathered, axis=1)
    return (wide + mixture).astype(jnp.bfloat16)[None]


def solution(mesh):
    placed = (
        P(("grp", "sub"), "seq", None),
        P(("grp", "sub"), "seq", None),
        P(("grp", "sub"), "seq", None),
        P(("grp", "sub"), "seq", None),
        P("seq", None),
        P(),
        P(("grp", "sub"), "seq", None),
        P(("grp", "sub"), "seq", None),
        P(("seq", "sub"), None, None),
        P(("seq", "sub"), None, None),
        P(("seq", "sub"), None, None),
    )
    return jax.shard_map(
        per_device,
        mesh=mesh,
        in_specs=placed,
        out_specs=P(("grp", "sub"), "seq", None),
        check_vma=False,
    )
```

```python
import functools

import jax
import jax.numpy as jnp
from jax import lax
from jax.experimental import pallas as pl
from jax.experimental.pallas import tpu as pltpu
from jax.sharding import PartitionSpec as P

D = 2048
HD = 128
QH = 16
KVH = 2
MIB = 1024 * 1024


def attend_head(queries, keys_one, values_one, block):
    length = queries.shape[0]
    scale = 1.0 / queries.shape[1] ** 0.5
    pieces = []
    for part_index in range(length // block):
        stop = (part_index + 1) * block
        rows_here = queries[part_index * block : stop]
        scores = (
            jnp.einsum("qd,kd->qk", rows_here, keys_one[:stop], preferred_element_type=jnp.float32)
            * scale
        )
        row_pos = part_index * block + jnp.arange(block, dtype=jnp.int32)
        col_pos = jnp.arange(stop, dtype=jnp.int32)
        scores = jnp.where(row_pos[:, None] >= col_pos[None, :], scores, -1e30)
        peak = jnp.max(scores, axis=1, keepdims=True)
        weights = jnp.exp(scores - peak)
        probs = (weights / jnp.sum(weights, axis=1, keepdims=True)).astype(jnp.bfloat16)
        pieces.append(
            jnp.dot(probs, values_one[:stop], preferred_element_type=jnp.float32).astype(
                jnp.bfloat16
            )
        )
    return jnp.concatenate(pieces, axis=0)


def rank_in_expert(flat_ids, experts):
    items = flat_ids.shape[0]
    width = 128
    n_parts = items // width
    onehot = (
        (flat_ids[:, None] == jnp.arange(experts, dtype=jnp.int32)[None, :])
        .astype(jnp.bfloat16)
        .reshape(n_parts, width, experts)
    )
    lower = (
        jnp.arange(width, dtype=jnp.int32)[:, None] > jnp.arange(width, dtype=jnp.int32)[None, :]
    ).astype(jnp.bfloat16)
    within = jnp.einsum("ij,bje->bie", lower, onehot, preferred_element_type=jnp.float32)
    part_counts = jnp.sum(onehot.astype(jnp.float32), axis=1)
    earlier = jnp.cumsum(part_counts, axis=0) - part_counts
    ranks = jnp.sum((within + earlier[:, None, :]) * onehot.astype(jnp.float32), axis=2)
    return ranks.reshape(items).astype(jnp.int32)


def pack_kernel(chip_ref, query_ref, key_ref, value_ref, id_ref, gate_ref, away_ref, here_kv_ref, away_kv_ref):
    tokens = query_ref.shape[0]
    head_size = key_ref.shape[1] // 2
    chip_width = away_ref.shape[1]
    chip = chip_ref[0]
    experts = here_kv_ref.shape[0] - tokens
    away_ref[...] = query_ref[:, pl.ds(pl.multiple_of((1 - chip) * chip_width, chip_width), chip_width)]
    number = lax.broadcasted_iota(jnp.int32, (experts, tokens), 0)
    table = jnp.zeros((experts, tokens), jnp.float32)
    for choice in range(id_ref.shape[0]):
        table += jnp.where(
            number == id_ref[choice : choice + 1, :],
            gate_ref[choice : choice + 1, :].astype(jnp.float32),
            0.0,
        )
    for out_ref, head in ((here_kv_ref, chip), (away_kv_ref, 1 - chip)):
        columns = pl.ds(pl.multiple_of(head * head_size, head_size), head_size)
        out_ref[0:tokens, 0:head_size] = key_ref[:, columns]
        out_ref[0:tokens, head_size:] = value_ref[:, columns]
        out_ref[tokens:, 0:head_size] = table.astype(jnp.bfloat16)
        out_ref[tokens:, head_size:] = jnp.zeros((experts, head_size), jnp.bfloat16)


def pack(chip, queries, keys, values, ids, gates, experts):
    tokens, width = queries.shape
    kv = jax.ShapeDtypeStruct((tokens + experts, keys.shape[1]), jnp.bfloat16)
    return pl.pallas_call(
        pack_kernel,
        in_specs=[pl.BlockSpec(memory_space=pltpu.SMEM)]
        + [pl.BlockSpec(memory_space=pltpu.VMEM)] * 5,
        out_specs=[pl.BlockSpec(memory_space=pltpu.VMEM)] * 3,
        out_shape=[jax.ShapeDtypeStruct((tokens, width // 2), jnp.bfloat16), kv, kv],
        compiler_params=pltpu.CompilerParams(vmem_limit_bytes=60 * MIB),
    )(chip.reshape(1), queries, keys, values, ids, gates)


def attend_kernel(place_ref, query_ref, *refs, scale):
    kv_refs, refs = refs[:4], refs[4:]
    base_refs = refs[: len(refs) - 13]
    w_own_ref, w_other_ref, out_ref, quad_ref, keys, values, heads = refs[-13:-6]
    w_own, w_other, stacked, scores, probs, done = refs[-6:]
    fetches = [
        pltpu.make_async_copy(w_own_ref, w_own, done.at[0]),
        pltpu.make_async_copy(w_other_ref, w_other, done.at[1]),
    ]
    for fetch in fetches:
        fetch.start()
    rows = keys.shape[0] // 4
    head_size = keys.shape[1]
    core = place_ref[0]
    query_start = pl.multiple_of(place_ref[1], head_size)
    row_pos = place_ref[2] * rows + lax.broadcasted_iota(jnp.int32, (rows, 1), 0)
    lane = lax.broadcasted_iota(jnp.int32, (1, rows), 1)
    col_pos = jnp.concatenate([place_ref[3 + part] * rows + lane for part in range(4)], axis=1)
    allowed = row_pos >= col_pos
    for part, kv_ref in enumerate(kv_refs):
        keys[part * rows : (part + 1) * rows, :] = kv_ref[0:rows, 0:head_size]
        values[part * rows : (part + 1) * rows, :] = kv_ref[0:rows, head_size:]
        quad_ref[:, part * rows : (part + 1) * rows] = kv_ref[rows:, 0:rows]
    key_block = keys[...]
    value_block = values[...]
    count = heads.shape[1] // head_size
    for head in range(count):
        stacked[head * rows : (head + 1) * rows, :] = query_ref[
            :, pl.ds(query_start + head * head_size, head_size)
        ]
    scores[...] = lax.dot_general(
        stacked[...], key_block, (((1,), (1,)), ((), ())), preferred_element_type=jnp.float32
    )
    for head in range(count):
        part = slice(head * rows, (head + 1) * rows)
        score = jnp.where(allowed, scores[part, :] * scale, -1e30)
        weights = jnp.exp(score - jnp.max(score, axis=1, keepdims=True))
        probs[part, :] = (weights * (1.0 / jnp.sum(weights, axis=1, keepdims=True))).astype(
            jnp.bfloat16
        )
    mixed = jnp.dot(probs[...], value_block, preferred_element_type=jnp.float32)
    for head in range(count):
        heads[:, head * head_size : (head + 1) * head_size] = mixed[
            head * rows : (head + 1) * rows
        ].astype(jnp.bfloat16)
    for fetch in fetches:
        fetch.wait()
    half = heads.shape[1] // 2
    own = heads[:, pl.ds(pl.multiple_of(core * half, half), half)]
    other = heads[:, pl.ds(pl.multiple_of((1 - core) * half, half), half)]
    total = jnp.dot(own, w_own[...], preferred_element_type=jnp.float32) + jnp.dot(
        other, w_other[...], preferred_element_type=jnp.float32
    )
    for base_ref in base_refs:
        total += base_ref[...].astype(jnp.float32)
    out_ref[...] = total.astype(out_ref.dtype)


def attend(place, queries, kv_parts, bases, w_own, w_other, dtype):
    tokens = queries.shape[0]
    width = w_own.shape[1]
    chip_width = 2 * w_own.shape[0]
    return pl.pallas_call(
        functools.partial(attend_kernel, scale=1.0 / HD**0.5),
        in_specs=[pl.BlockSpec(memory_space=pltpu.SMEM)]
        + [pl.BlockSpec(memory_space=pltpu.VMEM)] * (5 + len(bases))
        + [pl.BlockSpec(memory_space=pl.ANY)] * 2,
        out_specs=[pl.BlockSpec(memory_space=pltpu.VMEM)] * 2,
        out_shape=[
            jax.ShapeDtypeStruct((tokens, width), dtype),
            jax.ShapeDtypeStruct((kv_parts[0].shape[0] - tokens, 4 * tokens), jnp.bfloat16),
        ],
        scratch_shapes=[
            pltpu.VMEM((4 * tokens, HD), jnp.bfloat16),
            pltpu.VMEM((4 * tokens, HD), jnp.bfloat16),
            pltpu.VMEM((tokens, chip_width), jnp.bfloat16),
            pltpu.VMEM(w_own.shape, jnp.bfloat16),
            pltpu.VMEM(w_other.shape, jnp.bfloat16),
            pltpu.VMEM((tokens * chip_width // HD, HD), jnp.bfloat16),
            pltpu.VMEM((tokens * chip_width // HD, 4 * tokens), jnp.float32),
            pltpu.VMEM((tokens * chip_width // HD, 4 * tokens), jnp.bfloat16),
            pltpu.SemaphoreType.DMA((2,)),
        ],
        compiler_params=pltpu.CompilerParams(vmem_limit_bytes=60 * MIB),
        cost_estimate=pl.CostEstimate(
            flops=16 * tokens * tokens * chip_width + 2 * tokens * chip_width * width,
            bytes_accessed=4 * w_own.size + 4 * tokens * width,
            transcendentals=4 * tokens * tokens * chip_width // HD,
        ),
    )(place, queries, *kv_parts, *bases, w_own, w_other)


def norm_kernel(own_ref, other_ref, gain_ref, *refs):
    hidden_ref, normed_ref = refs[-2:]
    hidden = (own_ref[...] + other_ref[...].astype(jnp.float32)).astype(jnp.bfloat16)
    hidden_ref[...] = hidden
    wide = hidden.astype(jnp.float32)
    normed_ref[...] = (
        wide
        * lax.rsqrt(jnp.mean(wide * wide, axis=1, keepdims=True) + 1e-06)
        * gain_ref[...].astype(jnp.float32)
    ).astype(jnp.bfloat16)


def add_and_norm(own, other, gain, present):
    return pl.pallas_call(
        norm_kernel,
        in_specs=[pl.BlockSpec(memory_space=pltpu.VMEM)] * 3
        + [pl.BlockSpec(memory_space=pl.ANY)] * len(present),
        out_specs=[pl.BlockSpec(memory_space=pltpu.VMEM)] * 2,
        out_shape=[jax.ShapeDtypeStruct(own.shape, jnp.bfloat16)] * 2,
        compiler_params=pltpu.CompilerParams(vmem_limit_bytes=60 * MIB),
    )(own, other, gain, *present)


def pass_kernel(*refs):
    del refs


def meet(arrays, flops):
    return pl.pallas_call(
        pass_kernel,
        in_specs=[pl.BlockSpec(memory_space=pl.ANY)] * len(arrays),
        out_specs=[pl.BlockSpec(memory_space=pl.ANY)] * len(arrays),
        out_shape=[jax.ShapeDtypeStruct(array.shape, array.dtype) for array in arrays],
        input_output_aliases={index: index for index in range(len(arrays))},
    )(*arrays)


def pass_kernel(*refs):
    del refs


def meet(arrays, flops):
    return pl.pallas_call(
        pass_kernel,
        in_specs=[pl.BlockSpec(memory_space=pl.ANY)] * len(arrays),
        out_specs=[pl.BlockSpec(memory_space=pl.ANY)] * len(arrays),
        out_shape=[jax.ShapeDtypeStruct(array.shape, array.dtype) for array in arrays],
        input_output_aliases={index: index for index in range(len(arrays))},
        compiler_params=pltpu.CompilerParams(vmem_limit_bytes=MIB),
        cost_estimate=pl.CostEstimate(flops=flops, bytes_accessed=0, transcendentals=0),
    )(*arrays)


def experts_kernel(mine_ref, quad_ref, *refs, cap, pieces):
    row_refs = []
    for count in pieces:
        row_refs.append(refs[:count])
        refs = refs[count:]
    w_gate_ref, w_up_ref, w_down_ref, own_ref, across_ref, other_ref, packed = refs
    tokens = row_refs[0][0].shape[0]
    quad = quad_ref[...].astype(jnp.float32)
    expert = lax.broadcasted_iota(jnp.int32, quad.shape, 0)
    line = jnp.sum(jnp.where(expert == mine_ref[0], quad, 0.0), axis=0, keepdims=True)
    gates = jnp.concatenate(
        [line[:, block * tokens : (block + 1) * tokens] for block in range(4)], axis=0
    )
    named = gates > 0
    before = (
        lax.broadcasted_iota(jnp.int32, (tokens, tokens), 0)
        < lax.broadcasted_iota(jnp.int32, (tokens, tokens), 1)
    ).astype(jnp.bfloat16)
    rank = jnp.dot(
        named.astype(jnp.float32).astype(jnp.bfloat16), before, preferred_element_type=jnp.float32
    )
    slot = jnp.where(named, rank.astype(jnp.int32), -1)
    slots = lax.broadcasted_iota(jnp.int32, (cap, tokens), 0)
    picks = []
    weights = []
    for block in range(4):
        chosen = slots == slot[block : block + 1, :]
        picks.append(jnp.where(chosen, 1.0, 0.0).astype(jnp.bfloat16))
        weights.append(
            jnp.sum(jnp.where(chosen, gates[block : block + 1, :], 0.0), axis=1, keepdims=True)
        )
        start = 0
        for row_ref in row_refs[block]:
            stop = start + row_ref.shape[1]
            packed[block * cap : (block + 1) * cap, start:stop] = jnp.dot(
                picks[block], row_ref[...], preferred_element_type=jnp.float32
            ).astype(jnp.bfloat16)
            start = stop
    rows = packed[...]
    gate_proj = jnp.dot(rows, w_gate_ref[...], preferred_element_type=jnp.float32)
    up_proj = jnp.dot(rows, w_up_ref[...], preferred_element_type=jnp.float32)
    inner = (gate_proj / (1.0 + jnp.exp(-gate_proj)) * up_proj).astype(jnp.bfloat16)
    result = jnp.dot(inner, w_down_ref[...], preferred_element_type=jnp.float32)
    targets = (
        own_ref.at[...],
        other_ref.at[0:tokens],
        across_ref.at[...],
        other_ref.at[tokens : 2 * tokens],
    )
    for block in range(4):
        part = (result[block * cap : (block + 1) * cap, :] * weights[block]).astype(jnp.bfloat16)
        targets[block][...] = lax.dot_general(
            picks[block], part, (((0,), (0,)), ((), ())), preferred_element_type=jnp.float32
        ).astype(jnp.bfloat16)


def experts_on_rows(mine, quad, row_blocks, w_gate, w_up, w_down, cap):
    tokens = row_blocks[0][0].shape[0]
    width, hidden_units = w_gate.shape
    pieces = tuple(len(block) for block in row_blocks)
    return pl.pallas_call(
        functools.partial(experts_kernel, cap=cap, pieces=pieces),
        in_specs=[pl.BlockSpec(memory_space=pltpu.SMEM)]
        + [pl.BlockSpec(memory_space=pltpu.VMEM)] * (4 + sum(pieces)),
        out_specs=[pl.BlockSpec(memory_space=pltpu.VMEM)] * 3,
        out_shape=[
            jax.ShapeDtypeStruct((tokens, width), jnp.bfloat16),
            jax.ShapeDtypeStruct((tokens, width), jnp.bfloat16),
            jax.ShapeDtypeStruct((2 * tokens, width), jnp.bfloat16),
        ],
        scratch_shapes=[pltpu.VMEM((4 * cap, width), jnp.bfloat16)],
        compiler_params=pltpu.CompilerParams(vmem_limit_bytes=28 * MIB),
        cost_estimate=pl.CostEstimate(
            flops=24 * cap * width * hidden_units,
            bytes_accessed=16 * tokens * width + 6 * width * hidden_units,
            transcendentals=4 * cap * hidden_units,
        ),
    )(mine.reshape(1), quad, *sum(row_blocks, []), w_gate, w_up, w_down)


def gathered_plan(
    query_rows,
    key_rows,
    value_rows,
    residual_in,
    out_proj,
    norm_gain,
    expert_ids,
    gate_weights,
    expert_gate,
    expert_up,
    expert_down,
    cap,
):
    n_seq = lax.axis_size("seq")
    n_sub = lax.axis_size("sub")
    experts = n_seq * n_sub
    place = lax.axis_index("seq")
    core = place % 2
    chip = place // 2
    twin = [(index, index ^ 1) for index in range(n_seq)]
    across = [(index, (index + 2) % n_seq) for index in range(n_seq)]
    diagonal = [(index, (index ^ 1) ^ 2) for index in range(n_seq)]
    order = [0] + list(range(1, n_sub, 2)) + list(reversed(range(2, n_sub, 2)))

    def ring(steps):
        return [(order[at], order[(at + steps) % n_sub]) for at in range(n_sub)]

    queries = query_rows[0]
    chip_width = queries.shape[1] // 2

    tokens = queries.shape[0]
    queries_away, kv_here, kv_away = pack(
        chip,
        queries,
        key_rows[0],
        value_rows[0],
        expert_ids[0].T,
        gate_weights[0].T,
        experts,
    )
    incoming = lax.ppermute(queries_away, "seq", across)
    kv_parts = [
        kv_here,
        lax.ppermute(kv_here, "seq", twin),
        lax.ppermute(kv_away, "seq", across),
        lax.ppermute(kv_away, "seq", diagonal),
    ]
    w_other = lax.ppermute(out_proj, "seq", twin)
    columns = [place, place ^ 1, place ^ 2, place ^ 3]

    def place_of(query_start, row_block):
        return jnp.stack([core, query_start, row_block] + columns).astype(jnp.int32)

    sent, quad = attend(
        place_of(0 * place, place ^ 2), incoming, kv_parts, [], out_proj, w_other, jnp.bfloat16
    )
    projected_across = lax.ppermute(sent, "seq", across)
    projected, _ = attend(
        place_of(chip * chip_width, place),
        queries,
        kv_parts,
        [residual_in[0]],
        out_proj,
        w_other,
        jnp.float32,
    )
    quads = [lax.ppermute(quad, "sub", ring(steps)) for steps in range(1, n_sub)]
    hidden, normed = add_and_norm(projected, projected_across, norm_gain[None], quads)

    last = n_sub - 1
    mine = place * n_sub + lax.axis_index("sub")

    held = {("row", 0): normed, ("quad", 0): quad}
    held.update({("quad", steps): moved for steps, moved in enumerate(quads, 1)})
    half = normed.shape[1] // 2
    ways = {"across": ("seq", across), "twin": ("seq", twin), "on": ("sub", ring(1))}

    def move(array, way):
        return lax.ppermute(array, *ways[way])

    def experts_of(step):
        held["own", step], held["part", step], other = experts_on_rows(
            mine,
            held["quad", step],
            [
                [held[name, step]] if (name, step) in held else list(held[name, step, "pieces"])
                for name in ("row", "twin", "across", "diagonal")
            ],
            expert_gate[0],
            expert_up[0],
            expert_down[0],
            cap,
        )
        return other

    def twin_sum(step):
        met = move(held["other", step], "twin")
        held["met", step] = met[:tokens]
        return (held["part", step].astype(jnp.float32) + met[tokens:].astype(jnp.float32)).astype(
            jnp.bfloat16
        )

    def sum_of(step, more):
        parts = [held["own", step], held["met", step], held["back", step]] + more
        if held["back", step].shape[1] == half:
            left = sum(part[:, :half].astype(jnp.float32) for part in parts)
            right = sum(part[:, half:].astype(jnp.float32) for part in parts if part.shape[1] > half)
            return jnp.concatenate([left, right], axis=1)
        return sum(part.astype(jnp.float32) for part in parts)

    for turn in range(1, n_sub + 5):
        now = {}
        step = turn - 1
        if step < last:
            now["across", step] = move(held["row", step], "across")
            now["row", step + 1] = move(held["row", step], "on")
        if step == last:
            now["half", 0] = move(held["row", step][:, :half], "across")
            now["half", 1] = move(held["across", step - 1][:, half:], "on")
        if step <= last:
            held["twin", step] = move(held["row", step], "twin")
        step = turn - 4 if turn < n_sub + 4 else 0
        if 1 <= step <= last or turn == n_sub + 4:
            if step == 1 and last > 1:
                now["back", step] = move(held["away", step][:, :half], "across")
                now["late", step] = move(held["away", step][:, half:], "on")
            elif step == 2:
                away = held["away", step]
                added = away[:, half:].astype(jnp.float32) + held["late", 1].astype(jnp.float32)
                now["back", step] = move(
                    jnp.concatenate([away[:, :half], added.astype(jnp.bfloat16)], axis=1), "across"
                )
            else:
                now["back", step] = move(held["away", step], "across")
        step = turn - 5
        if 1 <= step <= last:
            more = [held["sum", step - 1]] if step > 1 else []
            now["sum", step] = move(sum_of(step, more).astype(jnp.bfloat16), "on")
        step = turn - 2
        if 0 <= step < last:
            held["diagonal", step] = move(held["across", step], "twin")
        if step == last:
            held["across", step, "pieces"] = [held["half", side] for side in range(2)]
            held["diagonal", step, "pieces"] = [
                move(held["half", side], "twin") for side in range(2)
            ]
        if 1 <= step <= last:
            now["other", step] = experts_of(step)
        if turn == n_sub + 2:
            now["other", 0] = experts_of(0)
        step = turn - 3 if turn < n_sub + 3 else 0
        if 1 <= step <= last or turn == n_sub + 3:
            now["away", step] = twin_sum(step)
        if turn < n_sub + 4:
            wait = 10_000_000_000 if turn <= 2 else 0
            now = dict(zip(now.keys(), meet(list(now.values()), wait)))
        held.update(now)
    total = hidden.astype(jnp.float32) + sum_of(0, [held["sum", last]])
    return total.astype(jnp.bfloat16)[None]


def per_device(
    query_rows,
    key_rows,
    value_rows,
    residual_in,
    out_proj,
    norm_gain,
    expert_ids,
    gate_weights,
    expert_gate,
    expert_up,
    expert_down,
):
    tokens = query_rows.shape[1]
    n_seq = lax.axis_size("seq")
    n_sub = lax.axis_size("sub")
    experts = n_seq * n_sub
    topk = expert_ids.shape[2]
    cap = max(2, (5 * tokens * topk + 4 * experts - 1) // (4 * experts))
    if n_seq == 2 * KVH and KVH == 2 and tokens == HD and n_sub > 2 and experts <= 2 * topk and cap % 16 == 0:
        return gathered_plan(
            query_rows,
            key_rows,
            value_rows,
            residual_in,
            out_proj,
            norm_gain,
            expert_ids,
            gate_weights,
            expert_gate,
            expert_up,
            expert_down,
            cap,
        )
    heads_here = QH // n_seq
    group = QH // KVH
    query_local = lax.all_to_all(query_rows, "seq", split_axis=2, concat_axis=1, tiled=True)
    key_full, value_full = (
        lax.all_gather(key_rows, "seq", axis=1, tiled=True),
        lax.all_gather(value_rows, "seq", axis=1, tiled=True),
    )
    first_head = lax.axis_index("seq") * heads_here
    key_list = []
    value_list = []
    for head in range(heads_here):
        kv_start = (first_head + head) // group * HD
        key_list.append(lax.dynamic_slice_in_dim(key_full[0], kv_start, HD, 1))
        value_list.append(lax.dynamic_slice_in_dim(value_full[0], kv_start, HD, 1))
    length = query_local.shape[1]
    block = min(length, max(512, length // 8))
    outputs = [
        attend_head(
            query_local[0, :, head * HD : (head + 1) * HD], key_list[head], value_list[head], block
        )
        for head in range(heads_here)
    ]
    head_block = jnp.concatenate(outputs, axis=1)[None]
    attended = lax.all_to_all(head_block, "seq", split_axis=1, concat_axis=2, tiled=True)[0]
    projected = jnp.dot(
        attended,
        lax.all_gather(out_proj, "seq", axis=0, tiled=True),
        preferred_element_type=jnp.float32,
    )
    hidden = (residual_in[0].astype(jnp.float32) + projected).astype(jnp.bfloat16)
    wide = hidden.astype(jnp.float32)
    normed = (
        wide
        * lax.rsqrt(jnp.mean(wide * wide, axis=1, keepdims=True) + 1e-06)
        * norm_gain.astype(jnp.float32)
    ).astype(jnp.bfloat16)
    flat_ids = expert_ids[0].reshape(-1)
    items = flat_ids.shape[0]
    ranks = rank_in_expert(flat_ids, experts)
    slot_of = flat_ids * cap + ranks
    slots_out = experts * cap
    item_of_slot = (
        jnp.full((slots_out,), items, jnp.int32).at[slot_of].set(jnp.arange(items, dtype=jnp.int32))
    )
    padded_rows = jnp.concatenate([normed, jnp.zeros((1, D), jnp.bfloat16)], axis=0)
    padded_gates = jnp.concatenate(
        [gate_weights[0].reshape(-1), jnp.zeros((1,), jnp.bfloat16)], axis=0
    )
    token_of_slot = jnp.where(item_of_slot < items, item_of_slot // topk, tokens)
    send_rows = padded_rows[token_of_slot].reshape(experts, cap, D)
    send_gates = padded_gates[item_of_slot].reshape(experts, cap)
    recv_rows, recv_gates = (
        lax.all_to_all(send_rows, ("seq", "sub"), split_axis=0, concat_axis=0, tiled=True),
        lax.all_to_all(send_gates, ("seq", "sub"), split_axis=0, concat_axis=0, tiled=True),
    )
    slots_in = experts * cap
    valid = recv_gates > 0
    counts = jnp.sum(valid.astype(jnp.int32), axis=1)
    offsets = jnp.cumsum(counts) - counts
    dest = jnp.where(
        valid, offsets[:, None] + jnp.arange(cap, dtype=jnp.int32)[None, :], slots_in
    ).reshape(-1)
    source_of = (
        jnp.full((slots_in + 1,), slots_in, jnp.int32)
        .at[dest]
        .set(jnp.arange(slots_in, dtype=jnp.int32))[:slots_in]
    )
    compact_rows = jnp.concatenate(
        [recv_rows.reshape(slots_in, D), jnp.zeros((1, D), jnp.bfloat16)], axis=0
    )[source_of]
    compact_gates = jnp.concatenate(
        [recv_gates.reshape(-1), jnp.zeros((1,), jnp.bfloat16)], axis=0
    )[source_of].astype(jnp.float32)
    filled = jnp.sum(counts)
    n_blocks = (filled + slots_in - 1) // slots_in
    w_gate = expert_gate[0]
    w_up = expert_up[0]
    w_down = expert_down[0]

    def expert_block(index, results):
        gate_proj = jnp.dot(compact_rows, w_gate, preferred_element_type=jnp.float32)
        up_proj = jnp.dot(compact_rows, w_up, preferred_element_type=jnp.float32)
        inner = (jax.nn.silu(gate_proj) * up_proj).astype(jnp.bfloat16)
        weighted = (
            jnp.dot(inner, w_down, preferred_element_type=jnp.float32) * compact_gates[:, None]
        )
        return weighted.astype(jnp.bfloat16)

    results = lax.fori_loop(0, n_blocks, expert_block, jnp.zeros((slots_in, D), jnp.bfloat16))
    returned = jnp.concatenate([results, jnp.zeros((1, D), jnp.bfloat16)], axis=0)[dest].reshape(
        experts, cap, D
    )
    back = lax.all_to_all(
        returned, ("seq", "sub"), split_axis=0, concat_axis=0, tiled=True
    ).reshape(slots_out, D)
    gathered = back[slot_of].reshape(tokens, topk, D).astype(jnp.float32)
    mixture = jnp.sum(gathered, axis=1)
    return (wide + mixture).astype(jnp.bfloat16)[None]


def solution(mesh):
    placed = (
        P(("grp", "sub"), "seq", None),
        P(("grp", "sub"), "seq", None),
        P(("grp", "sub"), "seq", None),
        P(("grp", "sub"), "seq", None),
        P("seq", None),
        P(),
        P(("grp", "sub"), "seq", None),
        P(("grp", "sub"), "seq", None),
        P(("seq", "sub"), None, None),
        P(("seq", "sub"), None, None),
        P(("seq", "sub"), None, None),
    )
    return jax.shard_map(
        per_device,
        mesh=mesh,
        in_specs=placed,
        out_specs=P(("grp", "sub"), "seq", None),
        check_vma=False,
    )
```

```python
import functools

import jax
import jax.numpy as jnp
from jax import lax
from jax.experimental import pallas as pl
from jax.experimental.pallas import tpu as pltpu
from jax.sharding import PartitionSpec as P

D = 2048
HD = 128
QH = 16
KVH = 2
MIB = 1024 * 1024


def attend_head(queries, keys_one, values_one, block):
    length = queries.shape[0]
    scale = 1.0 / queries.shape[1] ** 0.5
    pieces = []
    for part_index in range(length // block):
        stop = (part_index + 1) * block
        rows_here = queries[part_index * block : stop]
        scores = (
            jnp.einsum("qd,kd->qk", rows_here, keys_one[:stop], preferred_element_type=jnp.float32)
            * scale
        )
        row_pos = part_index * block + jnp.arange(block, dtype=jnp.int32)
        col_pos = jnp.arange(stop, dtype=jnp.int32)
        scores = jnp.where(row_pos[:, None] >= col_pos[None, :], scores, -1e30)
        peak = jnp.max(scores, axis=1, keepdims=True)
        weights = jnp.exp(scores - peak)
        probs = (weights / jnp.sum(weights, axis=1, keepdims=True)).astype(jnp.bfloat16)
        pieces.append(
            jnp.dot(probs, values_one[:stop], preferred_element_type=jnp.float32).astype(
                jnp.bfloat16
            )
        )
    return jnp.concatenate(pieces, axis=0)


def rank_in_expert(flat_ids, experts):
    items = flat_ids.shape[0]
    width = 128
    n_parts = items // width
    onehot = (
        (flat_ids[:, None] == jnp.arange(experts, dtype=jnp.int32)[None, :])
        .astype(jnp.bfloat16)
        .reshape(n_parts, width, experts)
    )
    lower = (
        jnp.arange(width, dtype=jnp.int32)[:, None] > jnp.arange(width, dtype=jnp.int32)[None, :]
    ).astype(jnp.bfloat16)
    within = jnp.einsum("ij,bje->bie", lower, onehot, preferred_element_type=jnp.float32)
    part_counts = jnp.sum(onehot.astype(jnp.float32), axis=1)
    earlier = jnp.cumsum(part_counts, axis=0) - part_counts
    ranks = jnp.sum((within + earlier[:, None, :]) * onehot.astype(jnp.float32), axis=2)
    return ranks.reshape(items).astype(jnp.int32)


def pack_kernel(chip_ref, query_ref, key_ref, value_ref, id_ref, gate_ref, away_ref, here_kv_ref, away_kv_ref):
    tokens = query_ref.shape[0]
    head_size = key_ref.shape[1] // 2
    chip_width = away_ref.shape[1]
    chip = chip_ref[0]
    experts = here_kv_ref.shape[0] - tokens
    away_ref[...] = query_ref[:, pl.ds(pl.multiple_of((1 - chip) * chip_width, chip_width), chip_width)]
    number = lax.broadcasted_iota(jnp.int32, (experts, tokens), 0)
    table = jnp.zeros((experts, tokens), jnp.float32)
    for choice in range(id_ref.shape[0]):
        table += jnp.where(
            number == id_ref[choice : choice + 1, :],
            gate_ref[choice : choice + 1, :].astype(jnp.float32),
            0.0,
        )
    for out_ref, head in ((here_kv_ref, chip), (away_kv_ref, 1 - chip)):
        columns = pl.ds(pl.multiple_of(head * head_size, head_size), head_size)
        out_ref[0:tokens, 0:head_size] = key_ref[:, columns]
        out_ref[0:tokens, head_size:] = value_ref[:, columns]
        out_ref[tokens:, 0:head_size] = table.astype(jnp.bfloat16)
        out_ref[tokens:, head_size:] = jnp.zeros((experts, head_size), jnp.bfloat16)


def pack(chip, queries, keys, values, ids, gates, experts):
    tokens, width = queries.shape
    kv = jax.ShapeDtypeStruct((tokens + experts, keys.shape[1]), jnp.bfloat16)
    return pl.pallas_call(
        pack_kernel,
        in_specs=[pl.BlockSpec(memory_space=pltpu.SMEM)]
        + [pl.BlockSpec(memory_space=pltpu.VMEM)] * 5,
        out_specs=[pl.BlockSpec(memory_space=pltpu.VMEM)] * 3,
        out_shape=[jax.ShapeDtypeStruct((tokens, width // 2), jnp.bfloat16), kv, kv],
        compiler_params=pltpu.CompilerParams(vmem_limit_bytes=60 * MIB),
    )(chip.reshape(1), queries, keys, values, ids, gates)


def attend_kernel(place_ref, query_ref, *refs, scale):
    kv_refs, refs = refs[:4], refs[4:]
    base_refs = refs[: len(refs) - 13]
    w_own_ref, w_other_ref, out_ref, quad_ref, keys, values, heads = refs[-13:-6]
    w_own, w_other, stacked, scores, probs, done = refs[-6:]
    fetches = [
        pltpu.make_async_copy(w_own_ref, w_own, done.at[0]),
        pltpu.make_async_copy(w_other_ref, w_other, done.at[1]),
    ]
    for fetch in fetches:
        fetch.start()
    rows = keys.shape[0] // 4
    head_size = keys.shape[1]
    core = place_ref[0]
    query_start = pl.multiple_of(place_ref[1], head_size)
    row_pos = place_ref[2] * rows + lax.broadcasted_iota(jnp.int32, (rows, 1), 0)
    lane = lax.broadcasted_iota(jnp.int32, (1, rows), 1)
    col_pos = jnp.concatenate([place_ref[3 + part] * rows + lane for part in range(4)], axis=1)
    allowed = row_pos >= col_pos
    for part, kv_ref in enumerate(kv_refs):
        keys[part * rows : (part + 1) * rows, :] = kv_ref[0:rows, 0:head_size]
        values[part * rows : (part + 1) * rows, :] = kv_ref[0:rows, head_size:]
        quad_ref[:, part * rows : (part + 1) * rows] = kv_ref[rows:, 0:rows]
    key_block = keys[...]
    value_block = values[...]
    count = heads.shape[1] // head_size
    for head in range(count):
        stacked[head * rows : (head + 1) * rows, :] = query_ref[
            :, pl.ds(query_start + head * head_size, head_size)
        ]
    scores[...] = lax.dot_general(
        stacked[...], key_block, (((1,), (1,)), ((), ())), preferred_element_type=jnp.float32
    )
    for head in range(count):
        part = slice(head * rows, (head + 1) * rows)
        score = jnp.where(allowed, scores[part, :] * scale, -1e30)
        weights = jnp.exp(score - jnp.max(score, axis=1, keepdims=True))
        probs[part, :] = (weights * (1.0 / jnp.sum(weights, axis=1, keepdims=True))).astype(
            jnp.bfloat16
        )
    mixed = jnp.dot(probs[...], value_block, preferred_element_type=jnp.float32)
    for head in range(count):
        heads[:, head * head_size : (head + 1) * head_size] = mixed[
            head * rows : (head + 1) * rows
        ].astype(jnp.bfloat16)
    for fetch in fetches:
        fetch.wait()
    half = heads.shape[1] // 2
    own = heads[:, pl.ds(pl.multiple_of(core * half, half), half)]
    other = heads[:, pl.ds(pl.multiple_of((1 - core) * half, half), half)]
    total = jnp.dot(own, w_own[...], preferred_element_type=jnp.float32) + jnp.dot(
        other, w_other[...], preferred_element_type=jnp.float32
    )
    for base_ref in base_refs:
        total += base_ref[...].astype(jnp.float32)
    out_ref[...] = total.astype(out_ref.dtype)


def attend(place, queries, kv_parts, bases, w_own, w_other, dtype):
    tokens = queries.shape[0]
    width = w_own.shape[1]
    chip_width = 2 * w_own.shape[0]
    return pl.pallas_call(
        functools.partial(attend_kernel, scale=1.0 / HD**0.5),
        in_specs=[pl.BlockSpec(memory_space=pltpu.SMEM)]
        + [pl.BlockSpec(memory_space=pltpu.VMEM)] * (5 + len(bases))
        + [pl.BlockSpec(memory_space=pl.ANY)] * 2,
        out_specs=[pl.BlockSpec(memory_space=pltpu.VMEM)] * 2,
        out_shape=[
            jax.ShapeDtypeStruct((tokens, width), dtype),
            jax.ShapeDtypeStruct((kv_parts[0].shape[0] - tokens, 4 * tokens), jnp.bfloat16),
        ],
        scratch_shapes=[
            pltpu.VMEM((4 * tokens, HD), jnp.bfloat16),
            pltpu.VMEM((4 * tokens, HD), jnp.bfloat16),
            pltpu.VMEM((tokens, chip_width), jnp.bfloat16),
            pltpu.VMEM(w_own.shape, jnp.bfloat16),
            pltpu.VMEM(w_other.shape, jnp.bfloat16),
            pltpu.VMEM((tokens * chip_width // HD, HD), jnp.bfloat16),
            pltpu.VMEM((tokens * chip_width // HD, 4 * tokens), jnp.float32),
            pltpu.VMEM((tokens * chip_width // HD, 4 * tokens), jnp.bfloat16),
            pltpu.SemaphoreType.DMA((2,)),
        ],
        compiler_params=pltpu.CompilerParams(vmem_limit_bytes=60 * MIB),
        cost_estimate=pl.CostEstimate(
            flops=16 * tokens * tokens * chip_width + 2 * tokens * chip_width * width,
            bytes_accessed=4 * w_own.size + 4 * tokens * width,
            transcendentals=4 * tokens * tokens * chip_width // HD,
        ),
    )(place, queries, *kv_parts, *bases, w_own, w_other)


def norm_kernel(own_ref, other_ref, gain_ref, *refs):
    hidden_ref, normed_ref = refs[-2:]
    hidden = (own_ref[...] + other_ref[...].astype(jnp.float32)).astype(jnp.bfloat16)
    hidden_ref[...] = hidden
    wide = hidden.astype(jnp.float32)
    normed_ref[...] = (
        wide
        * lax.rsqrt(jnp.mean(wide * wide, axis=1, keepdims=True) + 1e-06)
        * gain_ref[...].astype(jnp.float32)
    ).astype(jnp.bfloat16)


def add_and_norm(own, other, gain, present):
    return pl.pallas_call(
        norm_kernel,
        in_specs=[pl.BlockSpec(memory_space=pltpu.VMEM)] * 3
        + [pl.BlockSpec(memory_space=pl.ANY)] * len(present),
        out_specs=[pl.BlockSpec(memory_space=pltpu.VMEM)] * 2,
        out_shape=[jax.ShapeDtypeStruct(own.shape, jnp.bfloat16)] * 2,
        compiler_params=pltpu.CompilerParams(vmem_limit_bytes=60 * MIB),
    )(own, other, gain, *present)


def pass_kernel(*refs):
    del refs


def meet(arrays, flops):
    return pl.pallas_call(
        pass_kernel,
        in_specs=[pl.BlockSpec(memory_space=pl.ANY)] * len(arrays),
        out_specs=[pl.BlockSpec(memory_space=pl.ANY)] * len(arrays),
        out_shape=[jax.ShapeDtypeStruct(array.shape, array.dtype) for array in arrays],
        input_output_aliases={index: index for index in range(len(arrays))},
    )(*arrays)


def pass_kernel(*refs):
    del refs


def meet(arrays, flops):
    return pl.pallas_call(
        pass_kernel,
        in_specs=[pl.BlockSpec(memory_space=pl.ANY)] * len(arrays),
        out_specs=[pl.BlockSpec(memory_space=pl.ANY)] * len(arrays),
        out_shape=[jax.ShapeDtypeStruct(array.shape, array.dtype) for array in arrays],
        input_output_aliases={index: index for index in range(len(arrays))},
        compiler_params=pltpu.CompilerParams(vmem_limit_bytes=MIB),
        cost_estimate=pl.CostEstimate(flops=flops, bytes_accessed=0, transcendentals=0),
    )(*arrays)


def experts_kernel(mine_ref, quad_ref, *refs, cap, pieces):
    row_refs = []
    for count in pieces:
        row_refs.append(refs[:count])
        refs = refs[count:]
    w_gate_ref, w_up_ref, w_down_ref, own_ref, across_ref, other_ref, packed = refs
    tokens = row_refs[0][0].shape[0]
    quad = quad_ref[...].astype(jnp.float32)
    expert = lax.broadcasted_iota(jnp.int32, quad.shape, 0)
    line = jnp.sum(jnp.where(expert == mine_ref[0], quad, 0.0), axis=0, keepdims=True)
    gates = jnp.concatenate(
        [line[:, block * tokens : (block + 1) * tokens] for block in range(4)], axis=0
    )
    named = gates > 0
    before = (
        lax.broadcasted_iota(jnp.int32, (tokens, tokens), 0)
        < lax.broadcasted_iota(jnp.int32, (tokens, tokens), 1)
    ).astype(jnp.bfloat16)
    rank = jnp.dot(
        named.astype(jnp.float32).astype(jnp.bfloat16), before, preferred_element_type=jnp.float32
    )
    slot = jnp.where(named, rank.astype(jnp.int32), -1)
    slots = lax.broadcasted_iota(jnp.int32, (cap, tokens), 0)
    picks = []
    weights = []
    for block in range(4):
        chosen = slots == slot[block : block + 1, :]
        picks.append(jnp.where(chosen, 1.0, 0.0).astype(jnp.bfloat16))
        weights.append(
            jnp.sum(jnp.where(chosen, gates[block : block + 1, :], 0.0), axis=1, keepdims=True)
        )
        start = 0
        for row_ref in row_refs[block]:
            stop = start + row_ref.shape[1]
            packed[block * cap : (block + 1) * cap, start:stop] = jnp.dot(
                picks[block], row_ref[...], preferred_element_type=jnp.float32
            ).astype(jnp.bfloat16)
            start = stop
    rows = packed[...]
    gate_proj = jnp.dot(rows, w_gate_ref[...], preferred_element_type=jnp.float32)
    up_proj = jnp.dot(rows, w_up_ref[...], preferred_element_type=jnp.float32)
    inner = (gate_proj / (1.0 + jnp.exp(-gate_proj)) * up_proj).astype(jnp.bfloat16)
    result = jnp.dot(inner, w_down_ref[...], preferred_element_type=jnp.float32)
    targets = (
        own_ref.at[...],
        other_ref.at[0:tokens],
        across_ref.at[...],
        other_ref.at[tokens : 2 * tokens],
    )
    for block in range(4):
        part = (result[block * cap : (block + 1) * cap, :] * weights[block]).astype(jnp.bfloat16)
        targets[block][...] = lax.dot_general(
            picks[block], part, (((0,), (0,)), ((), ())), preferred_element_type=jnp.float32
        ).astype(jnp.bfloat16)


def experts_on_rows(mine, quad, row_blocks, w_gate, w_up, w_down, cap):
    tokens = row_blocks[0][0].shape[0]
    width, hidden_units = w_gate.shape
    pieces = tuple(len(block) for block in row_blocks)
    return pl.pallas_call(
        functools.partial(experts_kernel, cap=cap, pieces=pieces),
        in_specs=[pl.BlockSpec(memory_space=pltpu.SMEM)]
        + [pl.BlockSpec(memory_space=pltpu.VMEM)] * (4 + sum(pieces)),
        out_specs=[pl.BlockSpec(memory_space=pltpu.VMEM)] * 3,
        out_shape=[
            jax.ShapeDtypeStruct((tokens, width), jnp.bfloat16),
            jax.ShapeDtypeStruct((tokens, width), jnp.bfloat16),
            jax.ShapeDtypeStruct((2 * tokens, width), jnp.bfloat16),
        ],
        scratch_shapes=[pltpu.VMEM((4 * cap, width), jnp.bfloat16)],
        compiler_params=pltpu.CompilerParams(vmem_limit_bytes=28 * MIB),
        cost_estimate=pl.CostEstimate(
            flops=0,
            bytes_accessed=0,
            transcendentals=0,
        ),
    )(mine.reshape(1), quad, *sum(row_blocks, []), w_gate, w_up, w_down)


def gathered_plan(
    query_rows,
    key_rows,
    value_rows,
    residual_in,
    out_proj,
    norm_gain,
    expert_ids,
    gate_weights,
    expert_gate,
    expert_up,
    expert_down,
    cap,
):
    n_seq = lax.axis_size("seq")
    n_sub = lax.axis_size("sub")
    experts = n_seq * n_sub
    place = lax.axis_index("seq")
    core = place % 2
    chip = place // 2
    twin = [(index, index ^ 1) for index in range(n_seq)]
    across = [(index, (index + 2) % n_seq) for index in range(n_seq)]
    diagonal = [(index, (index ^ 1) ^ 2) for index in range(n_seq)]
    order = [0] + list(range(1, n_sub, 2)) + list(reversed(range(2, n_sub, 2)))

    def ring(steps):
        return [(order[at], order[(at + steps) % n_sub]) for at in range(n_sub)]

    queries = query_rows[0]
    chip_width = queries.shape[1] // 2

    tokens = queries.shape[0]
    queries_away, kv_here, kv_away = pack(
        chip,
        queries,
        key_rows[0],
        value_rows[0],
        expert_ids[0].T,
        gate_weights[0].T,
        experts,
    )
    incoming = lax.ppermute(queries_away, "seq", across)
    kv_parts = [
        kv_here,
        lax.ppermute(kv_here, "seq", twin),
        lax.ppermute(kv_away, "seq", across),
        lax.ppermute(kv_away, "seq", diagonal),
    ]
    w_other = lax.ppermute(out_proj, "seq", twin)
    columns = [place, place ^ 1, place ^ 2, place ^ 3]

    def place_of(query_start, row_block):
        return jnp.stack([core, query_start, row_block] + columns).astype(jnp.int32)

    sent, quad = attend(
        place_of(0 * place, place ^ 2), incoming, kv_parts, [], out_proj, w_other, jnp.bfloat16
    )
    projected_across = lax.ppermute(sent, "seq", across)
    projected, _ = attend(
        place_of(chip * chip_width, place),
        queries,
        kv_parts,
        [residual_in[0]],
        out_proj,
        w_other,
        jnp.float32,
    )
    quads = [lax.ppermute(quad, "sub", ring(steps)) for steps in range(1, n_sub)]
    hidden, normed = add_and_norm(projected, projected_across, norm_gain[None], quads)

    last = n_sub - 1
    mine = place * n_sub + lax.axis_index("sub")

    held = {("row", 0): normed, ("quad", 0): quad}
    held.update({("quad", steps): moved for steps, moved in enumerate(quads, 1)})
    half = normed.shape[1] // 2
    ways = {"across": ("seq", across), "twin": ("seq", twin), "on": ("sub", ring(1))}

    def move(array, way):
        return lax.ppermute(array, *ways[way])

    def experts_of(step):
        held["own", step], held["part", step], other = experts_on_rows(
            mine,
            held["quad", step],
            [
                [held[name, step]] if (name, step) in held else list(held[name, step, "pieces"])
                for name in ("row", "twin", "across", "diagonal")
            ],
            expert_gate[0],
            expert_up[0],
            expert_down[0],
            cap,
        )
        return other

    def twin_sum(step):
        met = move(held["other", step], "twin")
        held["met", step] = met[:tokens]
        return (held["part", step].astype(jnp.float32) + met[tokens:].astype(jnp.float32)).astype(
            jnp.bfloat16
        )

    def sum_of(step, more):
        parts = [held["own", step], held["met", step], held["back", step]] + more
        if held["back", step].shape[1] == half:
            left = sum(part[:, :half].astype(jnp.float32) for part in parts)
            right = sum(part[:, half:].astype(jnp.float32) for part in parts if part.shape[1] > half)
            return jnp.concatenate([left, right], axis=1)
        return sum(part.astype(jnp.float32) for part in parts)

    for turn in range(1, n_sub + 5):
        now = {}
        step = turn - 1
        if step < last:
            now["across", step] = move(held["row", step], "across")
            now["row", step + 1] = move(held["row", step], "on")
        if step == last:
            now["half", 0] = move(held["row", step][:, :half], "across")
            now["half", 1] = move(held["across", step - 1][:, half:], "on")
        if step <= last:
            held["twin", step] = move(held["row", step], "twin")
        step = turn - 4 if turn < n_sub + 4 else 0
        if 1 <= step <= last or turn == n_sub + 4:
            if step == 1:
                now["back", step] = move(held["away", step], "across")
                now["late", step] = move(held["apart", step], "on")
            elif step == 2:
                away = held["away", step]
                added = away[:, half:].astype(jnp.float32) + held["late", 1].astype(jnp.float32)
                now["back", step] = move(
                    jnp.concatenate([away[:, :half], added.astype(jnp.bfloat16)], axis=1), "across"
                )
            else:
                now["back", step] = move(held["away", step], "across")
        step = turn - 5
        if 1 <= step <= last:
            more = [held["sum", step - 1]] if step > 1 else []
            now["sum", step] = move(sum_of(step, more).astype(jnp.bfloat16), "on")
        step = turn - 2
        if 0 <= step < last:
            held["diagonal", step] = move(held["across", step], "twin")
        if step == last:
            held["across", step, "pieces"] = [held["half", side] for side in range(2)]
            held["diagonal", step, "pieces"] = [
                move(held["half", side], "twin") for side in range(2)
            ]
        if 1 <= step <= last:
            now["other", step] = experts_of(step)
        if turn == n_sub + 2:
            now["other", 0] = experts_of(0)
        step = turn - 3 if turn < n_sub + 3 else 0
        if 1 <= step <= last or turn == n_sub + 3:
            away = twin_sum(step)
            if step == 1:
                now["away", step] = away[:, :half]
                now["apart", step] = away[:, half:]
            else:
                now["away", step] = away
        if turn < n_sub + 4:
            wait = 10_000_000_000 if turn <= 2 else 0
            now = dict(zip(now.keys(), meet(list(now.values()), wait)))
        held.update(now)
    total = hidden.astype(jnp.float32) + sum_of(0, [held["sum", last]])
    return total.astype(jnp.bfloat16)[None]


def per_device(
    query_rows,
    key_rows,
    value_rows,
    residual_in,
    out_proj,
    norm_gain,
    expert_ids,
    gate_weights,
    expert_gate,
    expert_up,
    expert_down,
):
    tokens = query_rows.shape[1]
    n_seq = lax.axis_size("seq")
    n_sub = lax.axis_size("sub")
    experts = n_seq * n_sub
    topk = expert_ids.shape[2]
    cap = max(2, (5 * tokens * topk + 4 * experts - 1) // (4 * experts))
    if n_seq == 2 * KVH and KVH == 2 and tokens == HD and n_sub > 2 and experts <= 2 * topk and cap % 16 == 0:
        return gathered_plan(
            query_rows,
            key_rows,
            value_rows,
            residual_in,
            out_proj,
            norm_gain,
            expert_ids,
            gate_weights,
            expert_gate,
            expert_up,
            expert_down,
            cap,
        )
    heads_here = QH // n_seq
    group = QH // KVH
    query_local = lax.all_to_all(query_rows, "seq", split_axis=2, concat_axis=1, tiled=True)
    key_full, value_full = (
        lax.all_gather(key_rows, "seq", axis=1, tiled=True),
        lax.all_gather(value_rows, "seq", axis=1, tiled=True),
    )
    first_head = lax.axis_index("seq") * heads_here
    key_list = []
    value_list = []
    for head in range(heads_here):
        kv_start = (first_head + head) // group * HD
        key_list.append(lax.dynamic_slice_in_dim(key_full[0], kv_start, HD, 1))
        value_list.append(lax.dynamic_slice_in_dim(value_full[0], kv_start, HD, 1))
    length = query_local.shape[1]
    block = min(length, max(512, length // 8))
    outputs = [
        attend_head(
            query_local[0, :, head * HD : (head + 1) * HD], key_list[head], value_list[head], block
        )
        for head in range(heads_here)
    ]
    head_block = jnp.concatenate(outputs, axis=1)[None]
    attended = lax.all_to_all(head_block, "seq", split_axis=1, concat_axis=2, tiled=True)[0]
    projected = jnp.dot(
        attended,
        lax.all_gather(out_proj, "seq", axis=0, tiled=True),
        preferred_element_type=jnp.float32,
    )
    hidden = (residual_in[0].astype(jnp.float32) + projected).astype(jnp.bfloat16)
    wide = hidden.astype(jnp.float32)
    normed = (
        wide
        * lax.rsqrt(jnp.mean(wide * wide, axis=1, keepdims=True) + 1e-06)
        * norm_gain.astype(jnp.float32)
    ).astype(jnp.bfloat16)
    flat_ids = expert_ids[0].reshape(-1)
    items = flat_ids.shape[0]
    ranks = rank_in_expert(flat_ids, experts)
    slot_of = flat_ids * cap + ranks
    slots_out = experts * cap
    item_of_slot = (
        jnp.full((slots_out,), items, jnp.int32).at[slot_of].set(jnp.arange(items, dtype=jnp.int32))
    )
    padded_rows = jnp.concatenate([normed, jnp.zeros((1, D), jnp.bfloat16)], axis=0)
    padded_gates = jnp.concatenate(
        [gate_weights[0].reshape(-1), jnp.zeros((1,), jnp.bfloat16)], axis=0
    )
    token_of_slot = jnp.where(item_of_slot < items, item_of_slot // topk, tokens)
    send_rows = padded_rows[token_of_slot].reshape(experts, cap, D)
    send_gates = padded_gates[item_of_slot].reshape(experts, cap)
    recv_rows, recv_gates = (
        lax.all_to_all(send_rows, ("seq", "sub"), split_axis=0, concat_axis=0, tiled=True),
        lax.all_to_all(send_gates, ("seq", "sub"), split_axis=0, concat_axis=0, tiled=True),
    )
    slots_in = experts * cap
    valid = recv_gates > 0
    counts = jnp.sum(valid.astype(jnp.int32), axis=1)
    offsets = jnp.cumsum(counts) - counts
    dest = jnp.where(
        valid, offsets[:, None] + jnp.arange(cap, dtype=jnp.int32)[None, :], slots_in
    ).reshape(-1)
    source_of = (
        jnp.full((slots_in + 1,), slots_in, jnp.int32)
        .at[dest]
        .set(jnp.arange(slots_in, dtype=jnp.int32))[:slots_in]
    )
    compact_rows = jnp.concatenate(
        [recv_rows.reshape(slots_in, D), jnp.zeros((1, D), jnp.bfloat16)], axis=0
    )[source_of]
    compact_gates = jnp.concatenate(
        [recv_gates.reshape(-1), jnp.zeros((1,), jnp.bfloat16)], axis=0
    )[source_of].astype(jnp.float32)
    filled = jnp.sum(counts)
    n_blocks = (filled + slots_in - 1) // slots_in
    w_gate = expert_gate[0]
    w_up = expert_up[0]
    w_down = expert_down[0]

    def expert_block(index, results):
        gate_proj = jnp.dot(compact_rows, w_gate, preferred_element_type=jnp.float32)
        up_proj = jnp.dot(compact_rows, w_up, preferred_element_type=jnp.float32)
        inner = (jax.nn.silu(gate_proj) * up_proj).astype(jnp.bfloat16)
        weighted = (
            jnp.dot(inner, w_down, preferred_element_type=jnp.float32) * compact_gates[:, None]
        )
        return weighted.astype(jnp.bfloat16)

    results = lax.fori_loop(0, n_blocks, expert_block, jnp.zeros((slots_in, D), jnp.bfloat16))
    returned = jnp.concatenate([results, jnp.zeros((1, D), jnp.bfloat16)], axis=0)[dest].reshape(
        experts, cap, D
    )
    back = lax.all_to_all(
        returned, ("seq", "sub"), split_axis=0, concat_axis=0, tiled=True
    ).reshape(slots_out, D)
    gathered = back[slot_of].reshape(tokens, topk, D).astype(jnp.float32)
    mixture = jnp.sum(gathered, axis=1)
    return (wide + mixture).astype(jnp.bfloat16)[None]


def solution(mesh):
    placed = (
        P(("grp", "sub"), "seq", None),
        P(("grp", "sub"), "seq", None),
        P(("grp", "sub"), "seq", None),
        P(("grp", "sub"), "seq", None),
        P("seq", None),
        P(),
        P(("grp", "sub"), "seq", None),
        P(("grp", "sub"), "seq", None),
        P(("seq", "sub"), None, None),
        P(("seq", "sub"), None, None),
        P(("seq", "sub"), None, None),
    )
    return jax.shard_map(
        per_device,
        mesh=mesh,
        in_specs=placed,
        out_specs=P(("grp", "sub"), "seq", None),
        check_vma=False,
    )
```

```python
import functools

import jax
import jax.numpy as jnp
from jax import lax
from jax.experimental import pallas as pl
from jax.experimental.pallas import tpu as pltpu
from jax.sharding import PartitionSpec as P

D = 2048
HD = 128
QH = 16
KVH = 2
MIB = 1024 * 1024


def attend_head(queries, keys_one, values_one, block):
    length = queries.shape[0]
    scale = 1.0 / queries.shape[1] ** 0.5
    pieces = []
    for part_index in range(length // block):
        stop = (part_index + 1) * block
        rows_here = queries[part_index * block : stop]
        scores = (
            jnp.einsum("qd,kd->qk", rows_here, keys_one[:stop], preferred_element_type=jnp.float32)
            * scale
        )
        row_pos = part_index * block + jnp.arange(block, dtype=jnp.int32)
        col_pos = jnp.arange(stop, dtype=jnp.int32)
        scores = jnp.where(row_pos[:, None] >= col_pos[None, :], scores, -1e30)
        peak = jnp.max(scores, axis=1, keepdims=True)
        weights = jnp.exp(scores - peak)
        probs = (weights / jnp.sum(weights, axis=1, keepdims=True)).astype(jnp.bfloat16)
        pieces.append(
            jnp.dot(probs, values_one[:stop], preferred_element_type=jnp.float32).astype(
                jnp.bfloat16
            )
        )
    return jnp.concatenate(pieces, axis=0)


def rank_in_expert(flat_ids, experts):
    items = flat_ids.shape[0]
    width = 128
    n_parts = items // width
    onehot = (
        (flat_ids[:, None] == jnp.arange(experts, dtype=jnp.int32)[None, :])
        .astype(jnp.bfloat16)
        .reshape(n_parts, width, experts)
    )
    lower = (
        jnp.arange(width, dtype=jnp.int32)[:, None] > jnp.arange(width, dtype=jnp.int32)[None, :]
    ).astype(jnp.bfloat16)
    within = jnp.einsum("ij,bje->bie", lower, onehot, preferred_element_type=jnp.float32)
    part_counts = jnp.sum(onehot.astype(jnp.float32), axis=1)
    earlier = jnp.cumsum(part_counts, axis=0) - part_counts
    ranks = jnp.sum((within + earlier[:, None, :]) * onehot.astype(jnp.float32), axis=2)
    return ranks.reshape(items).astype(jnp.int32)


def pack_kernel(chip_ref, query_ref, key_ref, value_ref, id_ref, gate_ref, away_ref, here_kv_ref, away_kv_ref):
    tokens = query_ref.shape[0]
    head_size = key_ref.shape[1] // 2
    chip_width = away_ref.shape[1]
    chip = chip_ref[0]
    experts = here_kv_ref.shape[0] - tokens
    away_ref[...] = query_ref[:, pl.ds(pl.multiple_of((1 - chip) * chip_width, chip_width), chip_width)]
    number = lax.broadcasted_iota(jnp.int32, (experts, tokens), 0)
    table = jnp.zeros((experts, tokens), jnp.float32)
    for choice in range(id_ref.shape[0]):
        table += jnp.where(
            number == id_ref[choice : choice + 1, :],
            gate_ref[choice : choice + 1, :].astype(jnp.float32),
            0.0,
        )
    for out_ref, head in ((here_kv_ref, chip), (away_kv_ref, 1 - chip)):
        columns = pl.ds(pl.multiple_of(head * head_size, head_size), head_size)
        out_ref[0:tokens, 0:head_size] = key_ref[:, columns]
        out_ref[0:tokens, head_size:] = value_ref[:, columns]
        out_ref[tokens:, 0:head_size] = table.astype(jnp.bfloat16)
        out_ref[tokens:, head_size:] = jnp.zeros((experts, head_size), jnp.bfloat16)


def pack(chip, queries, keys, values, ids, gates, experts):
    tokens, width = queries.shape
    kv = jax.ShapeDtypeStruct((tokens + experts, keys.shape[1]), jnp.bfloat16)
    return pl.pallas_call(
        pack_kernel,
        in_specs=[pl.BlockSpec(memory_space=pltpu.SMEM)]
        + [pl.BlockSpec(memory_space=pltpu.VMEM)] * 5,
        out_specs=[pl.BlockSpec(memory_space=pltpu.VMEM)] * 3,
        out_shape=[jax.ShapeDtypeStruct((tokens, width // 2), jnp.bfloat16), kv, kv],
        compiler_params=pltpu.CompilerParams(vmem_limit_bytes=60 * MIB),
    )(chip.reshape(1), queries, keys, values, ids, gates)


def attend_kernel(place_ref, query_ref, *refs, scale):
    kv_refs, refs = refs[:4], refs[4:]
    base_refs = refs[: len(refs) - 13]
    w_own_ref, w_other_ref, out_ref, quad_ref, keys, values, heads = refs[-13:-6]
    w_own, w_other, stacked, scores, probs, done = refs[-6:]
    fetches = [
        pltpu.make_async_copy(w_own_ref, w_own, done.at[0]),
        pltpu.make_async_copy(w_other_ref, w_other, done.at[1]),
    ]
    for fetch in fetches:
        fetch.start()
    rows = keys.shape[0] // 4
    head_size = keys.shape[1]
    core = place_ref[0]
    query_start = pl.multiple_of(place_ref[1], head_size)
    row_pos = place_ref[2] * rows + lax.broadcasted_iota(jnp.int32, (rows, 1), 0)
    lane = lax.broadcasted_iota(jnp.int32, (1, rows), 1)
    col_pos = jnp.concatenate([place_ref[3 + part] * rows + lane for part in range(4)], axis=1)
    allowed = row_pos >= col_pos
    for part, kv_ref in enumerate(kv_refs):
        keys[part * rows : (part + 1) * rows, :] = kv_ref[0:rows, 0:head_size]
        values[part * rows : (part + 1) * rows, :] = kv_ref[0:rows, head_size:]
        quad_ref[:, part * rows : (part + 1) * rows] = kv_ref[rows:, 0:rows]
    key_block = keys[...]
    value_block = values[...]
    count = heads.shape[1] // head_size
    for head in range(count):
        stacked[head * rows : (head + 1) * rows, :] = query_ref[
            :, pl.ds(query_start + head * head_size, head_size)
        ]
    scores[...] = lax.dot_general(
        stacked[...], key_block, (((1,), (1,)), ((), ())), preferred_element_type=jnp.float32
    )
    for head in range(count):
        part = slice(head * rows, (head + 1) * rows)
        score = jnp.where(allowed, scores[part, :] * scale, -1e30)
        weights = jnp.exp(score - jnp.max(score, axis=1, keepdims=True))
        probs[part, :] = (weights * (1.0 / jnp.sum(weights, axis=1, keepdims=True))).astype(
            jnp.bfloat16
        )
    mixed = jnp.dot(probs[...], value_block, preferred_element_type=jnp.float32)
    for head in range(count):
        heads[:, head * head_size : (head + 1) * head_size] = mixed[
            head * rows : (head + 1) * rows
        ].astype(jnp.bfloat16)
    for fetch in fetches:
        fetch.wait()
    half = heads.shape[1] // 2
    own = heads[:, pl.ds(pl.multiple_of(core * half, half), half)]
    other = heads[:, pl.ds(pl.multiple_of((1 - core) * half, half), half)]
    total = jnp.dot(own, w_own[...], preferred_element_type=jnp.float32) + jnp.dot(
        other, w_other[...], preferred_element_type=jnp.float32
    )
    for base_ref in base_refs:
        total += base_ref[...].astype(jnp.float32)
    out_ref[...] = total.astype(out_ref.dtype)


def attend(place, queries, kv_parts, bases, w_own, w_other, dtype):
    tokens = queries.shape[0]
    width = w_own.shape[1]
    chip_width = 2 * w_own.shape[0]
    return pl.pallas_call(
        functools.partial(attend_kernel, scale=1.0 / HD**0.5),
        in_specs=[pl.BlockSpec(memory_space=pltpu.SMEM)]
        + [pl.BlockSpec(memory_space=pltpu.VMEM)] * (5 + len(bases))
        + [pl.BlockSpec(memory_space=pl.ANY)] * 2,
        out_specs=[pl.BlockSpec(memory_space=pltpu.VMEM)] * 2,
        out_shape=[
            jax.ShapeDtypeStruct((tokens, width), dtype),
            jax.ShapeDtypeStruct((kv_parts[0].shape[0] - tokens, 4 * tokens), jnp.bfloat16),
        ],
        scratch_shapes=[
            pltpu.VMEM((4 * tokens, HD), jnp.bfloat16),
            pltpu.VMEM((4 * tokens, HD), jnp.bfloat16),
            pltpu.VMEM((tokens, chip_width), jnp.bfloat16),
            pltpu.VMEM(w_own.shape, jnp.bfloat16),
            pltpu.VMEM(w_other.shape, jnp.bfloat16),
            pltpu.VMEM((tokens * chip_width // HD, HD), jnp.bfloat16),
            pltpu.VMEM((tokens * chip_width // HD, 4 * tokens), jnp.float32),
            pltpu.VMEM((tokens * chip_width // HD, 4 * tokens), jnp.bfloat16),
            pltpu.SemaphoreType.DMA((2,)),
        ],
        compiler_params=pltpu.CompilerParams(vmem_limit_bytes=60 * MIB),
        cost_estimate=pl.CostEstimate(
            flops=16 * tokens * tokens * chip_width + 2 * tokens * chip_width * width,
            bytes_accessed=4 * w_own.size + 4 * tokens * width,
            transcendentals=4 * tokens * tokens * chip_width // HD,
        ),
    )(place, queries, *kv_parts, *bases, w_own, w_other)


def norm_kernel(own_ref, other_ref, gain_ref, *refs):
    hidden_ref, normed_ref = refs[-2:]
    hidden = (own_ref[...] + other_ref[...].astype(jnp.float32)).astype(jnp.bfloat16)
    hidden_ref[...] = hidden
    wide = hidden.astype(jnp.float32)
    normed_ref[...] = (
        wide
        * lax.rsqrt(jnp.mean(wide * wide, axis=1, keepdims=True) + 1e-06)
        * gain_ref[...].astype(jnp.float32)
    ).astype(jnp.bfloat16)


def add_and_norm(own, other, gain, present):
    return pl.pallas_call(
        norm_kernel,
        in_specs=[pl.BlockSpec(memory_space=pltpu.VMEM)] * 3
        + [pl.BlockSpec(memory_space=pl.ANY)] * len(present),
        out_specs=[pl.BlockSpec(memory_space=pltpu.VMEM)] * 2,
        out_shape=[jax.ShapeDtypeStruct(own.shape, jnp.bfloat16)] * 2,
        compiler_params=pltpu.CompilerParams(vmem_limit_bytes=60 * MIB),
    )(own, other, gain, *present)


def pass_kernel(*refs):
    del refs


def meet(arrays, flops):
    return pl.pallas_call(
        pass_kernel,
        in_specs=[pl.BlockSpec(memory_space=pl.ANY)] * len(arrays),
        out_specs=[pl.BlockSpec(memory_space=pl.ANY)] * len(arrays),
        out_shape=[jax.ShapeDtypeStruct(array.shape, array.dtype) for array in arrays],
        input_output_aliases={index: index for index in range(len(arrays))},
    )(*arrays)


def pass_kernel(*refs):
    del refs


def meet(arrays, flops):
    return pl.pallas_call(
        pass_kernel,
        in_specs=[pl.BlockSpec(memory_space=pl.ANY)] * len(arrays),
        out_specs=[pl.BlockSpec(memory_space=pl.ANY)] * len(arrays),
        out_shape=[jax.ShapeDtypeStruct(array.shape, array.dtype) for array in arrays],
        input_output_aliases={index: index for index in range(len(arrays))},
        compiler_params=pltpu.CompilerParams(vmem_limit_bytes=MIB),
        cost_estimate=pl.CostEstimate(flops=flops, bytes_accessed=0, transcendentals=0),
    )(*arrays)


def experts_kernel(mine_ref, quad_ref, *refs, cap, pieces):
    row_refs = []
    for count in pieces:
        row_refs.append(refs[:count])
        refs = refs[count:]
    w_gate_ref, w_up_ref, w_down_ref, own_ref, across_ref, other_ref, packed = refs
    tokens = row_refs[0][0].shape[0]
    quad = quad_ref[...].astype(jnp.float32)
    expert = lax.broadcasted_iota(jnp.int32, quad.shape, 0)
    line = jnp.sum(jnp.where(expert == mine_ref[0], quad, 0.0), axis=0, keepdims=True)
    gates = jnp.concatenate(
        [line[:, block * tokens : (block + 1) * tokens] for block in range(4)], axis=0
    )
    named = gates > 0
    before = (
        lax.broadcasted_iota(jnp.int32, (tokens, tokens), 0)
        < lax.broadcasted_iota(jnp.int32, (tokens, tokens), 1)
    ).astype(jnp.bfloat16)
    rank = jnp.dot(
        named.astype(jnp.float32).astype(jnp.bfloat16), before, preferred_element_type=jnp.float32
    )
    slot = jnp.where(named, rank.astype(jnp.int32), -1)
    slots = lax.broadcasted_iota(jnp.int32, (cap, tokens), 0)
    picks = []
    weights = []
    for block in range(4):
        chosen = slots == slot[block : block + 1, :]
        picks.append(jnp.where(chosen, 1.0, 0.0).astype(jnp.bfloat16))
        weights.append(
            jnp.sum(jnp.where(chosen, gates[block : block + 1, :], 0.0), axis=1, keepdims=True)
        )
        start = 0
        for row_ref in row_refs[block]:
            stop = start + row_ref.shape[1]
            packed[block * cap : (block + 1) * cap, start:stop] = jnp.dot(
                picks[block], row_ref[...], preferred_element_type=jnp.float32
            ).astype(jnp.bfloat16)
            start = stop
    rows = packed[...]
    gate_proj = jnp.dot(rows, w_gate_ref[...], preferred_element_type=jnp.float32)
    up_proj = jnp.dot(rows, w_up_ref[...], preferred_element_type=jnp.float32)
    inner = (gate_proj / (1.0 + jnp.exp(-gate_proj)) * up_proj).astype(jnp.bfloat16)
    result = jnp.dot(inner, w_down_ref[...], preferred_element_type=jnp.float32)
    targets = (
        own_ref.at[...],
        other_ref.at[0:tokens],
        across_ref.at[...],
        other_ref.at[tokens : 2 * tokens],
    )
    for block in range(4):
        part = (result[block * cap : (block + 1) * cap, :] * weights[block]).astype(jnp.bfloat16)
        targets[block][...] = lax.dot_general(
            picks[block], part, (((0,), (0,)), ((), ())), preferred_element_type=jnp.float32
        ).astype(jnp.bfloat16)


def experts_on_rows(mine, quad, row_blocks, w_gate, w_up, w_down, cap):
    tokens = row_blocks[0][0].shape[0]
    width, hidden_units = w_gate.shape
    pieces = tuple(len(block) for block in row_blocks)
    return pl.pallas_call(
        functools.partial(experts_kernel, cap=cap, pieces=pieces),
        in_specs=[pl.BlockSpec(memory_space=pltpu.SMEM)]
        + [pl.BlockSpec(memory_space=pltpu.VMEM)] * (4 + sum(pieces)),
        out_specs=[pl.BlockSpec(memory_space=pltpu.VMEM)] * 3,
        out_shape=[
            jax.ShapeDtypeStruct((tokens, width), jnp.bfloat16),
            jax.ShapeDtypeStruct((tokens, width), jnp.bfloat16),
            jax.ShapeDtypeStruct((2 * tokens, width), jnp.bfloat16),
        ],
        scratch_shapes=[pltpu.VMEM((4 * cap, width), jnp.bfloat16)],
        compiler_params=pltpu.CompilerParams(vmem_limit_bytes=28 * MIB),
        cost_estimate=pl.CostEstimate(
            flops=0,
            bytes_accessed=0,
            transcendentals=0,
        ),
    )(mine.reshape(1), quad, *sum(row_blocks, []), w_gate, w_up, w_down)


def gathered_plan(
    query_rows,
    key_rows,
    value_rows,
    residual_in,
    out_proj,
    norm_gain,
    expert_ids,
    gate_weights,
    expert_gate,
    expert_up,
    expert_down,
    cap,
):
    n_seq = lax.axis_size("seq")
    n_sub = lax.axis_size("sub")
    experts = n_seq * n_sub
    place = lax.axis_index("seq")
    core = place % 2
    chip = place // 2
    twin = [(index, index ^ 1) for index in range(n_seq)]
    across = [(index, (index + 2) % n_seq) for index in range(n_seq)]
    diagonal = [(index, (index ^ 1) ^ 2) for index in range(n_seq)]
    order = [0] + list(range(1, n_sub, 2)) + list(reversed(range(2, n_sub, 2)))

    def ring(steps):
        return [(order[at], order[(at + steps) % n_sub]) for at in range(n_sub)]

    queries = query_rows[0]
    chip_width = queries.shape[1] // 2

    tokens = queries.shape[0]
    queries_away, kv_here, kv_away = pack(
        chip,
        queries,
        key_rows[0],
        value_rows[0],
        expert_ids[0].T,
        gate_weights[0].T,
        experts,
    )
    incoming = lax.ppermute(queries_away, "seq", across)
    kv_parts = [
        kv_here,
        lax.ppermute(kv_here, "seq", twin),
        lax.ppermute(kv_away, "seq", across),
        lax.ppermute(kv_away, "seq", diagonal),
    ]
    w_other = lax.ppermute(out_proj, "seq", twin)
    columns = [place, place ^ 1, place ^ 2, place ^ 3]

    def place_of(query_start, row_block):
        return jnp.stack([core, query_start, row_block] + columns).astype(jnp.int32)

    sent, quad = attend(
        place_of(0 * place, place ^ 2), incoming, kv_parts, [], out_proj, w_other, jnp.bfloat16
    )
    projected_across = lax.ppermute(sent, "seq", across)
    projected, _ = attend(
        place_of(chip * chip_width, place),
        queries,
        kv_parts,
        [residual_in[0]],
        out_proj,
        w_other,
        jnp.float32,
    )
    quads = [lax.ppermute(quad, "sub", ring(steps)) for steps in range(1, n_sub)]
    hidden, normed = add_and_norm(projected, projected_across, norm_gain[None], quads)

    last = n_sub - 1
    mine = place * n_sub + lax.axis_index("sub")

    held = {("row", 0): normed, ("quad", 0): quad}
    held.update({("quad", steps): moved for steps, moved in enumerate(quads, 1)})
    half = normed.shape[1] // 2
    cut = normed.shape[1] // 4 * 3
    ways = {"across": ("seq", across), "twin": ("seq", twin), "on": ("sub", ring(1))}

    def move(array, way):
        return lax.ppermute(array, *ways[way])

    def experts_of(step):
        held["own", step], held["part", step], other = experts_on_rows(
            mine,
            held["quad", step],
            [
                [held[name, step]] if (name, step) in held else list(held[name, step, "pieces"])
                for name in ("row", "twin", "across", "diagonal")
            ],
            expert_gate[0],
            expert_up[0],
            expert_down[0],
            cap,
        )
        return other

    def twin_sum(step):
        met = move(held["other", step], "twin")
        held["met", step] = met[:tokens]
        return (held["part", step].astype(jnp.float32) + met[tokens:].astype(jnp.float32)).astype(
            jnp.bfloat16
        )

    def sum_of(step, more):
        parts = [held["own", step], held["met", step], held["back", step]] + more
        if held["back", step].shape[1] == cut:
            left = sum(part[:, :cut].astype(jnp.float32) for part in parts)
            right = sum(part[:, cut:].astype(jnp.float32) for part in parts if part.shape[1] > cut)
            return jnp.concatenate([left, right], axis=1)
        return sum(part.astype(jnp.float32) for part in parts)

    for turn in range(1, n_sub + 5):
        now = {}
        step = turn - 1
        if step < last:
            now["across", step] = move(held["row", step], "across")
            now["row", step + 1] = move(held["row", step], "on")
        if step == last:
            now["half", 0] = move(held["row", step][:, :half], "across")
            now["half", 1] = move(held["across", step - 1][:, half:], "on")
        if step <= last:
            held["twin", step] = move(held["row", step], "twin")
        step = turn - 4 if turn < n_sub + 4 else 0
        if 1 <= step <= last or turn == n_sub + 4:
            if step == 1:
                now["back", step] = move(held["away", step], "across")
                now["late", step] = move(held["apart", step], "on")
            elif step == 2:
                away = held["away", step]
                added = away[:, cut:].astype(jnp.float32) + held["late", 1].astype(jnp.float32)
                now["back", step] = move(
                    jnp.concatenate([away[:, :cut], added.astype(jnp.bfloat16)], axis=1), "across"
                )
            else:
                now["back", step] = move(held["away", step], "across")
        step = turn - 5
        if 1 <= step <= last:
            more = [held["sum", step - 1]] if step > 1 else []
            now["sum", step] = move(sum_of(step, more).astype(jnp.bfloat16), "on")
        step = turn - 2
        if 0 <= step < last:
            held["diagonal", step] = move(held["across", step], "twin")
        if step == last:
            held["across", step, "pieces"] = [held["half", side] for side in range(2)]
            held["diagonal", step, "pieces"] = [
                move(held["half", side], "twin") for side in range(2)
            ]
        if 1 <= step <= last:
            now["other", step] = experts_of(step)
        if turn == n_sub + 2:
            now["other", 0] = experts_of(0)
        step = turn - 3 if turn < n_sub + 3 else 0
        if 1 <= step <= last or turn == n_sub + 3:
            away = twin_sum(step)
            if step == 1:
                now["away", step] = away[:, :cut]
                now["apart", step] = away[:, cut:]
            else:
                now["away", step] = away
        if turn < n_sub + 4:
            wait = 10_000_000_000 if turn <= 2 else 0
            now = dict(zip(now.keys(), meet(list(now.values()), wait)))
        held.update(now)
    total = hidden.astype(jnp.float32) + sum_of(0, [held["sum", last]])
    return total.astype(jnp.bfloat16)[None]


def per_device(
    query_rows,
    key_rows,
    value_rows,
    residual_in,
    out_proj,
    norm_gain,
    expert_ids,
    gate_weights,
    expert_gate,
    expert_up,
    expert_down,
):
    tokens = query_rows.shape[1]
    n_seq = lax.axis_size("seq")
    n_sub = lax.axis_size("sub")
    experts = n_seq * n_sub
    topk = expert_ids.shape[2]
    cap = max(2, (5 * tokens * topk + 4 * experts - 1) // (4 * experts))
    if n_seq == 2 * KVH and KVH == 2 and tokens == HD and n_sub > 2 and experts <= 2 * topk and cap % 16 == 0:
        return gathered_plan(
            query_rows,
            key_rows,
            value_rows,
            residual_in,
            out_proj,
            norm_gain,
            expert_ids,
            gate_weights,
            expert_gate,
            expert_up,
            expert_down,
            cap,
        )
    heads_here = QH // n_seq
    group = QH // KVH
    query_local = lax.all_to_all(query_rows, "seq", split_axis=2, concat_axis=1, tiled=True)
    key_full, value_full = (
        lax.all_gather(key_rows, "seq", axis=1, tiled=True),
        lax.all_gather(value_rows, "seq", axis=1, tiled=True),
    )
    first_head = lax.axis_index("seq") * heads_here
    key_list = []
    value_list = []
    for head in range(heads_here):
        kv_start = (first_head + head) // group * HD
        key_list.append(lax.dynamic_slice_in_dim(key_full[0], kv_start, HD, 1))
        value_list.append(lax.dynamic_slice_in_dim(value_full[0], kv_start, HD, 1))
    length = query_local.shape[1]
    block = min(length, max(512, length // 8))
    outputs = [
        attend_head(
            query_local[0, :, head * HD : (head + 1) * HD], key_list[head], value_list[head], block
        )
        for head in range(heads_here)
    ]
    head_block = jnp.concatenate(outputs, axis=1)[None]
    attended = lax.all_to_all(head_block, "seq", split_axis=1, concat_axis=2, tiled=True)[0]
    projected = jnp.dot(
        attended,
        lax.all_gather(out_proj, "seq", axis=0, tiled=True),
        preferred_element_type=jnp.float32,
    )
    hidden = (residual_in[0].astype(jnp.float32) + projected).astype(jnp.bfloat16)
    wide = hidden.astype(jnp.float32)
    normed = (
        wide
        * lax.rsqrt(jnp.mean(wide * wide, axis=1, keepdims=True) + 1e-06)
        * norm_gain.astype(jnp.float32)
    ).astype(jnp.bfloat16)
    flat_ids = expert_ids[0].reshape(-1)
    items = flat_ids.shape[0]
    ranks = rank_in_expert(flat_ids, experts)
    slot_of = flat_ids * cap + ranks
    slots_out = experts * cap
    item_of_slot = (
        jnp.full((slots_out,), items, jnp.int32).at[slot_of].set(jnp.arange(items, dtype=jnp.int32))
    )
    padded_rows = jnp.concatenate([normed, jnp.zeros((1, D), jnp.bfloat16)], axis=0)
    padded_gates = jnp.concatenate(
        [gate_weights[0].reshape(-1), jnp.zeros((1,), jnp.bfloat16)], axis=0
    )
    token_of_slot = jnp.where(item_of_slot < items, item_of_slot // topk, tokens)
    send_rows = padded_rows[token_of_slot].reshape(experts, cap, D)
    send_gates = padded_gates[item_of_slot].reshape(experts, cap)
    recv_rows, recv_gates = (
        lax.all_to_all(send_rows, ("seq", "sub"), split_axis=0, concat_axis=0, tiled=True),
        lax.all_to_all(send_gates, ("seq", "sub"), split_axis=0, concat_axis=0, tiled=True),
    )
    slots_in = experts * cap
    valid = recv_gates > 0
    counts = jnp.sum(valid.astype(jnp.int32), axis=1)
    offsets = jnp.cumsum(counts) - counts
    dest = jnp.where(
        valid, offsets[:, None] + jnp.arange(cap, dtype=jnp.int32)[None, :], slots_in
    ).reshape(-1)
    source_of = (
        jnp.full((slots_in + 1,), slots_in, jnp.int32)
        .at[dest]
        .set(jnp.arange(slots_in, dtype=jnp.int32))[:slots_in]
    )
    compact_rows = jnp.concatenate(
        [recv_rows.reshape(slots_in, D), jnp.zeros((1, D), jnp.bfloat16)], axis=0
    )[source_of]
    compact_gates = jnp.concatenate(
        [recv_gates.reshape(-1), jnp.zeros((1,), jnp.bfloat16)], axis=0
    )[source_of].astype(jnp.float32)
    filled = jnp.sum(counts)
    n_blocks = (filled + slots_in - 1) // slots_in
    w_gate = expert_gate[0]
    w_up = expert_up[0]
    w_down = expert_down[0]

    def expert_block(index, results):
        gate_proj = jnp.dot(compact_rows, w_gate, preferred_element_type=jnp.float32)
        up_proj = jnp.dot(compact_rows, w_up, preferred_element_type=jnp.float32)
        inner = (jax.nn.silu(gate_proj) * up_proj).astype(jnp.bfloat16)
        weighted = (
            jnp.dot(inner, w_down, preferred_element_type=jnp.float32) * compact_gates[:, None]
        )
        return weighted.astype(jnp.bfloat16)

    results = lax.fori_loop(0, n_blocks, expert_block, jnp.zeros((slots_in, D), jnp.bfloat16))
    returned = jnp.concatenate([results, jnp.zeros((1, D), jnp.bfloat16)], axis=0)[dest].reshape(
        experts, cap, D
    )
    back = lax.all_to_all(
        returned, ("seq", "sub"), split_axis=0, concat_axis=0, tiled=True
    ).reshape(slots_out, D)
    gathered = back[slot_of].reshape(tokens, topk, D).astype(jnp.float32)
    mixture = jnp.sum(gathered, axis=1)
    return (wide + mixture).astype(jnp.bfloat16)[None]


def solution(mesh):
    placed = (
        P(("grp", "sub"), "seq", None),
        P(("grp", "sub"), "seq", None),
        P(("grp", "sub"), "seq", None),
        P(("grp", "sub"), "seq", None),
        P("seq", None),
        P(),
        P(("grp", "sub"), "seq", None),
        P(("grp", "sub"), "seq", None),
        P(("seq", "sub"), None, None),
        P(("seq", "sub"), None, None),
        P(("seq", "sub"), None, None),
    )
    return jax.shard_map(
        per_device,
        mesh=mesh,
        in_specs=placed,
        out_specs=P(("grp", "sub"), "seq", None),
        check_vma=False,
    )
```

```python
import functools

import jax
import jax.numpy as jnp
from jax import lax
from jax.experimental import pallas as pl
from jax.experimental.pallas import tpu as pltpu
from jax.sharding import PartitionSpec as P

D = 2048
HD = 128
QH = 16
KVH = 2
MIB = 1024 * 1024


def attend_head(queries, keys_one, values_one, block):
    length = queries.shape[0]
    scale = 1.0 / queries.shape[1] ** 0.5
    pieces = []
    for part_index in range(length // block):
        stop = (part_index + 1) * block
        rows_here = queries[part_index * block : stop]
        scores = (
            jnp.einsum("qd,kd->qk", rows_here, keys_one[:stop], preferred_element_type=jnp.float32)
            * scale
        )
        row_pos = part_index * block + jnp.arange(block, dtype=jnp.int32)
        col_pos = jnp.arange(stop, dtype=jnp.int32)
        scores = jnp.where(row_pos[:, None] >= col_pos[None, :], scores, -1e30)
        peak = jnp.max(scores, axis=1, keepdims=True)
        weights = jnp.exp(scores - peak)
        probs = (weights / jnp.sum(weights, axis=1, keepdims=True)).astype(jnp.bfloat16)
        pieces.append(
            jnp.dot(probs, values_one[:stop], preferred_element_type=jnp.float32).astype(
                jnp.bfloat16
            )
        )
    return jnp.concatenate(pieces, axis=0)


def rank_in_expert(flat_ids, experts):
    items = flat_ids.shape[0]
    width = 128
    n_parts = items // width
    onehot = (
        (flat_ids[:, None] == jnp.arange(experts, dtype=jnp.int32)[None, :])
        .astype(jnp.bfloat16)
        .reshape(n_parts, width, experts)
    )
    lower = (
        jnp.arange(width, dtype=jnp.int32)[:, None] > jnp.arange(width, dtype=jnp.int32)[None, :]
    ).astype(jnp.bfloat16)
    within = jnp.einsum("ij,bje->bie", lower, onehot, preferred_element_type=jnp.float32)
    part_counts = jnp.sum(onehot.astype(jnp.float32), axis=1)
    earlier = jnp.cumsum(part_counts, axis=0) - part_counts
    ranks = jnp.sum((within + earlier[:, None, :]) * onehot.astype(jnp.float32), axis=2)
    return ranks.reshape(items).astype(jnp.int32)


def pack_kernel(chip_ref, query_ref, key_ref, value_ref, id_ref, gate_ref, away_ref, here_kv_ref, away_kv_ref):
    tokens = query_ref.shape[0]
    head_size = key_ref.shape[1] // 2
    chip_width = away_ref.shape[1]
    chip = chip_ref[0]
    experts = here_kv_ref.shape[0] - tokens
    away_ref[...] = query_ref[:, pl.ds(pl.multiple_of((1 - chip) * chip_width, chip_width), chip_width)]
    number = lax.broadcasted_iota(jnp.int32, (experts, tokens), 0)
    table = jnp.zeros((experts, tokens), jnp.float32)
    for choice in range(id_ref.shape[0]):
        table += jnp.where(
            number == id_ref[choice : choice + 1, :],
            gate_ref[choice : choice + 1, :].astype(jnp.float32),
            0.0,
        )
    for out_ref, head in ((here_kv_ref, chip), (away_kv_ref, 1 - chip)):
        columns = pl.ds(pl.multiple_of(head * head_size, head_size), head_size)
        out_ref[0:tokens, 0:head_size] = key_ref[:, columns]
        out_ref[0:tokens, head_size:] = value_ref[:, columns]
        out_ref[tokens:, 0:head_size] = table.astype(jnp.bfloat16)
        out_ref[tokens:, head_size:] = jnp.zeros((experts, head_size), jnp.bfloat16)


def pack(chip, queries, keys, values, ids, gates, experts):
    tokens, width = queries.shape
    kv = jax.ShapeDtypeStruct((tokens + experts, keys.shape[1]), jnp.bfloat16)
    return pl.pallas_call(
        pack_kernel,
        in_specs=[pl.BlockSpec(memory_space=pltpu.SMEM)]
        + [pl.BlockSpec(memory_space=pltpu.VMEM)] * 5,
        out_specs=[pl.BlockSpec(memory_space=pltpu.VMEM)] * 3,
        out_shape=[jax.ShapeDtypeStruct((tokens, width // 2), jnp.bfloat16), kv, kv],
        compiler_params=pltpu.CompilerParams(vmem_limit_bytes=60 * MIB),
    )(chip.reshape(1), queries, keys, values, ids, gates)


def attend_kernel(place_ref, query_ref, *refs, scale):
    kv_refs, refs = refs[:4], refs[4:]
    base_refs = refs[: len(refs) - 13]
    w_own_ref, w_other_ref, out_ref, quad_ref, keys, values, heads = refs[-13:-6]
    w_own, w_other, stacked, scores, probs, done = refs[-6:]
    fetches = [
        pltpu.make_async_copy(w_own_ref, w_own, done.at[0]),
        pltpu.make_async_copy(w_other_ref, w_other, done.at[1]),
    ]
    for fetch in fetches:
        fetch.start()
    rows = keys.shape[0] // 4
    head_size = keys.shape[1]
    core = place_ref[0]
    query_start = pl.multiple_of(place_ref[1], head_size)
    row_pos = place_ref[2] * rows + lax.broadcasted_iota(jnp.int32, (rows, 1), 0)
    lane = lax.broadcasted_iota(jnp.int32, (1, rows), 1)
    col_pos = jnp.concatenate([place_ref[3 + part] * rows + lane for part in range(4)], axis=1)
    allowed = row_pos >= col_pos
    for part, kv_ref in enumerate(kv_refs):
        keys[part * rows : (part + 1) * rows, :] = kv_ref[0:rows, 0:head_size]
        values[part * rows : (part + 1) * rows, :] = kv_ref[0:rows, head_size:]
        quad_ref[:, part * rows : (part + 1) * rows] = kv_ref[rows:, 0:rows]
    key_block = keys[...]
    value_block = values[...]
    count = heads.shape[1] // head_size
    for head in range(count):
        stacked[head * rows : (head + 1) * rows, :] = query_ref[
            :, pl.ds(query_start + head * head_size, head_size)
        ]
    scores[...] = lax.dot_general(
        stacked[...], key_block, (((1,), (1,)), ((), ())), preferred_element_type=jnp.float32
    )
    for head in range(count):
        part = slice(head * rows, (head + 1) * rows)
        score = jnp.where(allowed, scores[part, :] * scale, -1e30)
        weights = jnp.exp(score - jnp.max(score, axis=1, keepdims=True))
        probs[part, :] = (weights * (1.0 / jnp.sum(weights, axis=1, keepdims=True))).astype(
            jnp.bfloat16
        )
    mixed = jnp.dot(probs[...], value_block, preferred_element_type=jnp.float32)
    for head in range(count):
        heads[:, head * head_size : (head + 1) * head_size] = mixed[
            head * rows : (head + 1) * rows
        ].astype(jnp.bfloat16)
    for fetch in fetches:
        fetch.wait()
    half = heads.shape[1] // 2
    own = heads[:, pl.ds(pl.multiple_of(core * half, half), half)]
    other = heads[:, pl.ds(pl.multiple_of((1 - core) * half, half), half)]
    total = jnp.dot(own, w_own[...], preferred_element_type=jnp.float32) + jnp.dot(
        other, w_other[...], preferred_element_type=jnp.float32
    )
    for base_ref in base_refs:
        total += base_ref[...].astype(jnp.float32)
    out_ref[...] = total.astype(out_ref.dtype)


def attend(place, queries, kv_parts, bases, w_own, w_other, dtype):
    tokens = queries.shape[0]
    width = w_own.shape[1]
    chip_width = 2 * w_own.shape[0]
    return pl.pallas_call(
        functools.partial(attend_kernel, scale=1.0 / HD**0.5),
        in_specs=[pl.BlockSpec(memory_space=pltpu.SMEM)]
        + [pl.BlockSpec(memory_space=pltpu.VMEM)] * (5 + len(bases))
        + [pl.BlockSpec(memory_space=pl.ANY)] * 2,
        out_specs=[pl.BlockSpec(memory_space=pltpu.VMEM)] * 2,
        out_shape=[
            jax.ShapeDtypeStruct((tokens, width), dtype),
            jax.ShapeDtypeStruct((kv_parts[0].shape[0] - tokens, 4 * tokens), jnp.bfloat16),
        ],
        scratch_shapes=[
            pltpu.VMEM((4 * tokens, HD), jnp.bfloat16),
            pltpu.VMEM((4 * tokens, HD), jnp.bfloat16),
            pltpu.VMEM((tokens, chip_width), jnp.bfloat16),
            pltpu.VMEM(w_own.shape, jnp.bfloat16),
            pltpu.VMEM(w_other.shape, jnp.bfloat16),
            pltpu.VMEM((tokens * chip_width // HD, HD), jnp.bfloat16),
            pltpu.VMEM((tokens * chip_width // HD, 4 * tokens), jnp.float32),
            pltpu.VMEM((tokens * chip_width // HD, 4 * tokens), jnp.bfloat16),
            pltpu.SemaphoreType.DMA((2,)),
        ],
        compiler_params=pltpu.CompilerParams(vmem_limit_bytes=60 * MIB),
        cost_estimate=pl.CostEstimate(
            flops=16 * tokens * tokens * chip_width + 2 * tokens * chip_width * width,
            bytes_accessed=4 * w_own.size + 4 * tokens * width,
            transcendentals=4 * tokens * tokens * chip_width // HD,
        ),
    )(place, queries, *kv_parts, *bases, w_own, w_other)


def norm_kernel(own_ref, other_ref, gain_ref, *refs):
    hidden_ref, normed_ref = refs[-2:]
    hidden = (own_ref[...] + other_ref[...].astype(jnp.float32)).astype(jnp.bfloat16)
    hidden_ref[...] = hidden
    wide = hidden.astype(jnp.float32)
    normed_ref[...] = (
        wide
        * lax.rsqrt(jnp.mean(wide * wide, axis=1, keepdims=True) + 1e-06)
        * gain_ref[...].astype(jnp.float32)
    ).astype(jnp.bfloat16)


def add_and_norm(own, other, gain, present):
    return pl.pallas_call(
        norm_kernel,
        in_specs=[pl.BlockSpec(memory_space=pltpu.VMEM)] * 3
        + [pl.BlockSpec(memory_space=pl.ANY)] * len(present),
        out_specs=[pl.BlockSpec(memory_space=pltpu.VMEM)] * 2,
        out_shape=[jax.ShapeDtypeStruct(own.shape, jnp.bfloat16)] * 2,
        compiler_params=pltpu.CompilerParams(vmem_limit_bytes=10 * MIB),
    )(own, other, gain, *present)


def pass_kernel(*refs):
    del refs


def meet(arrays, flops):
    return pl.pallas_call(
        pass_kernel,
        in_specs=[pl.BlockSpec(memory_space=pl.ANY)] * len(arrays),
        out_specs=[pl.BlockSpec(memory_space=pl.ANY)] * len(arrays),
        out_shape=[jax.ShapeDtypeStruct(array.shape, array.dtype) for array in arrays],
        input_output_aliases={index: index for index in range(len(arrays))},
    )(*arrays)


def pass_kernel(*refs):
    del refs


def meet(arrays, flops):
    return pl.pallas_call(
        pass_kernel,
        in_specs=[pl.BlockSpec(memory_space=pl.ANY)] * len(arrays),
        out_specs=[pl.BlockSpec(memory_space=pl.ANY)] * len(arrays),
        out_shape=[jax.ShapeDtypeStruct(array.shape, array.dtype) for array in arrays],
        input_output_aliases={index: index for index in range(len(arrays))},
        compiler_params=pltpu.CompilerParams(vmem_limit_bytes=MIB),
        cost_estimate=pl.CostEstimate(flops=flops, bytes_accessed=0, transcendentals=0),
    )(*arrays)


def experts_kernel(mine_ref, quad_ref, *refs, cap, pieces):
    row_refs = []
    for count in pieces:
        row_refs.append(refs[:count])
        refs = refs[count:]
    w_gate_ref, w_up_ref, w_down_ref, own_ref, across_ref, other_ref, packed = refs
    tokens = row_refs[0][0].shape[0]
    quad = quad_ref[...].astype(jnp.float32)
    expert = lax.broadcasted_iota(jnp.int32, quad.shape, 0)
    line = jnp.sum(jnp.where(expert == mine_ref[0], quad, 0.0), axis=0, keepdims=True)
    gates = jnp.concatenate(
        [line[:, block * tokens : (block + 1) * tokens] for block in range(4)], axis=0
    )
    named = gates > 0
    before = (
        lax.broadcasted_iota(jnp.int32, (tokens, tokens), 0)
        < lax.broadcasted_iota(jnp.int32, (tokens, tokens), 1)
    ).astype(jnp.bfloat16)
    rank = jnp.dot(
        named.astype(jnp.float32).astype(jnp.bfloat16), before, preferred_element_type=jnp.float32
    )
    slot = jnp.where(named, rank.astype(jnp.int32), -1)
    slots = lax.broadcasted_iota(jnp.int32, (cap, tokens), 0)
    picks = []
    weights = []
    for block in range(4):
        chosen = slots == slot[block : block + 1, :]
        picks.append(jnp.where(chosen, 1.0, 0.0).astype(jnp.bfloat16))
        weights.append(
            jnp.sum(jnp.where(chosen, gates[block : block + 1, :], 0.0), axis=1, keepdims=True)
        )
        start = 0
        for row_ref in row_refs[block]:
            stop = start + row_ref.shape[1]
            packed[block * cap : (block + 1) * cap, start:stop] = jnp.dot(
                picks[block], row_ref[...], preferred_element_type=jnp.float32
            ).astype(jnp.bfloat16)
            start = stop
    rows = packed[...]
    gate_proj = jnp.dot(rows, w_gate_ref[...], preferred_element_type=jnp.float32)
    up_proj = jnp.dot(rows, w_up_ref[...], preferred_element_type=jnp.float32)
    inner = (gate_proj / (1.0 + jnp.exp(-gate_proj)) * up_proj).astype(jnp.bfloat16)
    result = jnp.dot(inner, w_down_ref[...], preferred_element_type=jnp.float32)
    targets = (
        own_ref.at[...],
        other_ref.at[0:tokens],
        across_ref.at[...],
        other_ref.at[tokens : 2 * tokens],
    )
    for block in range(4):
        part = (result[block * cap : (block + 1) * cap, :] * weights[block]).astype(jnp.bfloat16)
        targets[block][...] = lax.dot_general(
            picks[block], part, (((0,), (0,)), ((), ())), preferred_element_type=jnp.float32
        ).astype(jnp.bfloat16)


def experts_on_rows(mine, quad, row_blocks, w_gate, w_up, w_down, cap):
    tokens = row_blocks[0][0].shape[0]
    width, hidden_units = w_gate.shape
    pieces = tuple(len(block) for block in row_blocks)
    return pl.pallas_call(
        functools.partial(experts_kernel, cap=cap, pieces=pieces),
        in_specs=[pl.BlockSpec(memory_space=pltpu.SMEM)]
        + [pl.BlockSpec(memory_space=pltpu.VMEM)] * (4 + sum(pieces)),
        out_specs=[pl.BlockSpec(memory_space=pltpu.VMEM)] * 3,
        out_shape=[
            jax.ShapeDtypeStruct((tokens, width), jnp.bfloat16),
            jax.ShapeDtypeStruct((tokens, width), jnp.bfloat16),
            jax.ShapeDtypeStruct((2 * tokens, width), jnp.bfloat16),
        ],
        scratch_shapes=[pltpu.VMEM((4 * cap, width), jnp.bfloat16)],
        compiler_params=pltpu.CompilerParams(vmem_limit_bytes=28 * MIB),
        cost_estimate=pl.CostEstimate(
            flops=0,
            bytes_accessed=0,
            transcendentals=0,
        ),
    )(mine.reshape(1), quad, *sum(row_blocks, []), w_gate, w_up, w_down)


def gathered_plan(
    query_rows,
    key_rows,
    value_rows,
    residual_in,
    out_proj,
    norm_gain,
    expert_ids,
    gate_weights,
    expert_gate,
    expert_up,
    expert_down,
    cap,
):
    n_seq = lax.axis_size("seq")
    n_sub = lax.axis_size("sub")
    experts = n_seq * n_sub
    place = lax.axis_index("seq")
    core = place % 2
    chip = place // 2
    twin = [(index, index ^ 1) for index in range(n_seq)]
    across = [(index, (index + 2) % n_seq) for index in range(n_seq)]
    diagonal = [(index, (index ^ 1) ^ 2) for index in range(n_seq)]
    order = [0] + list(range(1, n_sub, 2)) + list(reversed(range(2, n_sub, 2)))

    def ring(steps):
        return [(order[at], order[(at + steps) % n_sub]) for at in range(n_sub)]

    queries = query_rows[0]
    chip_width = queries.shape[1] // 2

    tokens = queries.shape[0]
    queries_away, kv_here, kv_away = pack(
        chip,
        queries,
        key_rows[0],
        value_rows[0],
        expert_ids[0].T,
        gate_weights[0].T,
        experts,
    )
    incoming = lax.ppermute(queries_away, "seq", across)
    kv_parts = [
        kv_here,
        lax.ppermute(kv_here, "seq", twin),
        lax.ppermute(kv_away, "seq", across),
        lax.ppermute(kv_away, "seq", diagonal),
    ]
    w_other = lax.ppermute(out_proj, "seq", twin)
    columns = [place, place ^ 1, place ^ 2, place ^ 3]

    def place_of(query_start, row_block):
        return jnp.stack([core, query_start, row_block] + columns).astype(jnp.int32)

    sent, quad = attend(
        place_of(0 * place, place ^ 2), incoming, kv_parts, [], out_proj, w_other, jnp.bfloat16
    )
    projected_across = lax.ppermute(sent, "seq", across)
    projected, _ = attend(
        place_of(chip * chip_width, place),
        queries,
        kv_parts,
        [residual_in[0]],
        out_proj,
        w_other,
        jnp.float32,
    )
    quads = [lax.ppermute(quad, "sub", ring(steps)) for steps in range(1, n_sub)]
    hidden, normed = add_and_norm(projected, projected_across, norm_gain[None], quads)

    last = n_sub - 1
    mine = place * n_sub + lax.axis_index("sub")

    held = {("row", 0): normed, ("quad", 0): quad}
    held.update({("quad", steps): moved for steps, moved in enumerate(quads, 1)})
    half = normed.shape[1] // 2
    ways = {"across": ("seq", across), "twin": ("seq", twin), "on": ("sub", ring(1))}

    def move(array, way):
        return lax.ppermute(array, *ways[way])

    def experts_of(step):
        held["own", step], held["part", step], other = experts_on_rows(
            mine,
            held["quad", step],
            [
                [held[name, step]] if (name, step) in held else list(held[name, step, "pieces"])
                for name in ("row", "twin", "across", "diagonal")
            ],
            expert_gate[0],
            expert_up[0],
            expert_down[0],
            cap,
        )
        return other

    def twin_sum(step):
        met = move(held["other", step], "twin")
        held["met", step] = met[:tokens]
        return (held["part", step].astype(jnp.float32) + met[tokens:].astype(jnp.float32)).astype(
            jnp.bfloat16
        )

    def sum_of(step, more):
        parts = [held["own", step], held["met", step], held["back", step]] + more
        if held["back", step].shape[1] == half:
            left = sum(part[:, :half].astype(jnp.float32) for part in parts)
            right = sum(part[:, half:].astype(jnp.float32) for part in parts if part.shape[1] > half)
            return jnp.concatenate([left, right], axis=1)
        return sum(part.astype(jnp.float32) for part in parts)

    for turn in range(1, n_sub + 5):
        now = {}
        step = turn - 1
        if step < last:
            now["across", step] = move(held["row", step], "across")
            now["row", step + 1] = move(held["row", step], "on")
        if step == last:
            now["half", 0] = move(held["row", step][:, :half], "across")
            now["half", 1] = move(held["across", step - 1][:, half:], "on")
        if step <= last:
            held["twin", step] = move(held["row", step], "twin")
        step = turn - 4 if turn < n_sub + 4 else 0
        if 1 <= step <= last or turn == n_sub + 4:
            if step == 1:
                now["back", step] = move(held["away", step], "across")
                now["late", step] = move(held["apart", step], "on")
            elif step == 2:
                away = held["away", step]
                added = away[:, half:].astype(jnp.float32) + held["late", 1].astype(jnp.float32)
                now["back", step] = move(
                    jnp.concatenate([away[:, :half], added.astype(jnp.bfloat16)], axis=1), "across"
                )
            else:
                now["back", step] = move(held["away", step], "across")
        step = turn - 5
        if 1 <= step <= last:
            more = [held["sum", step - 1]] if step > 1 else []
            now["sum", step] = move(sum_of(step, more).astype(jnp.bfloat16), "on")
        step = turn - 2
        if 0 <= step < last:
            held["diagonal", step] = move(held["across", step], "twin")
        if step == last:
            held["across", step, "pieces"] = [held["half", side] for side in range(2)]
            held["diagonal", step, "pieces"] = [
                move(held["half", side], "twin") for side in range(2)
            ]
        if 1 <= step <= last:
            now["other", step] = experts_of(step)
        if turn == n_sub + 2:
            now["other", 0] = experts_of(0)
        step = turn - 3 if turn < n_sub + 3 else 0
        if 1 <= step <= last or turn == n_sub + 3:
            away = twin_sum(step)
            if step == 1:
                now["away", step] = away[:, :half]
                now["apart", step] = away[:, half:]
            else:
                now["away", step] = away
        if turn < n_sub + 4:
            wait = 10_000_000_000 if turn <= 2 else 0
            now = dict(zip(now.keys(), meet(list(now.values()), wait)))
        held.update(now)
    total = hidden.astype(jnp.float32) + sum_of(0, [held["sum", last]])
    return total.astype(jnp.bfloat16)[None]


def per_device(
    query_rows,
    key_rows,
    value_rows,
    residual_in,
    out_proj,
    norm_gain,
    expert_ids,
    gate_weights,
    expert_gate,
    expert_up,
    expert_down,
):
    tokens = query_rows.shape[1]
    n_seq = lax.axis_size("seq")
    n_sub = lax.axis_size("sub")
    experts = n_seq * n_sub
    topk = expert_ids.shape[2]
    cap = max(2, (5 * tokens * topk + 4 * experts - 1) // (4 * experts))
    if n_seq == 2 * KVH and KVH == 2 and tokens == HD and n_sub > 2 and experts <= 2 * topk and cap % 16 == 0:
        return gathered_plan(
            query_rows,
            key_rows,
            value_rows,
            residual_in,
            out_proj,
            norm_gain,
            expert_ids,
            gate_weights,
            expert_gate,
            expert_up,
            expert_down,
            cap,
        )
    heads_here = QH // n_seq
    group = QH // KVH
    query_local = lax.all_to_all(query_rows, "seq", split_axis=2, concat_axis=1, tiled=True)
    key_full, value_full = (
        lax.all_gather(key_rows, "seq", axis=1, tiled=True),
        lax.all_gather(value_rows, "seq", axis=1, tiled=True),
    )
    first_head = lax.axis_index("seq") * heads_here
    key_list = []
    value_list = []
    for head in range(heads_here):
        kv_start = (first_head + head) // group * HD
        key_list.append(lax.dynamic_slice_in_dim(key_full[0], kv_start, HD, 1))
        value_list.append(lax.dynamic_slice_in_dim(value_full[0], kv_start, HD, 1))
    length = query_local.shape[1]
    block = min(length, max(512, length // 8))
    outputs = [
        attend_head(
            query_local[0, :, head * HD : (head + 1) * HD], key_list[head], value_list[head], block
        )
        for head in range(heads_here)
    ]
    head_block = jnp.concatenate(outputs, axis=1)[None]
    attended = lax.all_to_all(head_block, "seq", split_axis=1, concat_axis=2, tiled=True)[0]
    projected = jnp.dot(
        attended,
        lax.all_gather(out_proj, "seq", axis=0, tiled=True),
        preferred_element_type=jnp.float32,
    )
    hidden = (residual_in[0].astype(jnp.float32) + projected).astype(jnp.bfloat16)
    wide = hidden.astype(jnp.float32)
    normed = (
        wide
        * lax.rsqrt(jnp.mean(wide * wide, axis=1, keepdims=True) + 1e-06)
        * norm_gain.astype(jnp.float32)
    ).astype(jnp.bfloat16)
    flat_ids = expert_ids[0].reshape(-1)
    items = flat_ids.shape[0]
    ranks = rank_in_expert(flat_ids, experts)
    slot_of = flat_ids * cap + ranks
    slots_out = experts * cap
    item_of_slot = (
        jnp.full((slots_out,), items, jnp.int32).at[slot_of].set(jnp.arange(items, dtype=jnp.int32))
    )
    padded_rows = jnp.concatenate([normed, jnp.zeros((1, D), jnp.bfloat16)], axis=0)
    padded_gates = jnp.concatenate(
        [gate_weights[0].reshape(-1), jnp.zeros((1,), jnp.bfloat16)], axis=0
    )
    token_of_slot = jnp.where(item_of_slot < items, item_of_slot // topk, tokens)
    send_rows = padded_rows[token_of_slot].reshape(experts, cap, D)
    send_gates = padded_gates[item_of_slot].reshape(experts, cap)
    recv_rows, recv_gates = (
        lax.all_to_all(send_rows, ("seq", "sub"), split_axis=0, concat_axis=0, tiled=True),
        lax.all_to_all(send_gates, ("seq", "sub"), split_axis=0, concat_axis=0, tiled=True),
    )
    slots_in = experts * cap
    valid = recv_gates > 0
    counts = jnp.sum(valid.astype(jnp.int32), axis=1)
    offsets = jnp.cumsum(counts) - counts
    dest = jnp.where(
        valid, offsets[:, None] + jnp.arange(cap, dtype=jnp.int32)[None, :], slots_in
    ).reshape(-1)
    source_of = (
        jnp.full((slots_in + 1,), slots_in, jnp.int32)
        .at[dest]
        .set(jnp.arange(slots_in, dtype=jnp.int32))[:slots_in]
    )
    compact_rows = jnp.concatenate(
        [recv_rows.reshape(slots_in, D), jnp.zeros((1, D), jnp.bfloat16)], axis=0
    )[source_of]
    compact_gates = jnp.concatenate(
        [recv_gates.reshape(-1), jnp.zeros((1,), jnp.bfloat16)], axis=0
    )[source_of].astype(jnp.float32)
    filled = jnp.sum(counts)
    n_blocks = (filled + slots_in - 1) // slots_in
    w_gate = expert_gate[0]
    w_up = expert_up[0]
    w_down = expert_down[0]

    def expert_block(index, results):
        gate_proj = jnp.dot(compact_rows, w_gate, preferred_element_type=jnp.float32)
        up_proj = jnp.dot(compact_rows, w_up, preferred_element_type=jnp.float32)
        inner = (jax.nn.silu(gate_proj) * up_proj).astype(jnp.bfloat16)
        weighted = (
            jnp.dot(inner, w_down, preferred_element_type=jnp.float32) * compact_gates[:, None]
        )
        return weighted.astype(jnp.bfloat16)

    results = lax.fori_loop(0, n_blocks, expert_block, jnp.zeros((slots_in, D), jnp.bfloat16))
    returned = jnp.concatenate([results, jnp.zeros((1, D), jnp.bfloat16)], axis=0)[dest].reshape(
        experts, cap, D
    )
    back = lax.all_to_all(
        returned, ("seq", "sub"), split_axis=0, concat_axis=0, tiled=True
    ).reshape(slots_out, D)
    gathered = back[slot_of].reshape(tokens, topk, D).astype(jnp.float32)
    mixture = jnp.sum(gathered, axis=1)
    return (wide + mixture).astype(jnp.bfloat16)[None]


def solution(mesh):
    placed = (
        P(("grp", "sub"), "seq", None),
        P(("grp", "sub"), "seq", None),
        P(("grp", "sub"), "seq", None),
        P(("grp", "sub"), "seq", None),
        P("seq", None),
        P(),
        P(("grp", "sub"), "seq", None),
        P(("grp", "sub"), "seq", None),
        P(("seq", "sub"), None, None),
        P(("seq", "sub"), None, None),
        P(("seq", "sub"), None, None),
    )
    return jax.shard_map(
        per_device,
        mesh=mesh,
        in_specs=placed,
        out_specs=P(("grp", "sub"), "seq", None),
        check_vma=False,
    )
```
